128 devices in a mesh: rep: 2 (over x_lo), shard: 64 (over x_hi, z, y, core).
Axes of the slice: x: 4 (x_hi: 2, x_lo: 2; x = x_hi * 2 + x_lo), y: 4, z: 4, core: 2. Of those that a mesh axis runs over, the one named last changes fastest.
Arguments:
- tokens: bfloat16 [32768, 1024], P(('rep', 'shard')), may hold values from -6 to 6
- w_qkv: bfloat16 [2, 1024, 3072], P(None, 'shard'), may hold values from -0.1875 to 0.1875
- b_qkv: bfloat16 [2, 3072], P(None, 'shard'), may hold values from -1.796875 to 1.796875
- w_out: bfloat16 [2, 1024, 1024], P(None, 'shard'), may hold values from -0.5 to 0.5
- w_up: bfloat16 [2, 1024, 4096], P(None, 'shard'), may hold values from -0.1875 to 0.1875
- b_up: bfloat16 [2, 4096], P(None, 'shard'), may hold values from -1.796875 to 1.796875
- w_down: bfloat16 [2, 4096, 1024], P(None, 'shard'), may hold values from -0.125 to 0.125
- ln_gain: bfloat16 [2, 1024], P(None, 'shard'), may hold values from 0.5 to 1.5
- ln_bias: bfloat16 [2, 1024], P(None, 'shard'), may hold values from -1.796875 to 1.796875
- out_bias: bfloat16 [2, 1024], P(None, 'shard'), may hold values from -1.796875 to 1.796875
- out_grad: bfloat16 [32768, 1024], P(('rep', 'shard')), may hold values from -6 to 6
Outputs:
- result: bfloat16 [32768, 1024], P(('rep', 'shard'))
- in_grad: float32 [32768, 1024], P(('rep', 'shard'))
- w_qkv_grad: float32 [2, 1024, 3072], P(None, 'shard')
- b_qkv_grad: float32 [2, 3072], P(None, 'shard')
- w_out_grad: float32 [2, 1024, 1024], P(None, 'shard')
- w_up_grad: float32 [2, 1024, 4096], P(None, 'shard')
- b_up_grad: float32 [2, 4096], P(None, 'shard')
- w_down_grad: float32 [2, 4096, 1024], P(None, 'shard')
- ln_gain_grad: float32 [2, 1024], P(None, 'shard')
- ln_bias_grad: float32 [2, 1024], P(None, 'shard')
- out_bias_grad: float32 [2, 1024], P(None, 'shard')
The draws below stay inside these ranges and needn't reach their ends.
All inputs are finite; a program needn't handle non-finite values.
Results may differ from the reference program's by a relative error of at most 0.013.
Values may be sent and summed in bfloat16 or wider, within the bound.
A program may use at most 320 MiB of HBM per device.

```python
import math
import jax
import jax.numpy as jnp
from jax import lax

D = 1024
FF = 4096
HEADS = 16
HEAD_DIM = 64
ROT = 16
LAYERS = 2
TOK_DEV = 256
TOKENS = 32768


def block_levels(key, dims, pieces, smallest, high):
    def one(dim, shards_of):
        heights = jax.random.uniform(jax.random.fold_in(jax.random.fold_in(key, 6), dim), (shards_of,), jnp.float32, smallest / len(pieces), high / len(pieces))
        return jnp.repeat(jnp.exp(heights), dims[dim] // shards_of).reshape((-1,) + (1,) * (len(dims) - dim - 1))

    factor_of = one(*pieces[0])
    for cut in pieces[1:]:
        factor_of = factor_of * one(*cut)
    return factor_of


def noise(rng, extent, scale, most, pieces=(), held_as=jnp.bfloat16):
    factor_of = block_levels(rng, extent, pieces, -0.22, 0.18) if pieces else 1.0
    result = jax.random.normal(rng, extent, jnp.float32) * scale * factor_of
    return jnp.minimum(jnp.maximum(result, -most), most).astype(held_as)


def setup_inputs(seed: int = 0) -> dict:
    key_of = jax.random.split(jax.random.key(seed), 12)
    tokens = noise(key_of[0], (TOKENS, D), 1.0, 6.0, ((0, 128),))
    w_qkv = noise(key_of[1], (LAYERS, D, 3 * D), D ** -0.5, 0.1875, ((1, 64),))
    b_qkv = noise(key_of[2], (LAYERS, 3 * D), 0.3, 1.796875, ((1, 64),))
    w_out = noise(key_of[3], (LAYERS, D, D), (D // 8) ** -0.5, 0.5, ((1, 64),))
    w_up = noise(key_of[4], (LAYERS, D, FF), D ** -0.5, 0.1875, ((1, 64),))
    b_up = noise(key_of[5], (LAYERS, FF), 0.3, 1.796875, ((1, 64),))
    w_down = noise(key_of[6], (LAYERS, FF, D), (FF // 2) ** -0.5, 0.125, ((1, 64),))
    ln_gain = jnp.clip(1.0 + 0.1 * jax.random.normal(key_of[7], (LAYERS, D), jnp.float32), 0.5, 1.5).astype(jnp.bfloat16)
    ln_bias = noise(key_of[8], (LAYERS, D), 0.3, 1.796875, ((1, 64),))
    out_bias = noise(key_of[9], (LAYERS, D), 0.3, 1.796875, ((1, 64),))
    out_grad = noise(key_of[10], (TOKENS, D), 1.0, 6.0, ((0, 128),))
    return dict(tokens=tokens, w_qkv=w_qkv, b_qkv=b_qkv, w_out=w_out, w_up=w_up, b_up=b_up, w_down=w_down, ln_gain=ln_gain, ln_bias=ln_bias, out_bias=out_bias, out_grad=out_grad)


EPS = 1e-05
FILL = -1e+30

@jax.custom_vjp
def low(v):
    return lax.optimization_barrier(v.astype(jnp.bfloat16)).astype(jnp.float32)

@jax.custom_vjp
def low_back(v):
    return v

def low_keep(v):
    return (low(v), None)

def low_pass(kept, grad):
    return (grad,)

def back_keep(v):
    return (v, None)

def back_low(kept, grad):
    return (low(grad),)
low.defvjp(low_keep, low_pass)
low_back.defvjp(back_keep, back_low)

def tables(count):
    places = jnp.arange(count, dtype=jnp.float32)
    rates = 10000.0 ** (-jnp.arange(0, ROT, 2, dtype=jnp.float32) / ROT)
    angles = places[:, None] * rates[None, :]
    cosine = jnp.concatenate([jnp.cos(angles), jnp.cos(angles)], -1)
    sine = jnp.concatenate([jnp.sin(angles), jnp.sin(angles)], -1)
    return (cosine, sine)

def rotate(values, cosine, sine):
    half = ROT // 2
    turned = values[..., :ROT]
    swapped = jnp.concatenate([-turned[..., half:], turned[..., :half]], -1)
    moved = turned * cosine[:, None, :] + swapped * sine[:, None, :]
    return jnp.concatenate([moved, values[..., ROT:]], -1)

def block_forward(inputs, params, cosine, sine, causal):
    w_qkv, b_qkv, w_out, w_up, b_up, w_down, gain, shift, out_bias = params
    highest = lax.Precision.HIGHEST
    width = w_out.shape[0]
    groups = inputs.shape[0]
    count = inputs.shape[1]
    centred = inputs - lax.optimization_barrier(jnp.mean(inputs, -1, keepdims=True))
    normed = centred * lax.rsqrt(lax.optimization_barrier(jnp.mean(centred * centred, -1, keepdims=True)) + EPS)
    hidden = low(normed * gain + shift)
    joined = low_back(jnp.einsum('gsd,de->gse', hidden, w_qkv, precision=highest) + b_qkv)
    split_shape = (groups, count, HEADS, HEAD_DIM)
    query = low(rotate(joined[..., :width].reshape(split_shape), cosine, sine))
    key_rot = low(rotate(joined[..., width:2 * width].reshape(split_shape), cosine, sine))
    values = low(joined[..., 2 * width:].reshape(split_shape))
    scores = low_back(jnp.einsum('gshd,gthd->ghst', query, key_rot, precision=highest) * HEAD_DIM ** (-0.5))
    scores = jnp.where(causal, scores, FILL)
    probs = low(jax.nn.softmax(scores, axis=-1))
    mixed = jnp.einsum('ghst,gthd->gshd', probs, values, precision=highest).reshape(groups, count, width)
    mixed = low(low_back(mixed))
    attended = jnp.einsum('gsd,de->gse', mixed, w_out, precision=highest)
    upward = low_back(jnp.einsum('gsd,df->gsf', hidden, w_up, precision=highest) + b_up)
    active = low(jax.nn.gelu(upward, approximate=False))
    lowered = jnp.einsum('gsf,fd->gsd', active, w_down, precision=highest)
    return inputs + low_back(attended + lowered) + out_bias

def reference(tokens, w_qkv, b_qkv, w_out, w_up, b_up, w_down, ln_gain, ln_bias, out_bias, out_grad):
    params = tuple((item.astype(jnp.float32) for item in (w_qkv, b_qkv, w_out, w_up, b_up, w_down, ln_gain, ln_bias, out_bias)))
    inputs = tokens.astype(jnp.float32)
    cotangent = out_grad.astype(jnp.float32)
    count = TOK_DEV
    sequences = inputs.shape[0] // count
    groups = math.gcd(sequences, max(1, 4096 // count))
    cosine, sine = tables(count)
    causal = jnp.tril(jnp.ones((count, count), jnp.bool_))

    def forward(start, weights):
        blocks = start.reshape(sequences // groups, groups, count, start.shape[1])

        def run(carry, block):
            for layer_at in range(LAYERS):
                block = block_forward(block, tuple((item[layer_at] for item in weights)), cosine, sine, causal)
            return (carry, block)
        unused, ends = lax.scan(jax.checkpoint(run), None, blocks)
        return ends.reshape(start.shape)
    outcome, pullback = jax.vjp(forward, inputs, params)
    in_grad, grads = pullback(cotangent)
    return (outcome.astype(jnp.bfloat16), in_grad, grads[0], grads[1], grads[2], grads[3], grads[4], grads[5], grads[6], grads[7], grads[8])
```

```python
import functools
import jax
import jax.numpy as jnp
from jax import lax
from jax.experimental import pallas as pl
from jax.experimental.pallas import tpu as pltpu
from jax.sharding import PartitionSpec as P

MESH = pl.DeviceIdType.MESH
LANE = 128
LAYERS = 2


def place():
    xl = lax.axis_index("rep")
    s = lax.axis_index("shard")
    return xl, s // 32, (s // 8) % 4, (s // 2) % 4, s % 2


def at(xl, xh, z, y, c):
    return (xl, xh * 32 + z * 8 + y * 2 + c)


def around(value, step):
    return lax.rem(value + (step + 4), 4)


def meet(others):
    barrier = pltpu.get_barrier_semaphore()
    for other in others:
        pl.semaphore_signal(barrier, inc=1, device_id=other, device_id_type=MESH)
    pl.semaphore_wait(barrier, len(others))


GATHERED = (
    ("small", True, 32, 128, 0, 1),
    ("qkv", True, 32, 1536, 4, 8),
    ("up", True, 32, 2048, 5, 11),
    ("out", False, 32, 1024, 3, 5),
    ("down", False, 128, 1024, 3, 5),
)
SLOTS = 18


class Stream:
    def __init__(self, number, spec, source, target, send, recv, xl, xh, z, y, core):
        self.name, self.by_columns, self.rows, self.columns, self.swapped, self.width = spec
        self.number = number
        self.source = source
        self.target = target
        self.send, self.recv = send, recv
        self.xl, self.xh, self.z, self.y, self.core = xl, xh, z, y, core
        self.half = self.rows // 2
        self.wide = pl.ds(pl.multiple_of(xl * (self.swapped * LANE), LANE), self.width * LANE)
        self.mine = pl.ds(
            pl.multiple_of(xl * ((self.width - self.swapped) * LANE) + xl * (self.swapped * LANE), LANE),
            max(self.swapped, 1) * LANE,
        )
        self.theirs = pl.ds(
            pl.multiple_of((1 - xl) * (self.width * LANE), LANE), max(self.swapped, 1) * LANE
        )
        self.across = lambda core_of: at(1 - xl, 1 - xh, z, y, core_of)
        self.partner = at(1 - xl, xh, z, y, core) if core == 0 else self.across(core)
        if core == 0:
            self.first, self.second = y, z
        else:
            self.first, self.second = z, y
        self.sent = []

    def neighbour(self, ring, step):
        z, y = self.z, self.y
        if (ring == 0) == (self.core == 0):
            y = around(y, step)
        else:
            z = around(z, step)
        return at(self.xl, self.xh, z, y, self.core)

    def block(self, first, rows, columns):
        if self.core == 0:
            return self.target.at[:, self.second, first, rows, columns]
        return self.target.at[:, first, self.second, rows, columns]

    def line(self, second, rows, columns):
        if self.core == 0:
            return self.target.at[:, second, :, rows, columns]
        return self.target.at[:, :, second, rows, columns]

    def push(self, source, target, slot, device):
        copy = pltpu.make_async_remote_copy(
            source,
            target,
            self.send.at[self.number, slot],
            self.recv.at[self.number, slot],
            device_id=device,
            device_id_type=MESH,
        )
        copy.start()
        self.sent.append((source, slot))

    def arrived(self, region, slot):
        pltpu.make_async_copy(region, region, self.recv.at[self.number, slot]).wait()

    def part(self, core_of):
        return pl.ds(core_of * self.half, self.half)

    def stage0(self):
        xh, z, y, core = self.xh, self.z, self.y, self.core
        whole = slice(None)
        if self.by_columns:
            here = self.target.at[xh, z, y, self.part(core), :]
            pltpu.make_async_copy(
                self.source(core), here, self.recv.at[self.number, xh * 2 + core]
            ).start()
            for slot, half, device in (
                (0, 1 - core, at(self.xl, xh, z, y, 1 - core)),
                (1, core, self.across(core)),
                (2, 1 - core, self.across(1 - core)),
            ):
                copy = pltpu.make_async_remote_copy(
                    self.source(half),
                    here,
                    self.send.at[self.number, slot],
                    self.recv.at[self.number, xh * 2 + core],
                    device_id=device,
                    device_id_type=MESH,
                )
                copy.start()
                self.sent.append((self.source(half), slot))
        else:
            here = self.target.at[0, z, y, self.part(core), :]
            mine = self.source(0)

            @pl.when(xh == core)
            def _():
                pltpu.make_async_copy(mine, here, self.recv.at[self.number, core]).start()

            @pl.when(xh != core)
            def _():
                pltpu.make_async_remote_copy(
                    mine,
                    here,
                    self.send.at[self.number, 0],
                    self.recv.at[self.number, core],
                    device_id=at(self.xl, xh, z, y, 1 - core),
                    device_id_type=MESH,
                ).start()

            pltpu.make_async_remote_copy(
                mine,
                here,
                self.send.at[self.number, 1],
                self.recv.at[self.number, core],
                device_id=self.across(xh),
                device_id_type=MESH,
            ).start()
            self.sent.append((mine, 1))

    def stage1(self):
        whole = slice(None)
        for bank in range(2 if self.by_columns else 1):
            for core_of in range(2):
                self.arrived(
                    self.target.at[bank, self.z, self.y, self.part(core_of), :], bank * 2 + core_of
                )
        own = self.block(self.first, whole, self.wide)
        self.push(own, own, 4, self.neighbour(0, 1))
        self.push(own, own, 5, self.neighbour(0, -1))

    def share(self, region, slot):
        if self.swapped:
            self.push(region(self.mine), region(self.mine), slot, self.partner)

    def stage2(self):
        whole = slice(None)
        for step, slot in ((-1, 4), (1, 5)):
            origin = around(self.first, step)
            self.arrived(self.block(origin, whole, self.wide), slot)
            half = self.block(origin, self.part(slot - 4), self.wide)
            self.push(half, half, slot + 2, self.neighbour(0, -step))
            self.share(lambda columns: self.block(origin, whole, columns), slot + 8)

    def stage3(self):
        whole = slice(None)
        far = around(self.first, 2)
        for half in range(2):
            self.arrived(self.block(far, self.part(half), self.wide), 6 + half)
        own = self.line(self.second, whole, self.wide)
        self.push(own, own, 8, self.neighbour(1, 1))
        self.push(own, own, 9, self.neighbour(1, -1))
        self.share(lambda columns: self.block(far, whole, columns), 14)

    def stage4(self):
        whole = slice(None)
        for step, slot in ((-1, 8), (1, 9)):
            origin = around(self.second, step)
            self.arrived(self.line(origin, whole, self.wide), slot)
            half = self.line(origin, self.part(slot - 8), self.wide)
            self.push(half, half, slot + 2, self.neighbour(1, -step))
            self.share(lambda columns: self.line(origin, whole, columns), slot + 7)

    def stage5(self):
        whole = slice(None)
        far = around(self.second, 2)
        for half in range(2):
            self.arrived(self.line(far, self.part(half), self.wide), 10 + half)
        self.share(lambda columns: self.line(far, whole, columns), 17)

    def stage6(self):
        whole = slice(None)
        if self.swapped:
            for step, slot in ((-1, 12), (1, 13), (2, 14)):
                self.arrived(self.block(around(self.first, step), whole, self.theirs), slot)
            for step, slot in ((-1, 15), (1, 16), (2, 17)):
                self.arrived(self.line(around(self.second, step), whole, self.theirs), slot)

    def finish(self):
        for source, slot in self.sent:
            pltpu.make_async_copy(source, source, self.send.at[self.number, slot]).wait()
        if not self.by_columns:

            @pl.when(self.xh != self.core)
            def _():
                mine = self.source(0)
                pltpu.make_async_copy(mine, mine, self.send.at[self.number, 0]).wait()


def streams_of(sources, targets, send, recv, core, xl, xh, z, y, layers):
    found = []
    small, qkv, up, out, down = sources
    for layer_at in layers:
        from_args = (
            lambda half: small,
            lambda half, layer_at=layer_at: qkv.at[half, layer_at],
            lambda half, layer_at=layer_at: up.at[layer_at, :, pl.ds(half * 2048, 2048)],
            lambda half, layer_at=layer_at: out.at[layer_at],
            lambda half, layer_at=layer_at: down.at[layer_at],
        )
        for spec, source in zip(GATHERED, from_args):
            if spec[0] == "small" and layer_at != layers[0]:
                continue
            number = len(found)
            found.append(
                Stream(number, spec, source, targets[number], send, recv, xl, xh, z, y, core)
            )
    return found


def gather_kernel(small, qkv, up, out, down, *rest):
    targets, (send, recv) = rest[:-2], rest[-2:]
    xl, xh, z, y, c = place()
    meet(
        [
            at(xl, xh, z, y, 1 - c),
            at(1 - xl, 1 - xh, z, y, c),
            at(1 - xl, 1 - xh, z, y, 1 - c),
            at(1 - xl, xh, z, y, c),
            at(xl, xh, around(z, 1), y, c),
            at(xl, xh, around(z, -1), y, c),
            at(xl, xh, z, around(y, 1), c),
            at(xl, xh, z, around(y, -1), c),
        ]
    )

    def run(core):
        streams = streams_of(
            (small, qkv, up, out, down), targets, send, recv, core, xl, xh, z, y, range(LAYERS)
        )
        for tick in range(len(streams) + 6):
            for stage in range(7):
                if 0 <= tick - stage < len(streams):
                    getattr(streams[tick - stage], f"stage{stage}")()
        for stream in streams:
            stream.finish()

    for core in range(2):
        pl.when(c == core)(functools.partial(run, core))


def gather(small, qkv, up, out, down):
    shapes = []
    for layer_at in range(LAYERS):
        for name, by_columns, rows, columns, swapped, width in GATHERED:
            if name == "small" and layer_at:
                continue
            shapes.append(
                jax.ShapeDtypeStruct((2 if by_columns else 1, 4, 4, rows, columns), jnp.bfloat16)
            )
    return pl.pallas_call(
        gather_kernel,
        out_shape=shapes,
        in_specs=[pl.BlockSpec(memory_space=pltpu.HBM)] * 5,
        out_specs=[pl.BlockSpec(memory_space=pltpu.HBM)] * len(shapes),
        scratch_shapes=[
            pltpu.SemaphoreType.DMA((len(shapes), SLOTS)),
            pltpu.SemaphoreType.DMA((len(shapes), SLOTS)),
        ],
        name="gather",
        compiler_params=pltpu.CompilerParams(collective_id=0, has_side_effects=True),
    )(small, qkv, up, out, down)


def halves(w_qkv):
    rows = w_qkv.shape[1]
    return w_qkv.reshape(LAYERS, rows, 3, 2, 512).transpose(3, 0, 1, 2, 4).reshape(
        2, LAYERS, rows, 1536
    )


SUMMED = (
    ("qkv", True, 32, 1536, 3, 9),
    ("up", True, 32, 2048, 4, 12),
    ("out", False, 32, 1024, 2, 6),
    ("down", False, 128, 1024, 2, 6),
)
SMALL = ("small", True, 16, 128, 0, 1)
SUM_SLOTS = 18


def scratch_of(spec):
    name, by_columns, rows, columns, swapped, width = spec
    banks = 2 if by_columns else 1
    kind = jnp.float32 if name == "small" else jnp.bfloat16
    wide = width * LANE
    return [
        pltpu.VMEM((banks, 4, 4, rows, columns), kind),
        pltpu.VMEM((banks, 4, 4, rows, max(swapped, 1) * LANE) if swapped else (8, LANE), kind),
        pltpu.VMEM((2, banks, 4, rows // 2, wide), kind),
        pltpu.VMEM((2, banks, 4, rows, wide), kind),
        pltpu.VMEM((2, banks, rows // 2, wide), kind),
        pltpu.VMEM((2, banks, rows, wide), kind),
        pltpu.VMEM((3, rows, wide), kind),
        pltpu.VMEM((rows, columns), jnp.float32),
        pltpu.VMEM((2, 8, LANE), jnp.float32),
    ]


class Sum:
    def __init__(self, number, spec, source, outputs, buffers, send, recv, xl, xh, z, y, core):
        self.name, self.by_columns, self.rows, self.columns, self.swapped, self.width = spec
        self.number, self.source, self.outputs = number, source, outputs
        (
            self.total,
            self.swap,
            self.far_line,
            self.near_line,
            self.far_block,
            self.near_block,
            self.last,
            self.ready,
            self.tail,
        ) = buffers
        self.send, self.recv = send, recv
        self.xl, self.xh, self.z, self.y, self.core = xl, xh, z, y, core
        self.banks = 2 if self.by_columns else 1
        self.half = self.rows // 2
        s, w = self.swapped, self.width
        self.wide = pl.ds(pl.multiple_of(xl * (s * LANE), LANE), w * LANE)
        self.mine = pl.ds(pl.multiple_of(xl * (w * LANE), LANE), max(s, 1) * LANE)
        self.theirs = pl.ds(pl.multiple_of((1 - xl) * (w * LANE), LANE), max(s, 1) * LANE)
        self.beside = at(1 - xl, xh, z, y, core)
        self.across = at(1 - xl, 1 - xh, z, y, core)
        self.beyond = at(xl, 1 - xh, z, y, core)
        self.sibling = at(xl, xh, z, y, 1 - core)
        self.partner = self.beside if core == 0 else self.across
        self.first, self.second = (y, z) if core == 0 else (z, y)
        self.sent = []

    def neighbour(self, ring, step):
        z, y = self.z, self.y
        if (ring == 0) == (self.core == 0):
            y = around(y, step)
        else:
            z = around(z, step)
        return at(self.xl, self.xh, z, y, self.core)

    def block(self, first, rows, columns):
        if self.core == 0:
            return self.total.at[:, self.second, first, rows, columns]
        return self.total.at[:, first, self.second, rows, columns]

    def line(self, second, rows, columns):
        if self.core == 0:
            return self.total.at[:, second, :, rows, columns]
        return self.total.at[:, :, second, rows, columns]

    def push(self, source, target, slot, device):
        copy = pltpu.make_async_remote_copy(
            source,
            target,
            self.send.at[self.number, slot],
            self.recv.at[self.number, slot],
            device_id=device,
            device_id_type=MESH,
        )
        copy.start()
        return (source, slot)

    def arrived(self, region, slot):
        pltpu.make_async_copy(region, region, self.recv.at[self.number, slot]).wait()

    def part(self, core_of):
        return pl.ds(core_of * self.half, self.half)

    def stage0(self):
        pltpu.make_async_copy(self.source, self.total, self.recv.at[self.number, 17]).start()

    def stage1(self):
        self.arrived(self.total, 17)
        if self.swapped:
            whole = self.total.at[:, :, :, :, self.theirs]
            self.sent.append(self.push(whole, self.swap, 0, self.partner))

    def stage2(self):
        whole = slice(None)
        if self.swapped:
            self.arrived(self.swap, 0)

            def add(step, carry):
                bank, z, y = step // 16, (step // 4) % 4, step % 4
                self.total[bank, z, y, :, self.mine] = (
                    self.total[bank, z, y, :, self.mine].astype(jnp.float32)
                    + self.swap[bank, z, y].astype(jnp.float32)
                ).astype(self.total.dtype)
                return carry

            lax.fori_loop(0, self.banks * 16, add, 0)
        far = around(self.second, 2)
        for half in range(2):
            self.sent.append(
                self.push(
                    self.line(far, self.part(half), self.wide),
                    self.far_line.at[half],
                    1 + half,
                    self.neighbour(1, 1 - 2 * half),
                )
            )

    def stage3(self):
        for half in range(2):
            self.arrived(self.far_line.at[half], 1 + half)
            to = around(self.second, 1 - 2 * half)
            rows = self.part(half)

            def add(step, carry):
                bank, at_ = step // 4, step % 4
                region = self.line(to, rows, self.wide).at[bank, at_]
                region[...] = (
                    region[...].astype(jnp.float32)
                    + self.far_line[half, bank, at_].astype(jnp.float32)
                ).astype(self.total.dtype)
                return carry

            lax.fori_loop(0, self.banks * 4, add, 0)
            self.sent.append(
                self.push(
                    self.line(to, slice(None), self.wide),
                    self.near_line.at[half],
                    3 + half,
                    self.neighbour(1, 1 - 2 * half),
                )
            )

    def stage4(self):
        for half in range(2):
            self.arrived(self.near_line.at[half], 3 + half)

        def add(step, carry):
            bank, at_ = step // 4, step % 4
            region = self.line(self.second, slice(None), self.wide).at[bank, at_]
            region[...] = (
                region[...].astype(jnp.float32)
                + self.near_line[0, bank, at_].astype(jnp.float32)
                + self.near_line[1, bank, at_].astype(jnp.float32)
            ).astype(self.total.dtype)
            return carry

        lax.fori_loop(0, self.banks * 4, add, 0)
        far = around(self.first, 2)
        for half in range(2):
            self.sent.append(
                self.push(
                    self.block(far, self.part(half), self.wide),
                    self.far_block.at[half],
                    5 + half,
                    self.neighbour(0, 1 - 2 * half),
                )
            )

    def stage5(self):
        for half in range(2):
            self.arrived(self.far_block.at[half], 5 + half)
            to = around(self.first, 1 - 2 * half)
            for bank in range(self.banks):
                region = self.block(to, self.part(half), self.wide).at[bank]
                region[...] = (
                    region[...].astype(jnp.float32)
                    + self.far_block[half, bank].astype(jnp.float32)
                ).astype(self.total.dtype)
            self.sent.append(
                self.push(
                    self.block(to, slice(None), self.wide),
                    self.near_block.at[half],
                    7 + half,
                    self.neighbour(0, 1 - 2 * half),
                )
            )

    def stage6(self):
        for half in range(2):
            self.arrived(self.near_block.at[half], 7 + half)
        own = self.block(self.first, slice(None), self.wide)
        for bank in range(self.banks):
            region = own.at[bank]
            region[...] = (
                region[...].astype(jnp.float32)
                + self.near_block[0, bank].astype(jnp.float32)
                + self.near_block[1, bank].astype(jnp.float32)
            ).astype(self.total.dtype)
        if self.by_columns:
            self.sent.append(self.push(own.at[self.xh], self.last.at[0], 9, self.beside))
            self.sent.append(self.push(own.at[1 - self.xh], self.last.at[1], 10, self.across))
            self.sent.append(self.push(own.at[1 - self.xh], self.last.at[2], 11, self.beyond))
        else:

            @pl.when(self.xh == self.core)
            def _():
                self.push(own.at[0], self.last.at[0], 9, self.beside)

            @pl.when(self.xh != self.core)
            def _():
                self.push(own.at[0], self.last.at[1], 10, self.across)
                self.push(own.at[0], self.last.at[2], 11, self.beyond)

    def add_last(self):
        for slot in range(3):
            self.arrived(self.last.at[slot], 9 + slot)
        s, w = self.swapped, self.width
        c = w - s
        own = self.block(self.first, slice(None), self.wide).at[self.xh if self.by_columns else 0]
        self.ready[:, self.wide] = own[...].astype(jnp.float32) + self.last[2].astype(jnp.float32)
        if s:
            there = pl.ds(pl.multiple_of((1 - self.xl) * (c * LANE), LANE), s * LANE)
            self.ready[:, self.theirs] = self.last[0, :, there].astype(jnp.float32) + self.last[
                1, :, there
            ].astype(jnp.float32)
        middle = pl.ds(s * LANE, c * LANE)
        there = pl.ds(pl.multiple_of(self.xl * (s * LANE), LANE), c * LANE)
        self.ready[:, middle] = (
            self.ready[:, middle]
            + self.last[0, :, there].astype(jnp.float32)
            + self.last[1, :, there].astype(jnp.float32)
        )

    def pieces(self, core_of, target):
        rows = self.part(core_of)
        if self.name == "qkv":
            return [
                (
                    self.ready.at[rows, pl.ds(third * 512, 512)],
                    target.at[:, pl.ds(third * 1024 + self.core * 512, 512)],
                )
                for third in range(3)
            ]
        if self.name == "up":
            return [(self.ready.at[rows, :], target.at[:, pl.ds(self.core * 2048, 2048)])]
        return [(self.ready.at[rows, :], target)]

    def deliver(self):
        core = self.core
        for index, (source, target) in enumerate(self.pieces(core, self.outputs)):
            pltpu.make_async_copy(source, target, self.recv.at[self.number, 15 + index]).start()
        for index, (source, target) in enumerate(self.pieces(1 - core, self.outputs)):
            self.push(source, target, 12 + index, self.sibling)

    def delivered(self):
        for index, (source, target) in enumerate(self.pieces(self.core, self.outputs)):
            pltpu.make_async_copy(source, target, self.recv.at[self.number, 15 + index]).wait()
        for index, (source, target) in enumerate(self.pieces(1 - self.core, self.outputs)):
            pltpu.make_async_copy(source, source, self.send.at[self.number, 12 + index]).wait()

    def stage7(self):
        if self.name == "small":
            self.add_last()
            self.sent.append(
                self.push(
                    self.ready.at[self.part(1 - self.core), :], self.tail.at[0], 12, self.sibling
                )
            )
        elif self.by_columns:
            self.add_last()
            self.deliver()
        else:

            @pl.when(self.xh == self.core)
            def _():
                self.add_last()
                self.deliver()

    def stage8(self):
        core = self.core
        if self.name == "small":
            self.arrived(self.tail.at[0], 12)
            self.tail[1] = self.ready[self.part(core), :] + self.tail[0]
            copy = pltpu.make_async_copy(
                self.tail.at[1], self.outputs, self.recv.at[self.number, 15]
            )
            copy.start()
            copy.wait()
        elif self.by_columns:
            self.delivered()
            for index, (source, target) in enumerate(self.pieces(1 - core, self.outputs)):
                there = target
                self.arrived(source, 12 + index)
        else:

            @pl.when(self.xh == core)
            def _():
                self.delivered()

            @pl.when(self.xh != core)
            def _():
                self.arrived(self.outputs, 12)

        for source, slot in self.sent:
            pltpu.make_async_copy(source, source, self.send.at[self.number, slot]).wait()
        if not self.by_columns:
            own = self.block(self.first, slice(None), self.wide).at[0]

            @pl.when(self.xh == core)
            def _():
                pltpu.make_async_copy(own, own, self.send.at[self.number, 9]).wait()

            @pl.when(self.xh != core)
            def _():
                pltpu.make_async_copy(own, own, self.send.at[self.number, 10]).wait()
                pltpu.make_async_copy(own, own, self.send.at[self.number, 11]).wait()


def plan(layers):
    found = []
    for layer_at in reversed(range(layers)):
        for which, spec in enumerate(SUMMED):
            found.append((spec, layer_at, which))
    found.insert(len(found) - 3, (SMALL, None, 4))
    return found


def scatter_kernel(streams, *rest):
    count = len(streams)
    sources, rest = rest[:count], rest[count:]
    outputs, rest = rest[:5], rest[5:]
    buffers, (send, recv) = rest[:-2], rest[-2:]
    xl, xh, z, y, c = place()
    meet(
        [
            at(xl, xh, z, y, 1 - c),
            at(1 - xl, 1 - xh, z, y, c),
            at(xl, 1 - xh, z, y, c),
            at(1 - xl, xh, z, y, c),
            at(xl, xh, around(z, 1), y, c),
            at(xl, xh, around(z, -1), y, c),
            at(xl, xh, z, around(y, 1), c),
            at(xl, xh, z, around(y, -1), c),
        ]
    )

    def run(core):
        sums = []
        for number, (spec, layer_at, which) in enumerate(streams):
            target = outputs[which] if layer_at is None else outputs[which].at[layer_at]
            sums.append(
                Sum(
                    number,
                    spec,
                    sources[number],
                    target,
                    buffers[9 * number : 9 * number + 9],
                    send,
                    recv,
                    xl,
                    xh,
                    z,
                    y,
                    core,
                )
            )
        for item in sums:
            item.stage0()
        for tick in range(len(sums) + 7):
            for stage in range(1, 9):
                if 0 <= tick - (stage - 1) < len(sums):
                    getattr(sums[tick - (stage - 1)], f"stage{stage}")()

    for core in range(2):
        pl.when(c == core)(functools.partial(run, core))


def scatter(grads, small):
    streams = plan(LAYERS)
    sources = [
        small if layer_at is None else grads[layer_at][which] for spec, layer_at, which in streams
    ]
    scratch = []
    for spec, layer_at, which in streams:
        scratch.extend(scratch_of(spec))
    f32 = jnp.float32
    return pl.pallas_call(
        functools.partial(scatter_kernel, streams),
        out_shape=[
            jax.ShapeDtypeStruct((LAYERS, 16, 3072), f32),
            jax.ShapeDtypeStruct((LAYERS, 16, 4096), f32),
            jax.ShapeDtypeStruct((LAYERS, 16, 1024), f32),
            jax.ShapeDtypeStruct((LAYERS, 64, 1024), f32),
            jax.ShapeDtypeStruct((8, LANE), f32),
        ],
        in_specs=[pl.BlockSpec(memory_space=pltpu.HBM)] * len(sources),
        out_specs=[pl.BlockSpec(memory_space=pltpu.HBM)] * 5,
        scratch_shapes=scratch
        + [
            pltpu.SemaphoreType.DMA((len(streams), SUM_SLOTS)),
            pltpu.SemaphoreType.DMA((len(streams), SUM_SLOTS)),
        ],
        name="scatter",
        compiler_params=pltpu.CompilerParams(
            collective_id=1, has_side_effects=True, vmem_limit_bytes=60 * 2**20
        ),
    )(*sources)


HEADS = 16
HEAD_DIM = 64
ROT = 16
EPS = 1e-05
FILL = -1e30


def tables(count):
    places = jnp.arange(count, dtype=jnp.float32)
    rates = 10000.0 ** (-jnp.arange(0, ROT, 2, dtype=jnp.float32) / ROT)
    angles = places[:, None] * rates[None, :]
    cosine = jnp.concatenate([jnp.cos(angles), jnp.cos(angles)], -1)
    sine = jnp.concatenate([jnp.sin(angles), jnp.sin(angles)], -1)
    return (cosine, sine)


def rotate(values, cosine, sine):
    half = ROT // 2
    turned = values[..., :ROT]
    swapped = jnp.concatenate([-turned[..., half:], turned[..., :half]], -1)
    moved = turned * cosine[:, None, :] + swapped * sine[:, None, :]
    return jnp.concatenate([moved, values[..., ROT:]], -1)


def gelu_exact(values):
    return jax.nn.gelu(values, approximate=False)


def contract_rows(left, right):
    return lax.dot_general(
        left, right, (((0,), (0,)), ((), ())), preferred_element_type=jnp.float32
    )


def contract_cols(left, right):
    return lax.dot_general(
        left, right, (((1,), (1,)), ((), ())), preferred_element_type=jnp.float32
    )


def exchange(values):
    return lax.ppermute(values, "shard", [(s, s ^ 1) for s in range(64)])


def forward_layer(inputs, gathered, cosine, sine, causal):
    w_qkv, b_qkv, w_out, w_up, b_up, w_down, gain, shift, out_bias = gathered
    count = inputs.shape[0]
    centred = inputs - jnp.mean(inputs, -1, keepdims=True)
    inv_std = lax.rsqrt(jnp.mean(centred * centred, -1, keepdims=True) + EPS)
    normed = centred * inv_std
    hidden = (normed * gain + shift).astype(jnp.bfloat16)
    hidden = jnp.concatenate([hidden, exchange(hidden)], 0)
    joined = jnp.dot(hidden, w_qkv, preferred_element_type=jnp.float32) + b_qkv
    split_shape = (2, count, 8, HEAD_DIM)
    query = rotate(joined[:, :512].reshape(split_shape), cosine, sine).astype(jnp.bfloat16)
    key_rot = rotate(joined[:, 512:1024].reshape(split_shape), cosine, sine).astype(jnp.bfloat16)
    values = joined[:, 1024:].reshape(split_shape).astype(jnp.bfloat16)
    scores = jnp.einsum(
        "gshd,gthd->ghst", query, key_rot, preferred_element_type=jnp.float32
    ) * HEAD_DIM ** (-0.5)
    scores = jnp.where(causal, scores, FILL)
    highest = jnp.max(scores, -1, keepdims=True)
    expo = jnp.exp(scores - highest)
    total = jnp.sum(expo, -1, keepdims=True)
    probs = (expo / total).astype(jnp.bfloat16)
    log_total = highest + jnp.log(total)
    mixed = jnp.einsum("ghst,gthd->gshd", probs, values, preferred_element_type=jnp.float32)
    mixed = mixed.reshape(2 * count, 512).astype(jnp.bfloat16)
    attended = jnp.dot(mixed, w_out, preferred_element_type=jnp.float32)
    upward = jnp.dot(hidden, w_up, preferred_element_type=jnp.float32) + b_up
    active = gelu_exact(upward).astype(jnp.bfloat16)
    lowered = jnp.dot(active, w_down, preferred_element_type=jnp.float32)
    partial = attended + lowered
    outputs = inputs + (partial[:count] + exchange(partial[count:])) + out_bias
    kept = (normed, inv_std, hidden, query, key_rot, values, log_total, mixed, upward, active)
    return (outputs, kept)


def backward_layer(upstream, kept, gathered, cosine, sine, causal):
    w_qkv, b_qkv, w_out, w_up, b_up, w_down, gain, shift, out_bias = gathered
    normed, inv_std, hidden, query, key_rot, values, log_total, mixed, upward, active = kept
    count = upstream.shape[0]
    split_shape = (2, count, 8, HEAD_DIM)
    out_bias_grad = jnp.sum(upstream, 0)
    up_low = upstream.astype(jnp.bfloat16)
    up_low = jnp.concatenate([up_low, exchange(up_low)], 0)
    w_down_grad = contract_rows(active, up_low).astype(jnp.bfloat16)
    d_active = contract_cols(up_low, w_down)
    unused, gelu_pull = jax.vjp(gelu_exact, upward)
    d_upward = gelu_pull(d_active)[0].astype(jnp.bfloat16)
    w_up_grad = contract_rows(hidden, d_upward).astype(jnp.bfloat16)
    b_up_grad = jnp.sum(d_upward.astype(jnp.float32), 0)
    w_out_grad = contract_rows(mixed, up_low).astype(jnp.bfloat16)
    d_mixed = contract_cols(up_low, w_out).astype(jnp.bfloat16).reshape(split_shape)
    scores = jnp.einsum(
        "gshd,gthd->ghst", query, key_rot, preferred_element_type=jnp.float32
    ) * HEAD_DIM ** (-0.5)
    scores = jnp.where(causal, scores, FILL)
    probs_full = jnp.exp(scores - log_total)
    d_probs = jnp.einsum("gshd,gthd->ghst", d_mixed, values, preferred_element_type=jnp.float32)
    row_terms = jnp.sum(d_probs * probs_full, -1, keepdims=True)
    d_scores = (probs_full * (d_probs - row_terms)).astype(jnp.bfloat16)
    d_query = jnp.einsum(
        "ghst,gthd->gshd", d_scores, key_rot, preferred_element_type=jnp.float32
    ) * HEAD_DIM ** (-0.5)
    d_key = jnp.einsum(
        "ghst,gshd->gthd", d_scores, query, preferred_element_type=jnp.float32
    ) * HEAD_DIM ** (-0.5)
    d_values = jnp.einsum(
        "ghst,gshd->gthd", probs_full.astype(jnp.bfloat16), d_mixed,
        preferred_element_type=jnp.float32,
    )
    wide = (2 * count, 512)
    d_query = rotate(d_query, cosine, -sine).reshape(wide)
    d_key = rotate(d_key, cosine, -sine).reshape(wide)
    d_joined = jnp.concatenate([d_query, d_key, d_values.reshape(wide)], 1).astype(jnp.bfloat16)
    w_qkv_grad = contract_rows(hidden, d_joined).astype(jnp.bfloat16)
    b_qkv_grad = jnp.sum(d_joined.astype(jnp.float32), 0)
    d_hidden = contract_cols(d_joined, w_qkv) + contract_cols(d_upward, w_up)
    d_hidden = d_hidden[:count] + exchange(d_hidden[count:])
    gain_grad = jnp.sum(d_hidden * normed, 0)
    shift_grad = jnp.sum(d_hidden, 0)
    scaled = d_hidden * gain
    d_inputs = upstream + inv_std * (
        scaled
        - jnp.mean(scaled, -1, keepdims=True)
        - normed * jnp.mean(scaled * normed, -1, keepdims=True)
    )
    large = (w_qkv_grad, w_up_grad, w_out_grad, w_down_grad)
    small = (b_qkv_grad, b_up_grad, gain_grad, shift_grad, out_bias_grad)
    return (d_inputs, large, small)


def pack_small(b_qkv, b_up, ln_gain, ln_bias, out_bias):
    own = jnp.concatenate([b_qkv, b_up, ln_gain, ln_bias, out_bias], 1).reshape(320)
    return jnp.pad(own, (0, 2048 - 320)).reshape(16, 128)


def unpack_small(full, core):
    rows = full.reshape(64, 2048)[:, :320].reshape(64, 2, 160).astype(jnp.float32)
    layers = []
    for layer_at in range(LAYERS):
        b_qkv = rows[:, layer_at, :48].reshape(3, 2, 512)
        b_qkv = lax.dynamic_index_in_dim(b_qkv, core, 1, False).reshape(1536)
        b_up = rows[:, layer_at, 48:112].reshape(2, 2048)
        b_up = lax.dynamic_index_in_dim(b_up, core, 0, False)
        rest = [rows[:, layer_at, 112 + 16 * i : 128 + 16 * i].reshape(1024) for i in range(3)]
        layers.append((b_qkv, b_up, *rest))
    return layers


def pack_small_grads(layers, core):
    flag = jnp.stack([core == 0, core == 1]).astype(jnp.float32)
    found = []
    for b_qkv, b_up, gain, shift, out_bias in layers:
        found.append((b_qkv.reshape(3, 1, 512) * flag[None, :, None]).reshape(64, 48))
        found.append((b_up.reshape(1, 2048) * flag[:, None]).reshape(64, 64))
        found.extend([gain.reshape(64, 16), shift.reshape(64, 16), out_bias.reshape(64, 16)])
    return jnp.pad(jnp.concatenate(found, 1), ((0, 0), (0, 704))).reshape(2, 4, 4, 16, 128)


def on_device(
    tokens, w_qkv, b_qkv, w_out, w_up, b_up, w_down, ln_gain, ln_bias, out_bias, out_grad
):
    core = lax.axis_index("shard") % 2
    count = tokens.shape[0]
    cosine, sine = tables(count)
    causal = jnp.tril(jnp.ones((count, count), jnp.bool_))
    found = gather(
        pack_small(b_qkv, b_up, ln_gain, ln_bias, out_bias), halves(w_qkv), w_up, w_out, w_down
    )
    small = unpack_small(found[0], core)
    current = tokens.astype(jnp.float32)
    gathered_all = []
    kept_all = []
    for layer_at in range(LAYERS):
        wq, wu, wo, wd = found[1 + 4 * layer_at : 5 + 4 * layer_at]
        bq, bu, gain, shift, ob = small[layer_at]
        gathered = (
            wq.reshape(1024, 1536),
            bq,
            wo.reshape(512, 1024),
            wu.reshape(1024, 2048),
            bu,
            wd.reshape(2048, 1024),
            gain,
            shift,
            ob,
        )
        current, kept = forward_layer(current, gathered, cosine, sine, causal)
        gathered_all.append(gathered)
        kept_all.append(kept)
    outcome = current.astype(jnp.bfloat16)
    upstream = out_grad.astype(jnp.float32)
    large = [None] * LAYERS
    small_grads = [None] * LAYERS
    for layer_at in reversed(range(LAYERS)):
        upstream, large[layer_at], small_grads[layer_at] = backward_layer(
            upstream, kept_all[layer_at], gathered_all[layer_at], cosine, sine, causal
        )
    blocks = []
    for layer_at in range(LAYERS):
        q, u, o, d = large[layer_at]
        blocks.append(
            [
                q.reshape(2, 4, 4, 32, 1536),
                u.reshape(2, 4, 4, 32, 2048),
                o.reshape(1, 4, 4, 32, 1024),
                d.reshape(1, 4, 4, 128, 1024),
            ]
        )
    g_qkv, g_up, g_out, g_down, g_small = scatter(blocks, pack_small_grads(small_grads, core))
    g_small = g_small.reshape(1024)[:320].reshape(2, 160)
    return (
        outcome,
        upstream,
        g_qkv,
        g_small[:, :48],
        g_out,
        g_up,
        g_small[:, 48:112],
        g_down,
        g_small[:, 112:128],
        g_small[:, 128:144],
        g_small[:, 144:160],
    )


def solution(mesh):
    placed = (
        P(("rep", "shard"), None),
        P(None, "shard", None),
        P(None, "shard"),
        P(None, "shard", None),
        P(None, "shard", None),
        P(None, "shard"),
        P(None, "shard", None),
        P(None, "shard"),
        P(None, "shard"),
        P(None, "shard"),
        P(("rep", "shard"), None),
    )
    return jax.shard_map(
        on_device,
        mesh=mesh,
        in_specs=placed,
        out_specs=(
            P(("rep", "shard"), None),
            P(("rep", "shard"), None),
            P(None, "shard", None),
            P(None, "shard"),
            P(None, "shard", None),
            P(None, "shard", None),
            P(None, "shard"),
            P(None, "shard", None),
            P(None, "shard"),
            P(None, "shard"),
            P(None, "shard"),
        ),
        check_vma=False,
    )
```

```python
import functools
import math

import jax
import jax.numpy as jnp
import numpy as np
from jax import lax
from jax.experimental import pallas as pl
from jax.experimental.pallas import tpu as pltpu
from jax.sharding import PartitionSpec as P


MESH = pl.DeviceIdType.MESH
LANE = 128
LAYERS = 2


def place():
    xl = lax.axis_index("rep")
    s = lax.axis_index("shard")
    return xl, s // 32, (s // 8) % 4, (s // 2) % 4, s % 2


def at(xl, xh, z, y, c):
    return (xl, xh * 32 + z * 8 + y * 2 + c)


def around(value, step):
    return lax.rem(value + (step + 4), 4)


def meet(others):
    barrier = pltpu.get_barrier_semaphore()
    for other in others:
        pl.semaphore_signal(barrier, inc=1, device_id=other, device_id_type=MESH)
    pl.semaphore_wait(barrier, len(others))


GATHERED = (
    ("small", True, 16, 128, 0, 1),
    ("qkv", True, 32, 1536, 4, 8),
    ("up", True, 32, 2048, 5, 11),
    ("out", False, 32, 1024, 3, 5),
    ("down", False, 128, 1024, 3, 5),
)
SLOTS = 18


class Stream:
    def __init__(self, number, spec, source, target, send, recv, xl, xh, z, y, core):
        self.name, self.by_columns, self.rows, self.columns, self.swapped, self.width = spec
        self.number = number
        self.source = source
        self.target = target
        self.send, self.recv = send, recv
        self.xl, self.xh, self.z, self.y, self.core = xl, xh, z, y, core
        self.half = self.rows // 2
        self.wide = pl.ds(pl.multiple_of(xl * (self.swapped * LANE), LANE), self.width * LANE)
        self.mine = pl.ds(
            pl.multiple_of(xl * ((self.width - self.swapped) * LANE) + xl * (self.swapped * LANE), LANE),
            max(self.swapped, 1) * LANE,
        )
        self.theirs = pl.ds(
            pl.multiple_of((1 - xl) * (self.width * LANE), LANE), max(self.swapped, 1) * LANE
        )
        self.across = lambda core_of: at(1 - xl, 1 - xh, z, y, core_of)
        self.partner = at(1 - xl, xh, z, y, core) if core == 0 else self.across(core)
        if core == 0:
            self.first, self.second = y, z
        else:
            self.first, self.second = z, y
        self.sent = []

    def neighbour(self, ring, step):
        z, y = self.z, self.y
        if (ring == 0) == (self.core == 0):
            y = around(y, step)
        else:
            z = around(z, step)
        return at(self.xl, self.xh, z, y, self.core)

    def block(self, first, rows, columns):
        if self.core == 0:
            return self.target.at[:, self.second, first, rows, columns]
        return self.target.at[:, first, self.second, rows, columns]

    def line(self, second, rows, columns):
        if self.core == 0:
            return self.target.at[:, second, :, rows, columns]
        return self.target.at[:, :, second, rows, columns]

    def push(self, source, target, slot, device):
        copy = pltpu.make_async_remote_copy(
            source,
            target,
            self.send.at[self.number, slot],
            self.recv.at[self.number, slot],
            device_id=device,
            device_id_type=MESH,
        )
        copy.start()
        self.sent.append((source, slot))

    def arrived(self, region, slot):
        pltpu.make_async_copy(region, region, self.recv.at[self.number, slot]).wait()

    def part(self, core_of):
        return pl.ds(core_of * self.half, self.half)

    def stage0(self):
        xh, z, y, core = self.xh, self.z, self.y, self.core
        whole = slice(None)
        if self.by_columns:
            here = self.target.at[xh, z, y, self.part(core), :]
            pltpu.make_async_copy(
                self.source(core), here, self.recv.at[self.number, xh * 2 + core]
            ).start()
            for slot, half, device in (
                (0, 1 - core, at(self.xl, xh, z, y, 1 - core)),
                (1, core, self.across(core)),
                (2, 1 - core, self.across(1 - core)),
            ):
                copy = pltpu.make_async_remote_copy(
                    self.source(half),
                    here,
                    self.send.at[self.number, slot],
                    self.recv.at[self.number, xh * 2 + core],
                    device_id=device,
                    device_id_type=MESH,
                )
                copy.start()
                self.sent.append((self.source(half), slot))
        else:
            here = self.target.at[0, z, y, self.part(core), :]
            mine = self.source(0)

            @pl.when(xh == core)
            def _():
                pltpu.make_async_copy(mine, here, self.recv.at[self.number, core]).start()

            @pl.when(xh != core)
            def _():
                pltpu.make_async_remote_copy(
                    mine,
                    here,
                    self.send.at[self.number, 0],
                    self.recv.at[self.number, core],
                    device_id=at(self.xl, xh, z, y, 1 - core),
                    device_id_type=MESH,
                ).start()

            pltpu.make_async_remote_copy(
                mine,
                here,
                self.send.at[self.number, 1],
                self.recv.at[self.number, core],
                device_id=self.across(xh),
                device_id_type=MESH,
            ).start()
            self.sent.append((mine, 1))

    def stage1(self):
        whole = slice(None)
        for bank in range(2 if self.by_columns else 1):
            for core_of in range(2):
                self.arrived(
                    self.target.at[bank, self.z, self.y, self.part(core_of), :], bank * 2 + core_of
                )
        own = self.block(self.first, whole, self.wide)
        self.push(own, own, 4, self.neighbour(0, 1))
        self.push(own, own, 5, self.neighbour(0, -1))

    def share(self, region, slot):
        if self.swapped:
            self.push(region(self.mine), region(self.mine), slot, self.partner)

    def stage2(self):
        whole = slice(None)
        for step, slot in ((-1, 4), (1, 5)):
            origin = around(self.first, step)
            self.arrived(self.block(origin, whole, self.wide), slot)
            half = self.block(origin, self.part(slot - 4), self.wide)
            self.push(half, half, slot + 2, self.neighbour(0, -step))
            self.share(lambda columns: self.block(origin, whole, columns), slot + 8)

    def stage3(self):
        whole = slice(None)
        far = around(self.first, 2)
        for half in range(2):
            self.arrived(self.block(far, self.part(half), self.wide), 6 + half)
        own = self.line(self.second, whole, self.wide)
        self.push(own, own, 8, self.neighbour(1, 1))
        self.push(own, own, 9, self.neighbour(1, -1))
        self.share(lambda columns: self.block(far, whole, columns), 14)

    def stage4(self):
        whole = slice(None)
        for step, slot in ((-1, 8), (1, 9)):
            origin = around(self.second, step)
            self.arrived(self.line(origin, whole, self.wide), slot)
            half = self.line(origin, self.part(slot - 8), self.wide)
            self.push(half, half, slot + 2, self.neighbour(1, -step))
            self.share(lambda columns: self.line(origin, whole, columns), slot + 7)

    def stage5(self):
        whole = slice(None)
        far = around(self.second, 2)
        for half in range(2):
            self.arrived(self.line(far, self.part(half), self.wide), 10 + half)
        self.share(lambda columns: self.line(far, whole, columns), 17)

    def stage6(self):
        whole = slice(None)
        if self.swapped:
            for step, slot in ((-1, 12), (1, 13), (2, 14)):
                self.arrived(self.block(around(self.first, step), whole, self.theirs), slot)
            for step, slot in ((-1, 15), (1, 16), (2, 17)):
                self.arrived(self.line(around(self.second, step), whole, self.theirs), slot)

    def finish(self):
        for source, slot in self.sent:
            pltpu.make_async_copy(source, source, self.send.at[self.number, slot]).wait()
        if not self.by_columns:

            @pl.when(self.xh != self.core)
            def _():
                mine = self.source(0)
                pltpu.make_async_copy(mine, mine, self.send.at[self.number, 0]).wait()


def streams_of(sources, targets, send, recv, core, xl, xh, z, y, layers):
    found = []
    small, qkv, up, out, down = sources
    for layer_at in layers:
        from_args = (
            lambda half: small,
            lambda half, layer_at=layer_at: qkv.at[half, layer_at],
            lambda half, layer_at=layer_at: up.at[layer_at, :, pl.ds(half * 2048, 2048)],
            lambda half, layer_at=layer_at: out.at[layer_at],
            lambda half, layer_at=layer_at: down.at[layer_at],
        )
        for spec, source in zip(GATHERED, from_args):
            if spec[0] == "small" and layer_at != layers[0]:
                continue
            number = len(found)
            found.append(
                Stream(number, spec, source, targets[number], send, recv, xl, xh, z, y, core)
            )
    return found


def gather_kernel(small, qkv, up, out, down, *rest):
    targets, (send, recv) = rest[:-2], rest[-2:]
    xl, xh, z, y, c = place()
    meet(
        [
            at(xl, xh, z, y, 1 - c),
            at(1 - xl, 1 - xh, z, y, c),
            at(1 - xl, 1 - xh, z, y, 1 - c),
            at(1 - xl, xh, z, y, c),
            at(xl, xh, around(z, 1), y, c),
            at(xl, xh, around(z, -1), y, c),
            at(xl, xh, z, around(y, 1), c),
            at(xl, xh, z, around(y, -1), c),
        ]
    )

    def run(core):
        streams = streams_of(
            (small, qkv, up, out, down), targets, send, recv, core, xl, xh, z, y, range(LAYERS)
        )
        for tick in range(len(streams) + 6):
            for stage in range(7):
                if 0 <= tick - stage < len(streams):
                    getattr(streams[tick - stage], f"stage{stage}")()
        for stream in streams:
            stream.finish()

    for core in range(2):
        pl.when(c == core)(functools.partial(run, core))


def gather(small, qkv, up, out, down):
    shapes = []
    for layer_at in range(LAYERS):
        for name, by_columns, rows, columns, swapped, width in GATHERED:
            if name == "small" and layer_at:
                continue
            shapes.append(
                jax.ShapeDtypeStruct(
                    (2 if by_columns else 1, 4, 4, rows, columns),
                    jnp.float32 if name == "small" else jnp.bfloat16,
                )
            )
    return pl.pallas_call(
        gather_kernel,
        out_shape=shapes,
        in_specs=[pl.BlockSpec(memory_space=pltpu.HBM)] * 5,
        out_specs=[pl.BlockSpec(memory_space=pltpu.HBM)] * len(shapes),
        scratch_shapes=[
            pltpu.SemaphoreType.DMA((len(shapes), SLOTS)),
            pltpu.SemaphoreType.DMA((len(shapes), SLOTS)),
        ],
        name="gather",
        compiler_params=pltpu.CompilerParams(collective_id=0, has_side_effects=True),
    )(small, qkv, up, out, down)


def halves(w_qkv):
    rows = w_qkv.shape[1]
    return w_qkv.reshape(LAYERS, rows, 3, 2, 512).transpose(3, 0, 1, 2, 4).reshape(
        2, LAYERS, rows, 1536
    )


SUMMED = (
    ("qkv", True, 32, 1536, 3, 9),
    ("up", True, 32, 2048, 4, 12),
    ("out", False, 32, 1024, 2, 6),
    ("down", False, 128, 1024, 2, 6),
)
SMALL = ("small", True, 16, 128, 0, 1)
SUM_SLOTS = 18


def scratch_of(spec):
    name, by_columns, rows, columns, swapped, width = spec
    banks = 2 if by_columns else 1
    kind = jnp.float32 if name == "small" else jnp.bfloat16
    wide = width * LANE
    return [
        pltpu.VMEM((banks, 4, 4, rows, columns), kind),
        pltpu.VMEM((banks, 4, 4, rows, max(swapped, 1) * LANE) if swapped else (8, LANE), kind),
        pltpu.VMEM((2, banks, 4, rows // 2, wide), kind),
        pltpu.VMEM((2, banks, 4, rows, wide), kind),
        pltpu.VMEM((2, banks, rows // 2, wide), kind),
        pltpu.VMEM((2, banks, rows, wide), kind),
        pltpu.VMEM((3, rows, wide), kind),
        pltpu.VMEM((rows, columns), jnp.float32),
        pltpu.VMEM((2, 8, LANE), jnp.float32),
    ]


class Sum:
    def __init__(self, number, spec, source, outputs, buffers, send, recv, xl, xh, z, y, core):
        self.name, self.by_columns, self.rows, self.columns, self.swapped, self.width = spec
        self.number, self.source, self.outputs = number, source, outputs
        (
            self.total,
            self.swap,
            self.far_line,
            self.near_line,
            self.far_block,
            self.near_block,
            self.last,
            self.ready,
            self.tail,
        ) = buffers
        self.send, self.recv = send, recv
        self.xl, self.xh, self.z, self.y, self.core = xl, xh, z, y, core
        self.banks = 2 if self.by_columns else 1
        self.half = self.rows // 2
        s, w = self.swapped, self.width
        self.wide = pl.ds(pl.multiple_of(xl * (s * LANE), LANE), w * LANE)
        self.mine = pl.ds(pl.multiple_of(xl * (w * LANE), LANE), max(s, 1) * LANE)
        self.theirs = pl.ds(pl.multiple_of((1 - xl) * (w * LANE), LANE), max(s, 1) * LANE)
        self.beside = at(1 - xl, xh, z, y, core)
        self.across = at(1 - xl, 1 - xh, z, y, core)
        self.beyond = at(xl, 1 - xh, z, y, core)
        self.sibling = at(xl, xh, z, y, 1 - core)
        self.partner = self.beside if core == 0 else self.across
        self.first, self.second = (y, z) if core == 0 else (z, y)
        self.sent = []

    def neighbour(self, ring, step):
        z, y = self.z, self.y
        if (ring == 0) == (self.core == 0):
            y = around(y, step)
        else:
            z = around(z, step)
        return at(self.xl, self.xh, z, y, self.core)

    def block(self, first, rows, columns):
        if self.core == 0:
            return self.total.at[:, self.second, first, rows, columns]
        return self.total.at[:, first, self.second, rows, columns]

    def line(self, second, rows, columns):
        if self.core == 0:
            return self.total.at[:, second, :, rows, columns]
        return self.total.at[:, :, second, rows, columns]

    def push(self, source, target, slot, device):
        copy = pltpu.make_async_remote_copy(
            source,
            target,
            self.send.at[self.number, slot],
            self.recv.at[self.number, slot],
            device_id=device,
            device_id_type=MESH,
        )
        copy.start()
        return (source, slot)

    def arrived(self, region, slot):
        pltpu.make_async_copy(region, region, self.recv.at[self.number, slot]).wait()

    def part(self, core_of):
        return pl.ds(core_of * self.half, self.half)

    def stage0(self):
        pltpu.make_async_copy(self.source, self.total, self.recv.at[self.number, 17]).start()

    def stage1(self):
        self.arrived(self.total, 17)
        if self.swapped:
            whole = self.total.at[:, :, :, :, self.theirs]
            self.sent.append(self.push(whole, self.swap, 0, self.partner))

    def stage2(self):
        whole = slice(None)
        if self.swapped:
            self.arrived(self.swap, 0)

            def add(step, carry):
                bank, z, y = step // 16, (step // 4) % 4, step % 4
                self.total[bank, z, y, :, self.mine] = (
                    self.total[bank, z, y, :, self.mine].astype(jnp.float32)
                    + self.swap[bank, z, y].astype(jnp.float32)
                ).astype(self.total.dtype)
                return carry

            lax.fori_loop(0, self.banks * 16, add, 0)
        far = around(self.second, 2)
        for half in range(2):
            self.sent.append(
                self.push(
                    self.line(far, self.part(half), self.wide),
                    self.far_line.at[half],
                    1 + half,
                    self.neighbour(1, 1 - 2 * half),
                )
            )

    def stage3(self):
        for half in range(2):
            self.arrived(self.far_line.at[half], 1 + half)
            to = around(self.second, 1 - 2 * half)
            rows = self.part(half)

            def add(step, carry):
                bank, at_ = step // 4, step % 4
                region = self.line(to, rows, self.wide).at[bank, at_]
                region[...] = (
                    region[...].astype(jnp.float32)
                    + self.far_line[half, bank, at_].astype(jnp.float32)
                ).astype(self.total.dtype)
                return carry

            lax.fori_loop(0, self.banks * 4, add, 0)
            self.sent.append(
                self.push(
                    self.line(to, slice(None), self.wide),
                    self.near_line.at[half],
                    3 + half,
                    self.neighbour(1, 1 - 2 * half),
                )
            )

    def stage4(self):
        for half in range(2):
            self.arrived(self.near_line.at[half], 3 + half)

        def add(step, carry):
            bank, at_ = step // 4, step % 4
            region = self.line(self.second, slice(None), self.wide).at[bank, at_]
            region[...] = (
                region[...].astype(jnp.float32)
                + self.near_line[0, bank, at_].astype(jnp.float32)
                + self.near_line[1, bank, at_].astype(jnp.float32)
            ).astype(self.total.dtype)
            return carry

        lax.fori_loop(0, self.banks * 4, add, 0)
        far = around(self.first, 2)
        for half in range(2):
            self.sent.append(
                self.push(
                    self.block(far, self.part(half), self.wide),
                    self.far_block.at[half],
                    5 + half,
                    self.neighbour(0, 1 - 2 * half),
                )
            )

    def stage5(self):
        for half in range(2):
            self.arrived(self.far_block.at[half], 5 + half)
            to = around(self.first, 1 - 2 * half)
            for bank in range(self.banks):
                region = self.block(to, self.part(half), self.wide).at[bank]
                region[...] = (
                    region[...].astype(jnp.float32)
                    + self.far_block[half, bank].astype(jnp.float32)
                ).astype(self.total.dtype)
            self.sent.append(
                self.push(
                    self.block(to, slice(None), self.wide),
                    self.near_block.at[half],
                    7 + half,
                    self.neighbour(0, 1 - 2 * half),
                )
            )

    def stage6(self):
        for half in range(2):
            self.arrived(self.near_block.at[half], 7 + half)
        own = self.block(self.first, slice(None), self.wide)
        for bank in range(self.banks):
            region = own.at[bank]
            region[...] = (
                region[...].astype(jnp.float32)
                + self.near_block[0, bank].astype(jnp.float32)
                + self.near_block[1, bank].astype(jnp.float32)
            ).astype(self.total.dtype)
        if self.by_columns:
            self.sent.append(self.push(own.at[self.xh], self.last.at[0], 9, self.beside))
            self.sent.append(self.push(own.at[1 - self.xh], self.last.at[1], 10, self.across))
            self.sent.append(self.push(own.at[1 - self.xh], self.last.at[2], 11, self.beyond))
        else:

            @pl.when(self.xh == self.core)
            def _():
                self.push(own.at[0], self.last.at[0], 9, self.beside)

            @pl.when(self.xh != self.core)
            def _():
                self.push(own.at[0], self.last.at[1], 10, self.across)
                self.push(own.at[0], self.last.at[2], 11, self.beyond)

    def add_last(self):
        for slot in range(3):
            self.arrived(self.last.at[slot], 9 + slot)
        s, w = self.swapped, self.width
        c = w - s
        own = self.block(self.first, slice(None), self.wide).at[self.xh if self.by_columns else 0]
        self.ready[:, self.wide] = own[...].astype(jnp.float32) + self.last[2].astype(jnp.float32)
        if s:
            there = pl.ds(pl.multiple_of((1 - self.xl) * (c * LANE), LANE), s * LANE)
            self.ready[:, self.theirs] = self.last[0, :, there].astype(jnp.float32) + self.last[
                1, :, there
            ].astype(jnp.float32)
        middle = pl.ds(s * LANE, c * LANE)
        there = pl.ds(pl.multiple_of(self.xl * (s * LANE), LANE), c * LANE)
        self.ready[:, middle] = (
            self.ready[:, middle]
            + self.last[0, :, there].astype(jnp.float32)
            + self.last[1, :, there].astype(jnp.float32)
        )

    def pieces(self, core_of, target):
        rows = self.part(core_of)
        if self.name == "qkv":
            return [
                (
                    self.ready.at[rows, pl.ds(third * 512, 512)],
                    target.at[:, pl.ds(third * 1024 + self.core * 512, 512)],
                )
                for third in range(3)
            ]
        if self.name == "up":
            return [(self.ready.at[rows, :], target.at[:, pl.ds(self.core * 2048, 2048)])]
        return [(self.ready.at[rows, :], target)]

    def deliver(self):
        core = self.core
        for index, (source, target) in enumerate(self.pieces(core, self.outputs)):
            pltpu.make_async_copy(source, target, self.recv.at[self.number, 15 + index]).start()
        for index, (source, target) in enumerate(self.pieces(1 - core, self.outputs)):
            self.push(source, target, 12 + index, self.sibling)

    def delivered(self):
        for index, (source, target) in enumerate(self.pieces(self.core, self.outputs)):
            pltpu.make_async_copy(source, target, self.recv.at[self.number, 15 + index]).wait()
        for index, (source, target) in enumerate(self.pieces(1 - self.core, self.outputs)):
            pltpu.make_async_copy(source, source, self.send.at[self.number, 12 + index]).wait()

    def stage7(self):
        if self.name == "small":
            self.add_last()
            self.sent.append(
                self.push(
                    self.ready.at[self.part(1 - self.core), :], self.tail.at[0], 12, self.sibling
                )
            )
        elif self.by_columns:
            self.add_last()
            self.deliver()
        else:

            @pl.when(self.xh == self.core)
            def _():
                self.add_last()
                self.deliver()

    def stage8(self):
        core = self.core
        if self.name == "small":
            self.arrived(self.tail.at[0], 12)
            self.tail[1] = self.ready[self.part(core), :] + self.tail[0]
            copy = pltpu.make_async_copy(
                self.tail.at[1], self.outputs, self.recv.at[self.number, 15]
            )
            copy.start()
            copy.wait()
        elif self.by_columns:
            self.delivered()
            for index, (source, target) in enumerate(self.pieces(1 - core, self.outputs)):
                there = target
                self.arrived(source, 12 + index)
        else:

            @pl.when(self.xh == core)
            def _():
                self.delivered()

            @pl.when(self.xh != core)
            def _():
                self.arrived(self.outputs, 12)

        for source, slot in self.sent:
            pltpu.make_async_copy(source, source, self.send.at[self.number, slot]).wait()
        if not self.by_columns:
            own = self.block(self.first, slice(None), self.wide).at[0]

            @pl.when(self.xh == core)
            def _():
                pltpu.make_async_copy(own, own, self.send.at[self.number, 9]).wait()

            @pl.when(self.xh != core)
            def _():
                pltpu.make_async_copy(own, own, self.send.at[self.number, 10]).wait()
                pltpu.make_async_copy(own, own, self.send.at[self.number, 11]).wait()


def plan(layers):
    found = []
    for layer_at in reversed(range(layers)):
        for which, spec in enumerate(SUMMED):
            found.append((spec, layer_at, which))
    found.insert(len(found) - 3, (SMALL, None, 4))
    return found


def scatter_kernel(streams, *rest):
    count = len(streams)
    sources, rest = rest[:count], rest[count:]
    outputs, rest = rest[:5], rest[5:]
    buffers, (send, recv) = rest[:-2], rest[-2:]
    xl, xh, z, y, c = place()
    meet(
        [
            at(xl, xh, z, y, 1 - c),
            at(1 - xl, 1 - xh, z, y, c),
            at(xl, 1 - xh, z, y, c),
            at(1 - xl, xh, z, y, c),
            at(xl, xh, around(z, 1), y, c),
            at(xl, xh, around(z, -1), y, c),
            at(xl, xh, z, around(y, 1), c),
            at(xl, xh, z, around(y, -1), c),
        ]
    )

    def run(core):
        sums = []
        for number, (spec, layer_at, which) in enumerate(streams):
            target = outputs[which] if layer_at is None else outputs[which].at[layer_at]
            sums.append(
                Sum(
                    number,
                    spec,
                    sources[number],
                    target,
                    buffers[9 * number : 9 * number + 9],
                    send,
                    recv,
                    xl,
                    xh,
                    z,
                    y,
                    core,
                )
            )
        for item in sums:
            item.stage0()
        for tick in range(len(sums) + 7):
            for stage in range(1, 9):
                if 0 <= tick - (stage - 1) < len(sums):
                    getattr(sums[tick - (stage - 1)], f"stage{stage}")()

    for core in range(2):
        pl.when(c == core)(functools.partial(run, core))


def scatter(grads, small):
    streams = plan(LAYERS)
    sources = [
        small if layer_at is None else grads[layer_at][which] for spec, layer_at, which in streams
    ]
    scratch = []
    for spec, layer_at, which in streams:
        scratch.extend(scratch_of(spec))
    f32 = jnp.float32
    return pl.pallas_call(
        functools.partial(scatter_kernel, streams),
        out_shape=[
            jax.ShapeDtypeStruct((LAYERS, 16, 3072), f32),
            jax.ShapeDtypeStruct((LAYERS, 16, 4096), f32),
            jax.ShapeDtypeStruct((LAYERS, 16, 1024), f32),
            jax.ShapeDtypeStruct((LAYERS, 64, 1024), f32),
            jax.ShapeDtypeStruct((8, LANE), f32),
        ],
        in_specs=[pl.BlockSpec(memory_space=pltpu.HBM)] * len(sources),
        out_specs=[pl.BlockSpec(memory_space=pltpu.HBM)] * 5,
        scratch_shapes=scratch
        + [
            pltpu.SemaphoreType.DMA((len(streams), SUM_SLOTS)),
            pltpu.SemaphoreType.DMA((len(streams), SUM_SLOTS)),
        ],
        name="scatter",
        compiler_params=pltpu.CompilerParams(
            collective_id=1, has_side_effects=True, vmem_limit_bytes=60 * 2**20
        ),
    )(*sources)


COUNT = 256
BOTH = 512
D = 1024
HEAD_DIM = 64
ROT = 16
EPS = 1e-05
FILL = -1e30
F32 = jnp.float32
BF16 = jnp.bfloat16
TILE = 256


def turn_tables():
    places = np.arange(COUNT, dtype=np.float32)
    rates = np.float32(10000.0) ** (-np.arange(0, ROT, 2, dtype=np.float32) / np.float32(ROT))
    angles = places[:, None] * rates[None, :]
    cosine, sine = np.cos(angles), np.sin(angles)
    half = ROT // 2
    keep = np.ones((COUNT, HEAD_DIM), np.float32)
    ahead = np.zeros((COUNT, HEAD_DIM), np.float32)
    behind = np.zeros((COUNT, HEAD_DIM), np.float32)
    keep[:, :half] = cosine
    keep[:, half:ROT] = cosine
    ahead[:, :half] = -sine
    behind[:, half:ROT] = sine
    return np.stack([np.concatenate([t, t], 1) for t in (keep, ahead, behind)])


def turn(values, tables, sign):
    return values * tables[0] + sign * (
        pltpu.roll(values, LANE - ROT // 2, 1) * tables[1]
        + pltpu.roll(values, ROT // 2, 1) * tables[2]
    )


def dot(left, right):
    return jnp.dot(left, right, preferred_element_type=F32)


def dot_nt(left, right):
    return lax.dot_general(left, right, (((1,), (1,)), ((), ())), preferred_element_type=F32)


def dot_tn(left, right):
    return lax.dot_general(left, right, (((0,), (0,)), ((), ())), preferred_element_type=F32)


def columns_of(index, width=TILE):
    return pl.ds(pl.multiple_of(index * width, width), width)


def loop(count, body):
    def step(index, carry):
        body(index)
        return carry

    lax.fori_loop(0, count, step, 0)


KINDS = {
    "b_qkv": (0, 0, 48, 43691, 21),
    "b_up": (1, 0, 64, 1, 6),
    "gain": (2, 0, 16, 1, 4),
    "shift": (2, 16, 16, 1, 4),
    "out_bias": (2, 32, 16, 1, 4),
}
CHUNK = 512


def chunks_of(kind, core):
    if kind == "b_qkv":
        return [(t * CHUNK, t * 1024 + core * CHUNK) for t in range(3)]
    if kind == "b_up":
        return [(t * CHUNK, core * 2048 + t * CHUNK) for t in range(4)]
    return [(t * CHUNK, t * CHUNK) for t in range(2)]


def owner_masks(kind, start):
    row, lane, size, factor, shift = KINDS[kind]
    place_of = lax.broadcasted_iota(jnp.int32, (LANE, CHUNK), 1) + start
    owner = lax.shift_right_logical(place_of * factor, shift)
    within = place_of - owner * size + lane
    spread = lax.broadcasted_iota(jnp.int32, (LANE, CHUNK), 0) == within
    owned = lax.broadcasted_iota(jnp.int32, (64, CHUNK), 0) == owner[:64]
    return spread, owned


def unpack_vector(rows_ref, layer_at, kind, core, target):
    row = KINDS[kind][0] + 3 * layer_at
    held = rows_ref[pl.ds(row, 64, stride=8), :].astype(BF16)
    for place_at, start in chunks_of(kind, core):
        spread, owned = owner_masks(kind, start)
        every = dot(held, jnp.where(spread, 1.0, 0.0).astype(BF16))
        target[:, pl.ds(place_at, CHUNK)] = jnp.sum(
            jnp.where(owned, every, 0.0), 0, keepdims=True
        )


def pack_vectors(rows_ref, layer_at, core, vectors):
    found = {}
    for kind, vector in vectors.items():
        total = jnp.zeros((64, LANE), F32)
        for place_at, start in chunks_of(kind, core):
            spread, owned = owner_masks(kind, start)
            mine = jnp.where(owned, vector[:, pl.ds(place_at, CHUNK)], 0.0)
            total = total + lax.dot_general(
                mine,
                jnp.where(spread, 1.0, 0.0),
                (((1,), (1,)), ((), ())),
                precision=lax.Precision.HIGHEST,
                preferred_element_type=F32,
            )
        row = KINDS[kind][0]
        found[row] = found[row] + total if row in found else total
    for row, total in found.items():
        rows_ref[pl.ds(row + 3 * layer_at, 64, stride=8), :] = total


def centre(values):
    centred = values - jnp.mean(values, -1, keepdims=True)
    inv_std = lax.rsqrt(jnp.mean(centred * centred, -1, keepdims=True) + EPS)
    return centred * inv_std, inv_std


def norm_piece(x_ref, gain, shift, hidden):
    def body(index):
        rows = columns_of(index, 64)
        normed, unused = centre(x_ref[rows, :])
        hidden[rows, :] = (normed * gain[...] + shift[...]).astype(BF16)

    loop(COUNT // 64, body)


def joined_piece(third, hidden, w_qkv, b_qkv, tables, target):
    def body(index):
        columns = columns_of(index + third * 2)
        found = dot(hidden[...], w_qkv(columns)) + b_qkv[:, columns]
        for sequence in range(2):
            for pair in range(2):
                part = found[sequence * COUNT : (sequence + 1) * COUNT, pair * LANE : (pair + 1) * LANE]
                if third < 2:
                    part = turn(part, tables, 1.0)
                if third == 0:
                    part = part * HEAD_DIM**-0.5
                target[pl.ds(sequence * COUNT, COUNT), columns_of(index * 2 + pair, LANE)] = (
                    part.astype(BF16)
                )

    loop(2, body)


def first_head():
    return lax.broadcasted_iota(jnp.int32, (COUNT, LANE), 1) < HEAD_DIM


def only_head(values, half):
    keep = first_head() if half == 0 else jnp.logical_not(first_head())
    return jnp.where(keep, values, jnp.zeros_like(values))


def attention_piece(query, key, value, probs, mixed):
    def body(index):
        sequence, pair = index // 4, index % 4
        rows, columns = columns_of(sequence, COUNT), columns_of(pair, LANE)
        q2, k2, v2 = query[rows, columns], key[rows, columns], value[rows, columns]
        causal = lax.broadcasted_iota(jnp.int32, (COUNT, COUNT), 0) >= lax.broadcasted_iota(
            jnp.int32, (COUNT, COUNT), 1
        )
        out = []
        for half in range(2):
            scores = jnp.where(causal, dot_nt(only_head(q2, half), k2), FILL)
            expo = jnp.exp(scores - jnp.max(scores, -1, keepdims=True))
            prob = (expo * (1.0 / jnp.sum(expo, -1, keepdims=True))).astype(BF16)
            probs[index * 2 + half] = prob
            out.append(dot(prob, v2))
        mixed[rows, columns] = jnp.where(first_head(), out[0], out[1]).astype(BF16)

    loop(8, body)


def up_piece(hidden, w_up, b_up, active, slope):
    def body(index):
        columns = columns_of(index)
        upward = dot(hidden[...], w_up(columns)) + b_up[:, columns]
        spread = 0.5 + 0.5 * lax.erf(upward * (0.5**0.5))
        active[:, columns] = (upward * spread).astype(BF16)
        dense = jnp.exp(upward * upward * -0.5) * (1.0 / math.sqrt(2.0 * math.pi))
        slope[:, columns] = (spread + upward * dense).astype(BF16)

    loop(8, body)


def down_piece(active, w_down, mixed, w_out, partial):
    def body(index):
        columns = columns_of(index)
        partial[:, columns] = dot(mixed[...], w_out(columns)) + dot(active[...], w_down(columns))

    loop(4, body)


def residual_piece(x_ref, partial, received, out_bias, target):
    def body(index):
        rows = columns_of(index, 64)
        target[rows, :] = (
            x_ref[rows, :] + (partial[rows, :] + received[rows, :]) + out_bias[...]
        ).astype(target.dtype)

    loop(COUNT // 64, body)


def start_piece(dy, dy_low, out_bias_grad):
    def body(index):
        rows = columns_of(index, 64)
        values = dy[rows, :].astype(F32)
        dy_low[rows, :] = values.astype(BF16)
        out_bias_grad[...] += jnp.sum(values, 0, keepdims=True)

    out_bias_grad[...] = jnp.zeros_like(out_bias_grad)
    loop(COUNT // 64, body)


def flip_piece(source, target):
    rows, columns = source.shape
    for at_row in range(rows // TILE):

        def body(index, at_row=at_row):
            target[columns_of(index), pl.ds(at_row * TILE, TILE)] = source[
                pl.ds(at_row * TILE, TILE), columns_of(index)
            ].T

        loop(columns // TILE, body)


def rows_grad_piece(count, left, right, store):
    def body(index):
        store(index, dot_tn(left[:, columns_of(index)], right[...]).astype(BF16))

    loop(count, body)


def columns_grad_piece(count, left_flipped, right, store):
    def body(index):
        store(index, dot(left_flipped[...], right[:, columns_of(index)]).astype(BF16))

    loop(count, body)


def slope_piece(dy_low, w_down_rows, slope, d_up, b_up_grad):
    def body(index):
        columns = columns_of(index)
        found = (dot_nt(dy_low[...], w_down_rows(index)) * slope[:, columns].astype(F32)).astype(BF16)
        d_up[:, columns] = found
        b_up_grad[:, columns] = jnp.sum(found.astype(F32), 0, keepdims=True)

    loop(8, body)


def d_mixed_piece(dy_low, w_out_rows, d_mixed):
    def body(index):
        d_mixed[:, columns_of(index)] = dot_nt(dy_low[...], w_out_rows(index)).astype(BF16)

    loop(2, body)


def attention_back_piece(query, key, value, probs, d_mixed, tables, d_joined, b_qkv_grad):
    b_qkv_grad[...] = jnp.zeros_like(b_qkv_grad)

    def body(index):
        sequence, pair = index // 4, index % 4
        rows, columns = columns_of(sequence, COUNT), columns_of(pair, LANE)
        q2, k2, v2 = query[rows, columns], key[rows, columns], value[rows, columns]
        dm2 = d_mixed[rows, columns]
        found = []
        for half in range(2):
            prob = probs[index * 2 + half]
            full = prob.astype(F32)
            d_probs = dot_nt(only_head(dm2, half), v2)
            d_scores = (
                full * (d_probs - jnp.sum(d_probs * full, -1, keepdims=True))
            ).astype(BF16)
            found.append((dot(d_scores, k2), dot_tn(d_scores, q2), dot_tn(prob, dm2)))
        for third in range(3):
            part = jnp.where(first_head(), found[0][third], found[1][third])
            if third == 0:
                part = part * HEAD_DIM**-0.5
            if third < 2:
                part = turn(part, tables, -1.0)
            part = part.astype(BF16)
            there = columns_of(pair + third * 4, LANE)
            d_joined[rows, there] = part
            b_qkv_grad[:, there] += jnp.sum(part.astype(F32), 0, keepdims=True)

    loop(8, body)


def d_hidden_piece(d_joined, w_qkv_rows, d_up, w_up_rows, d_hidden):
    def body(index):
        d_hidden[:, columns_of(index)] = dot_nt(d_joined[...], w_qkv_rows(index)) + dot_nt(
            d_up[...], w_up_rows(index)
        )

    loop(4, body)


def norm_back_piece(x_ref, gain, dy, d_hidden, received, target, gain_grad, shift_grad):
    gain_grad[...] = jnp.zeros_like(gain_grad)
    shift_grad[...] = jnp.zeros_like(shift_grad)

    def body(index):
        rows = columns_of(index, 64)
        normed, inv_std = centre(x_ref[rows, :].astype(F32))
        total = d_hidden[rows, :] + received[rows, :]
        gain_grad[...] += jnp.sum(total * normed, 0, keepdims=True)
        shift_grad[...] += jnp.sum(total, 0, keepdims=True)
        scaled = total * gain[...]
        target[rows, :] = dy[rows, :].astype(F32) + inv_std * (
            scaled
            - jnp.mean(scaled, -1, keepdims=True)
            - normed * jnp.mean(scaled * normed, -1, keepdims=True)
        )

    loop(COUNT // 64, body)


class Pair:
    def __init__(self, send, recv):
        xl, xh, z, y, c = place()
        self.device = at(xl, xh, z, y, 1 - c)
        self.send, self.recv = send, recv

    def push(self, source, target, slot):
        pltpu.make_async_remote_copy(
            source,
            target,
            self.send.at[slot],
            self.recv.at[slot],
            device_id=self.device,
            device_id_type=MESH,
        ).start()

    def wait(self, source, target, slot):
        pltpu.make_async_copy(source, source, self.send.at[slot]).wait()
        pltpu.make_async_copy(target, target, self.recv.at[slot]).wait()


def forward_kernel(layer_at, x_in, rows_ref, w_qkv, w_up, w_out, w_down, tables, *rest):
    (
        x_out, hidden, query, key, value, probs, mixed, active, slope, gain,
        x_ref, b_qkv, b_up, shift, out_bias, partial, received, send, recv,
    ) = rest
    xl, xh, z, y, c = place()
    meet([at(xl, xh, z, y, 1 - c)])
    pair = Pair(send, recv)
    for core in range(2):

        @pl.when(c == core)
        def _():
            for kind, target in (
                ("b_qkv", b_qkv), ("b_up", b_up), ("gain", gain), ("shift", shift), ("out_bias", out_bias),
            ):
                unpack_vector(rows_ref, layer_at, kind, core, target)

    x_ref[...] = x_in[...].astype(F32)
    own, other = pl.ds(0, COUNT), pl.ds(COUNT, COUNT)
    norm_piece(x_ref, gain, shift, hidden)
    pair.push(hidden.at[own], hidden.at[other], 0)
    pair.wait(hidden.at[own], hidden.at[other], 0)
    for third, target in enumerate((query, key, value)):
        joined_piece(third, hidden, lambda n: w_qkv[:, n], b_qkv, tables, target)
    attention_piece(query, key, value, probs, mixed)
    up_piece(hidden, lambda n: w_up[:, n], b_up, active, slope)
    down_piece(active, lambda n: w_down[:, n], mixed, lambda n: w_out[:, n], partial)
    pair.push(partial.at[other], received, 1)
    pair.wait(partial.at[other], received, 1)
    residual_piece(x_ref, partial, received, out_bias, x_out)


def forward_call(layer_at, x, rows, w_qkv, w_up, w_out, w_down, tables):
    last = layer_at == LAYERS - 1
    vmem = pl.BlockSpec(memory_space=pltpu.VMEM)
    shape = jax.ShapeDtypeStruct
    return pl.pallas_call(
        functools.partial(forward_kernel, layer_at),
        out_shape=[
            shape((COUNT, D), BF16 if last else F32),
            shape((BOTH, D), BF16),
            shape((BOTH, 512), BF16),
            shape((BOTH, 512), BF16),
            shape((BOTH, 512), BF16),
            shape((16, COUNT, COUNT), BF16),
            shape((BOTH, 512), BF16),
            shape((BOTH, 2048), BF16),
            shape((BOTH, 2048), BF16),
            shape((1, D), F32),
        ],
        in_specs=[vmem] * 7,
        out_specs=[vmem] * 10,
        scratch_shapes=[
            pltpu.VMEM((COUNT, D), F32),
            pltpu.VMEM((1, 1536), F32),
            pltpu.VMEM((1, 2048), F32),
            pltpu.VMEM((1, D), F32),
            pltpu.VMEM((1, D), F32),
            pltpu.VMEM((BOTH, D), F32),
            pltpu.VMEM((COUNT, D), F32),
            pltpu.SemaphoreType.DMA((2,)),
            pltpu.SemaphoreType.DMA((2,)),
        ],
        name=f"forward{layer_at}",
        compiler_params=pltpu.CompilerParams(
            collective_id=2 + layer_at, has_side_effects=True, vmem_limit_bytes=60 * 2**20
        ),
    )(x, rows, w_qkv, w_up, w_out, w_down, tables)


def backward_kernel(
    layer_at, x_in, dy, hidden, query, key, value, probs, mixed, active, slope, gain,
    w_qkv, w_up, w_out, w_down, tables, *rest
):
    (
        dx, g_qkv, g_up, g_out, g_down, g_small,
        hidden_flipped, dy_low, d_up, d_mixed, d_joined, d_hidden, received,
        b_qkv_grad, b_up_grad, gain_grad, shift_grad, out_bias_grad, send, recv,
    ) = rest
    xl, xh, z, y, c = place()
    meet([at(xl, xh, z, y, 1 - c)])
    pair = Pair(send, recv)
    own, other = pl.ds(0, COUNT), pl.ds(COUNT, COUNT)
    start_piece(dy, dy_low, out_bias_grad)
    pair.push(dy_low.at[own], dy_low.at[other], 0)
    flip_piece(hidden, hidden_flipped)
    pair.wait(dy_low.at[own], dy_low.at[other], 0)

    def by_rows(target):
        def store(index, found):
            target[columns_of(index), :] = found

        return store

    def by_columns(target):
        def store(index, found):
            target[:, columns_of(index)] = found

        return store

    rows_grad_piece(8, active, dy_low, by_rows(g_down))
    slope_piece(dy_low, lambda n: w_down[columns_of(n), :], slope, d_up, b_up_grad)
    columns_grad_piece(8, hidden_flipped, d_up, by_columns(g_up))
    d_mixed_piece(dy_low, lambda n: w_out[columns_of(n), :], d_mixed)
    rows_grad_piece(2, mixed, dy_low, by_rows(g_out))
    attention_back_piece(query, key, value, probs, d_mixed, tables, d_joined, b_qkv_grad)
    d_hidden_piece(
        d_joined, lambda n: w_qkv[columns_of(n), :], d_up, lambda n: w_up[columns_of(n), :], d_hidden
    )
    pair.push(d_hidden.at[other], received, 1)
    columns_grad_piece(6, hidden_flipped, d_joined, by_columns(g_qkv))
    pair.wait(d_hidden.at[other], received, 1)
    norm_back_piece(x_in, gain, dy, d_hidden, received, dx, gain_grad, shift_grad)
    for core in range(2):

        @pl.when(c == core)
        def _():
            pack_vectors(
                g_small,
                0,
                core,
                {
                    "b_qkv": b_qkv_grad,
                    "b_up": b_up_grad,
                    "gain": gain_grad,
                    "shift": shift_grad,
                    "out_bias": out_bias_grad,
                },
            )


def backward_call(layer_at, x, dy, kept, weights, tables):
    vmem = pl.BlockSpec(memory_space=pltpu.VMEM)
    shape = jax.ShapeDtypeStruct
    return pl.pallas_call(
        functools.partial(backward_kernel, layer_at),
        out_shape=[
            shape((COUNT, D), F32),
            shape((D, 1536), BF16),
            shape((D, 2048), BF16),
            shape((512, D), BF16),
            shape((2048, D), BF16),
            shape((512, LANE), F32),
        ],
        in_specs=[vmem] * (2 + len(kept) + 5),
        out_specs=[vmem] * 6,
        scratch_shapes=[
            pltpu.VMEM((D, BOTH), BF16),
            pltpu.VMEM((BOTH, D), BF16),
            pltpu.VMEM((BOTH, 2048), BF16),
            pltpu.VMEM((BOTH, 512), BF16),
            pltpu.VMEM((BOTH, 1536), BF16),
            pltpu.VMEM((BOTH, D), F32),
            pltpu.VMEM((COUNT, D), F32),
            pltpu.VMEM((1, 1536), F32),
            pltpu.VMEM((1, 2048), F32),
            pltpu.VMEM((1, D), F32),
            pltpu.VMEM((1, D), F32),
            pltpu.VMEM((1, D), F32),
            pltpu.SemaphoreType.DMA((2,)),
            pltpu.SemaphoreType.DMA((2,)),
        ],
        name=f"backward{layer_at}",
        compiler_params=pltpu.CompilerParams(
            collective_id=4 + layer_at, has_side_effects=True, vmem_limit_bytes=60 * 2**20
        ),
    )(x, dy, *kept, *weights, tables)


def pack_small(b_qkv, b_up, ln_gain, ln_bias, out_bias):
    rows = []
    for layer_at in range(LAYERS):
        rows.append(jnp.pad(b_qkv[layer_at], (0, LANE - 48)))
        rows.append(jnp.pad(b_up[layer_at], (0, LANE - 64)))
        rows.append(
            jnp.pad(
                jnp.concatenate([ln_gain[layer_at], ln_bias[layer_at], out_bias[layer_at]]),
                (0, LANE - 48),
            )
        )
    return jnp.pad(jnp.stack(rows).astype(F32), ((0, 2), (0, 0)))


def on_device(
    tokens, w_qkv, b_qkv, w_out, w_up, b_up, w_down, ln_gain, ln_bias, out_bias, out_grad
):
    tables = jnp.asarray(turn_tables())
    found = gather(
        pack_small(b_qkv, b_up, ln_gain, ln_bias, out_bias), halves(w_qkv), w_up, w_out, w_down
    )
    rows = found[0].reshape(512, LANE)
    current = tokens
    inputs = []
    weights_all = []
    kept_all = []
    for layer_at in range(LAYERS):
        wq, wu, wo, wd = found[1 + 4 * layer_at : 5 + 4 * layer_at]
        weights = (
            wq.reshape(D, 1536), wu.reshape(D, 2048), wo.reshape(512, D), wd.reshape(2048, D)
        )
        inputs.append(current)
        current, *kept = forward_call(layer_at, current, rows, *weights, tables)
        weights_all.append(weights)
        kept_all.append(kept)
    outcome = current
    upstream = out_grad
    blocks = [None] * LAYERS
    small = [None] * LAYERS
    for layer_at in reversed(range(LAYERS)):
        upstream, q, u, o, d, small[layer_at] = backward_call(
            layer_at, inputs[layer_at], upstream, kept_all[layer_at], weights_all[layer_at], tables
        )
        blocks[layer_at] = [
            q.reshape(2, 4, 4, 32, 1536),
            u.reshape(2, 4, 4, 32, 2048),
            o.reshape(1, 4, 4, 32, 1024),
            d.reshape(1, 4, 4, 128, 1024),
        ]
    small = jnp.concatenate([s.reshape(64, 8, LANE)[:, :3] for s in small] + [jnp.zeros((64, 2, LANE), F32)], 1)
    g_qkv, g_up, g_out, g_down, g_small = scatter(blocks, small.reshape(2, 4, 4, 16, LANE))
    g_small = g_small[:6].reshape(LAYERS, 3, LANE)
    return (
        outcome,
        upstream,
        g_qkv,
        g_small[:, 0, :48],
        g_out,
        g_up,
        g_small[:, 1, :64],
        g_down,
        g_small[:, 2, :16],
        g_small[:, 2, 16:32],
        g_small[:, 2, 32:48],
    )


def solution(mesh):
    placed = (
        P(("rep", "shard"), None),
        P(None, "shard", None),
        P(None, "shard"),
        P(None, "shard", None),
        P(None, "shard", None),
        P(None, "shard"),
        P(None, "shard", None),
        P(None, "shard"),
        P(None, "shard"),
        P(None, "shard"),
        P(("rep", "shard"), None),
    )
    return jax.shard_map(
        on_device,
        mesh=mesh,
        in_specs=placed,
        out_specs=(
            P(("rep", "shard"), None),
            P(("rep", "shard"), None),
            P(None, "shard", None),
            P(None, "shard"),
            P(None, "shard", None),
            P(None, "shard", None),
            P(None, "shard"),
            P(None, "shard", None),
            P(None, "shard"),
            P(None, "shard"),
            P(None, "shard"),
        ),
        check_vma=False,
    )
```

```python
import functools
import math

import jax
import jax.numpy as jnp
import numpy as np
from jax import lax
from jax.experimental import pallas as pl
from jax.experimental.pallas import tpu as pltpu
from jax.sharding import PartitionSpec as P


MESH = pl.DeviceIdType.MESH
LANE = 128
LAYERS = 2


def place():
    xl = lax.axis_index("rep")
    s = lax.axis_index("shard")
    return xl, s // 32, (s // 8) % 4, (s // 2) % 4, s % 2


def at(xl, xh, z, y, c):
    return (xl, xh * 32 + z * 8 + y * 2 + c)


def around(value, step):
    return lax.rem(value + (step + 4), 4)


def meet(others):
    barrier = pltpu.get_barrier_semaphore()
    for other in others:
        pl.semaphore_signal(barrier, inc=1, device_id=other, device_id_type=MESH)
    pl.semaphore_wait(barrier, len(others))


GATHERED = (
    ("small", True, 32, 128, 0, 1),
    ("qkv", True, 32, 1536, 4, 8),
    ("up", True, 32, 2048, 5, 11),
    ("out", False, 32, 1024, 3, 5),
    ("down", False, 128, 1024, 3, 5),
)
SLOTS = 18


class Stream:
    def __init__(self, number, spec, source, target, send, recv, xl, xh, z, y, core):
        self.name, self.by_columns, self.rows, self.columns, self.swapped, self.width = spec
        self.number = number
        self.source = source
        self.target = target
        self.send, self.recv = send, recv
        self.xl, self.xh, self.z, self.y, self.core = xl, xh, z, y, core
        self.half = self.rows // 2
        self.wide = pl.ds(pl.multiple_of(xl * (self.swapped * LANE), LANE), self.width * LANE)
        self.mine = pl.ds(
            pl.multiple_of(xl * ((self.width - self.swapped) * LANE) + xl * (self.swapped * LANE), LANE),
            max(self.swapped, 1) * LANE,
        )
        self.theirs = pl.ds(
            pl.multiple_of((1 - xl) * (self.width * LANE), LANE), max(self.swapped, 1) * LANE
        )
        self.across = lambda core_of: at(1 - xl, 1 - xh, z, y, core_of)
        self.partner = at(1 - xl, xh, z, y, core) if core == 0 else self.across(core)
        if core == 0:
            self.first, self.second = y, z
        else:
            self.first, self.second = z, y
        self.sent = []

    def neighbour(self, ring, step):
        z, y = self.z, self.y
        if (ring == 0) == (self.core == 0):
            y = around(y, step)
        else:
            z = around(z, step)
        return at(self.xl, self.xh, z, y, self.core)

    def block(self, first, rows, columns):
        if self.core == 0:
            return self.target.at[:, self.second, first, rows, columns]
        return self.target.at[:, first, self.second, rows, columns]

    def line(self, second, rows, columns):
        if self.core == 0:
            return self.target.at[:, second, :, rows, columns]
        return self.target.at[:, :, second, rows, columns]

    def push(self, region, slot, device):
        copy = pltpu.make_async_remote_copy(
            region(),
            region(),
            self.send.at[self.number, slot],
            self.recv.at[self.number, slot],
            device_id=device,
            device_id_type=MESH,
        )
        copy.start()
        self.sent.append((region, slot))

    def arrived(self, region, slot):
        pltpu.make_async_copy(region, region, self.recv.at[self.number, slot]).wait()

    def part(self, core_of):
        return pl.ds(core_of * self.half, self.half)

    def stage0(self):
        xh, z, y, core = self.xh, self.z, self.y, self.core
        whole = slice(None)
        if self.by_columns:
            region = lambda: self.target.at[xh, z, y, self.part(core), :]
            here = region()
            landed = self.recv.at[self.number, xh * 2 + core]
            for source, columns in self.source(core):
                pltpu.make_async_copy(source, here.at[:, columns], landed).start()
            for slot, half, device in (
                (0, 1 - core, at(self.xl, xh, z, y, 1 - core)),
                (1, core, self.across(core)),
                (2, 1 - core, self.across(1 - core)),
            ):
                for source, columns in self.source(half):
                    pltpu.make_async_remote_copy(
                        source,
                        here.at[:, columns],
                        self.send.at[self.number, slot],
                        landed,
                        device_id=device,
                        device_id_type=MESH,
                    ).start()
                self.sent.append((region, slot))
        else:
            here = self.target.at[0, z, y, self.part(core), :]
            mine = self.source(0)

            @pl.when(xh == core)
            def _():
                pltpu.make_async_copy(mine, here, self.recv.at[self.number, core]).start()

            @pl.when(xh != core)
            def _():
                pltpu.make_async_remote_copy(
                    mine,
                    here,
                    self.send.at[self.number, 0],
                    self.recv.at[self.number, core],
                    device_id=at(self.xl, xh, z, y, 1 - core),
                    device_id_type=MESH,
                ).start()

            pltpu.make_async_remote_copy(
                mine,
                here,
                self.send.at[self.number, 1],
                self.recv.at[self.number, core],
                device_id=self.across(xh),
                device_id_type=MESH,
            ).start()
            self.sent.append((lambda: self.source(0), 1))

    def stage1(self):
        whole = slice(None)
        for bank in range(2 if self.by_columns else 1):
            for core_of in range(2):
                self.arrived(
                    self.target.at[bank, self.z, self.y, self.part(core_of), :], bank * 2 + core_of
                )
        own = lambda: self.block(self.first, whole, self.wide)
        self.push(own, 4, self.neighbour(0, 1))
        self.push(own, 5, self.neighbour(0, -1))

    def share(self, region, slot):
        if self.swapped:
            self.push(lambda: region(self.mine), slot, self.partner)

    def stage2(self):
        whole = slice(None)
        for step, slot in ((-1, 4), (1, 5)):
            found = lambda rows, columns, step=step: self.block(
                around(self.first, step), rows, columns
            )
            self.arrived(found(whole, self.wide), slot)
            self.push(
                lambda found=found, slot=slot: found(self.part(slot - 4), self.wide),
                slot + 2,
                self.neighbour(0, -step),
            )
            self.share(lambda columns, found=found: found(whole, columns), slot + 8)

    def stage3(self):
        whole = slice(None)
        far = lambda rows, columns: self.block(around(self.first, 2), rows, columns)
        for half in range(2):
            self.arrived(far(self.part(half), self.wide), 6 + half)
        own = lambda: self.line(self.second, whole, self.wide)
        self.push(own, 8, self.neighbour(1, 1))
        self.push(own, 9, self.neighbour(1, -1))
        self.share(lambda columns: far(whole, columns), 14)

    def stage4(self):
        whole = slice(None)
        for step, slot in ((-1, 8), (1, 9)):
            found = lambda rows, columns, step=step: self.line(
                around(self.second, step), rows, columns
            )
            self.arrived(found(whole, self.wide), slot)
            self.push(
                lambda found=found, slot=slot: found(self.part(slot - 8), self.wide),
                slot + 2,
                self.neighbour(1, -step),
            )
            self.share(lambda columns, found=found: found(whole, columns), slot + 7)

    def stage5(self):
        whole = slice(None)
        far = lambda rows, columns: self.line(around(self.second, 2), rows, columns)
        for half in range(2):
            self.arrived(far(self.part(half), self.wide), 10 + half)
        self.share(lambda columns: far(whole, columns), 17)

    def stage6(self):
        whole = slice(None)
        if self.swapped:
            for step, slot in ((-1, 12), (1, 13), (2, 14)):
                self.arrived(self.block(around(self.first, step), whole, self.theirs), slot)
            for step, slot in ((-1, 15), (1, 16), (2, 17)):
                self.arrived(self.line(around(self.second, step), whole, self.theirs), slot)

    def finish(self):
        for region, slot in self.sent:
            pltpu.make_async_copy(region(), region(), self.send.at[self.number, slot]).wait()
        if not self.by_columns:

            @pl.when(self.xh != self.core)
            def _():
                mine = self.source(0)
                pltpu.make_async_copy(mine, mine, self.send.at[self.number, 0]).wait()


def owned_pieces(name, owned, layer_at):
    if name == "small":
        return lambda half: [(owned, slice(None))]
    if name == "qkv":
        return lambda half: [
            (
                owned.at[layer_at, :, pl.ds(third * 1024 + half * 512, 512)],
                pl.ds(third * 512, 512),
            )
            for third in range(3)
        ]
    if name == "up":
        return lambda half: [(owned.at[layer_at, :, pl.ds(half * 2048, 2048)], slice(None))]
    return lambda half: owned.at[layer_at]


def neighbours():
    xl, xh, z, y, c = place()
    return [
        at(xl, xh, z, y, 1 - c),
        at(1 - xl, 1 - xh, z, y, c),
        at(1 - xl, 1 - xh, z, y, 1 - c),
        at(xl, 1 - xh, z, y, c),
        at(1 - xl, xh, z, y, c),
        at(xl, xh, around(z, 1), y, c),
        at(xl, xh, around(z, -1), y, c),
        at(xl, xh, z, around(y, 1), c),
        at(xl, xh, z, around(y, -1), c),
    ]


COUNT = 256
BOTH = 512
D = 1024
HEAD_DIM = 64
ROT = 16
EPS = 1e-05
FILL = -1e30
F32 = jnp.float32
BF16 = jnp.bfloat16
TILE = 256


def turn_tables():
    places = np.arange(COUNT, dtype=np.float32)
    rates = np.float32(10000.0) ** (-np.arange(0, ROT, 2, dtype=np.float32) / np.float32(ROT))
    angles = places[:, None] * rates[None, :]
    cosine, sine = np.cos(angles), np.sin(angles)
    half = ROT // 2
    keep = np.ones((COUNT, HEAD_DIM), np.float32)
    ahead = np.zeros((COUNT, HEAD_DIM), np.float32)
    behind = np.zeros((COUNT, HEAD_DIM), np.float32)
    keep[:, :half] = cosine
    keep[:, half:ROT] = cosine
    ahead[:, :half] = -sine
    behind[:, half:ROT] = sine
    return np.stack([np.concatenate([t, t], 1) for t in (keep, ahead, behind)])


def turn(values, tables, sign):
    return values * tables[0] + sign * (
        pltpu.roll(values, LANE - ROT // 2, 1) * tables[1]
        + pltpu.roll(values, ROT // 2, 1) * tables[2]
    )


def dot(left, right):
    return jnp.dot(left, right, preferred_element_type=F32)


def dot_nt(left, right):
    return lax.dot_general(left, right, (((1,), (1,)), ((), ())), preferred_element_type=F32)


def dot_tn(left, right):
    return lax.dot_general(left, right, (((0,), (0,)), ((), ())), preferred_element_type=F32)


def columns_of(index, width=TILE):
    return pl.ds(pl.multiple_of(index * width, width), width)


def loop(count, body):
    def step(index, carry):
        body(index)
        return carry

    lax.fori_loop(0, count, step, 0)


KINDS = {
    "b_qkv": (0, 48, 43691, 21),
    "b_up": (1, 64, 1, 6),
    "gain": (2, 16, 1, 4),
    "shift": (3, 16, 1, 4),
    "out_bias": (4, 16, 1, 4),
}
OWNED_ROWS = 16
CHUNK = 512


def chunks_of(kind, core):
    if kind == "b_qkv":
        return [(t * CHUNK, t * 1024 + core * CHUNK) for t in range(3)]
    if kind == "b_up":
        return [(t * CHUNK, core * 2048 + t * CHUNK) for t in range(4)]
    return [(t * CHUNK, t * CHUNK) for t in range(2)]


def owner_masks(kind, start):
    row, size, factor, shift = KINDS[kind]
    place_of = lax.broadcasted_iota(jnp.int32, (LANE, CHUNK), 1) + start
    owner = lax.shift_right_logical(place_of * factor, shift)
    within = place_of - owner * size
    spread = lax.broadcasted_iota(jnp.int32, (LANE, CHUNK), 0) == within
    owned = lax.broadcasted_iota(jnp.int32, (64, CHUNK), 0) == owner[:64]
    return spread, owned


def unpack_vector(rows_ref, layer_at, kind, core, target):
    row = KINDS[kind][0] + 5 * layer_at
    held = rows_ref[pl.ds(row, 64, stride=OWNED_ROWS), :].astype(BF16)
    for place_at, start in chunks_of(kind, core):
        spread, owned = owner_masks(kind, start)
        every = dot(held, jnp.where(spread, 1.0, 0.0).astype(BF16))
        target[:, pl.ds(place_at, CHUNK)] = jnp.sum(
            jnp.where(owned, every, 0.0), 0, keepdims=True
        )


def pack_vector(rows_ref, layer_at, kind, core, vector):
    total = jnp.zeros((64, LANE), F32)
    for place_at, start in chunks_of(kind, core):
        spread, owned = owner_masks(kind, start)
        mine = jnp.where(owned, vector[:, pl.ds(place_at, CHUNK)], 0.0)
        spread = jnp.where(spread, 1.0, 0.0).astype(BF16)
        high = mine.astype(BF16)
        total = total + dot_nt(high, spread)
        total = total + dot_nt((mine - high.astype(F32)).astype(BF16), spread)
    rows_ref[pl.ds(KINDS[kind][0] + 5 * layer_at, 64, stride=OWNED_ROWS), :] = total


def centre(values):
    centred = values - jnp.mean(values, -1, keepdims=True)
    inv_std = lax.rsqrt(jnp.mean(centred * centred, -1, keepdims=True) + EPS)
    return centred * inv_std, inv_std


def norm_piece(x_ref, gain, shift, hidden):
    def body(index):
        rows = columns_of(index, 64)
        normed, unused = centre(x_ref[rows, :])
        hidden[rows, :] = (normed * gain[...] + shift[...]).astype(BF16)

    loop(COUNT // 64, body)


def joined_piece(third, hidden, w_qkv, b_qkv, tables, target):
    def body(index):
        columns = columns_of(index + third * 2)
        found = dot(hidden[...], w_qkv(columns)) + b_qkv[:, columns]
        for sequence in range(2):
            for pair in range(2):
                part = found[sequence * COUNT : (sequence + 1) * COUNT, pair * LANE : (pair + 1) * LANE]
                if third < 2:
                    part = turn(part, tables, 1.0)
                if third == 0:
                    part = part * HEAD_DIM**-0.5
                target[
                    pl.ds(sequence * COUNT, COUNT), columns_of(index * 2 + pair + third * 4, LANE)
                ] = part.astype(BF16)

    loop(2, body)


def first_head():
    return lax.broadcasted_iota(jnp.int32, (COUNT, LANE), 1) < HEAD_DIM


def only_head(values, half):
    keep = first_head() if half == 0 else jnp.logical_not(first_head())
    return jnp.where(keep, values, jnp.zeros_like(values))


def attention_piece(turned, probs, mixed, start=0, stop=8):
    def body(index):
        index = index + start
        sequence, pair = index // 4, index % 4
        rows, columns = columns_of(sequence, COUNT), columns_of(pair, LANE)
        q2, k2, v2 = (turned[rows, columns_of(pair + third * 4, LANE)] for third in range(3))
        causal = lax.broadcasted_iota(jnp.int32, (COUNT, COUNT), 0) >= lax.broadcasted_iota(
            jnp.int32, (COUNT, COUNT), 1
        )
        out = []
        for half in range(2):
            scores = jnp.where(causal, dot_nt(only_head(q2, half), k2), FILL)
            expo = jnp.exp(scores - jnp.max(scores, -1, keepdims=True))
            prob = (expo * (1.0 / jnp.sum(expo, -1, keepdims=True))).astype(BF16)
            probs[index * 2 + half] = prob
            out.append(dot(prob, v2))
        mixed[rows, columns] = jnp.where(first_head(), out[0], out[1]).astype(BF16)

    loop(stop - start, body)


def up_piece(hidden, w_up, b_up, active, slope):
    def body(index):
        columns = columns_of(index)
        upward = dot(hidden[...], w_up(columns)) + b_up[:, columns]
        spread = 0.5 + 0.5 * lax.erf(upward * (0.5**0.5))
        active[:, columns] = (upward * spread).astype(BF16)
        dense = jnp.exp(upward * upward * -0.5) * (1.0 / math.sqrt(2.0 * math.pi))
        slope[:, columns] = (spread + upward * dense).astype(BF16)

    loop(8, body)


def down_piece(active, w_down, mixed, w_out, partial):
    def body(index):
        columns = columns_of(index)
        partial[:, columns] = dot(mixed[...], w_out(columns)) + dot(active[...], w_down(columns))

    loop(4, body)


def residual_piece(x_ref, partial, received, out_bias, target):
    def body(index):
        rows = columns_of(index, 64)
        target[rows, :] = (
            x_ref[rows, :] + (partial[rows, :] + received[rows, :]) + out_bias[...]
        ).astype(target.dtype)

    loop(COUNT // 64, body)


def start_piece(dy, dy_low, out_bias_grad):
    def body(index):
        rows = columns_of(index, 64)
        values = dy[rows, :]
        dy_low[rows, :] = values.astype(BF16)
        out_bias_grad[...] += jnp.sum(values, 0, keepdims=True)

    out_bias_grad[...] = jnp.zeros_like(out_bias_grad)
    loop(COUNT // 64, body)


def flip_piece(source, target):
    rows, columns = source.shape
    for at_row in range(rows // TILE):

        def body(index, at_row=at_row):
            target[columns_of(index), pl.ds(at_row * TILE, TILE)] = source[
                pl.ds(at_row * TILE, TILE), columns_of(index)
            ].T

        loop(columns // TILE, body)


def rows_grad_piece(count, left, right, store):
    def body(index):
        store(index, dot_tn(left[:, columns_of(index)], right[...]).astype(BF16))

    loop(count, body)


def columns_grad_piece(count, left_flipped, right, store):
    def body(index):
        store(index, dot(left_flipped[...], right[:, columns_of(index)]).astype(BF16))

    loop(count, body)


def slope_piece(dy_low, w_down_rows, slope, d_up, b_up_grad):
    def body(index):
        columns = columns_of(index)
        found = (dot_nt(dy_low[...], w_down_rows(index)) * slope[:, columns].astype(F32)).astype(BF16)
        d_up[:, columns] = found
        b_up_grad[:, columns] = jnp.sum(found.astype(F32), 0, keepdims=True)

    loop(8, body)


def d_mixed_piece(dy_low, w_out_rows, d_mixed):
    def body(index):
        d_mixed[:, columns_of(index)] = dot_nt(dy_low[...], w_out_rows(index)).astype(BF16)

    loop(2, body)


def attention_back_piece(turned, probs, d_mixed, tables, d_joined, b_qkv_grad, start=0, stop=8):
    if start == 0:
        b_qkv_grad[...] = jnp.zeros_like(b_qkv_grad)

    def body(index):
        index = index + start
        sequence, pair = index // 4, index % 4
        rows, columns = columns_of(sequence, COUNT), columns_of(pair, LANE)
        q2, k2, v2 = (turned[rows, columns_of(pair + third * 4, LANE)] for third in range(3))
        dm2 = d_mixed[rows, columns]
        found = []
        for half in range(2):
            prob = probs[index * 2 + half]
            full = prob.astype(F32)
            d_probs = dot_nt(only_head(dm2, half), v2)
            d_scores = (
                full * (d_probs - jnp.sum(d_probs * full, -1, keepdims=True))
            ).astype(BF16)
            found.append((dot(d_scores, k2), dot_tn(d_scores, q2), dot_tn(prob, dm2)))
        for third in range(3):
            part = jnp.where(first_head(), found[0][third], found[1][third])
            if third == 0:
                part = part * HEAD_DIM**-0.5
            if third < 2:
                part = turn(part, tables, -1.0)
            part = part.astype(BF16)
            there = columns_of(pair + third * 4, LANE)
            d_joined[rows, there] = part
            b_qkv_grad[:, there] += jnp.sum(part.astype(F32), 0, keepdims=True)

    loop(stop - start, body)


def d_hidden_piece(d_joined, w_qkv_rows, d_up, w_up_rows, d_hidden):
    def body(index):
        d_hidden[:, columns_of(index)] = dot_nt(d_joined[...], w_qkv_rows(index)) + dot_nt(
            d_up[...], w_up_rows(index)
        )

    loop(4, body)


def norm_back_piece(x_ref, gain, dy, d_hidden, received, target, gain_grad, shift_grad):
    gain_grad[...] = jnp.zeros_like(gain_grad)
    shift_grad[...] = jnp.zeros_like(shift_grad)

    def body(index):
        rows = columns_of(index, 64)
        normed, inv_std = centre(x_ref[rows, :].astype(F32))
        total = d_hidden[rows, :] + received[rows, :]
        gain_grad[...] += jnp.sum(total * normed, 0, keepdims=True)
        shift_grad[...] += jnp.sum(total, 0, keepdims=True)
        scaled = total * gain[...]
        target[rows, :] = dy[rows, :].astype(F32) + inv_std * (
            scaled
            - jnp.mean(scaled, -1, keepdims=True)
            - normed * jnp.mean(scaled * normed, -1, keepdims=True)
        )

    loop(COUNT // 64, body)


class Pair:
    def __init__(self, send, recv):
        xl, xh, z, y, c = place()
        self.device = at(xl, xh, z, y, 1 - c)
        self.send, self.recv = send, recv

    def push(self, source, target, slot):
        pltpu.make_async_remote_copy(
            source,
            target,
            self.send.at[slot],
            self.recv.at[slot],
            device_id=self.device,
            device_id_type=MESH,
        ).start()

    def wait(self, source, target, slot):
        pltpu.make_async_copy(source, source, self.send.at[slot]).wait()
        pltpu.make_async_copy(target, target, self.recv.at[slot]).wait()


class Moves:
    def __init__(self, done):
        self.done = done
        self.count = 0
        self.open = []

    def start(self, source, target):
        copy = pltpu.make_async_copy(source, target, self.done.at[self.count])
        self.count += 1
        copy.start()
        self.open.append(copy)
        return copy

    def finish(self, copy):
        copy.wait()
        self.open = [other for other in self.open if other is not copy]


KEPT = (
    ("flipped", (D, BOTH), BF16),
    ("turned", (BOTH, 1536), BF16),
    ("probs", (16, COUNT, COUNT), BF16),
    ("mixed", (BOTH, 512), BF16),
    ("active", (BOTH, 2048), BF16),
    ("slope", (BOTH, 2048), BF16),
    ("gain", (1, D), F32),
)
WEIGHTS = GATHERED[1:]


def weight_shape(spec):
    name, by_columns, rows, columns, swapped, width = spec
    return (2 if by_columns else 1, 4, 4, rows, columns)


def all_rows(weight, columns):
    found = weight[:, :, :, :, columns]
    return found.reshape(-1, found.shape[-1])


def forward_kernel(tokens, b_qkv, b_up, ln_gain, ln_bias, out_bias, tables, qkv, up, out, down, *rest):
    rest = list(rest)

    def take(count):
        found = rest[:count]
        del rest[:count]
        return found

    (result, x_kept) = take(2)
    gathered = [take(4) for layer_at in range(LAYERS)]
    kept_out = [dict(zip((k[0] for k in KEPT), take(len(KEPT)))) for layer_at in range(LAYERS)]
    kept = [dict(zip((k[0] for k in KEPT), take(len(KEPT)))) for layer_at in range(LAYERS)]
    weights = [take(4) for layer_at in range(LAYERS)]
    vectors = [dict(zip(("b_qkv", "b_up", "shift", "out_bias"), take(4))) for layer_at in range(LAYERS)]
    owned, every, rows, x0, x1, last = take(6)
    hidden = take(2)
    partial, = take(1)
    received = take(2)
    send, recv, pair_send, pair_recv, moved = take(5)

    owned[...] = jnp.zeros_like(owned)
    for layer_at in range(LAYERS):
        for row, vector in enumerate((b_qkv, b_up, ln_gain, ln_bias, out_bias)):
            owned[5 * layer_at + row : 5 * layer_at + row + 1, : vector.shape[1]] = vector[
                layer_at : layer_at + 1, :
            ].astype(F32)
    xl, xh, z, y, c = place()
    meet(neighbours())
    pair = Pair(pair_send, pair_recv)
    moves = Moves(moved)

    streams = []
    for core in range(2):
        found = [
            Stream(0, GATHERED[0], owned_pieces("small", owned, 0), every, send, recv, xl, xh, z, y, core)
        ]
        for layer_at in range(LAYERS):
            for spec, source, target in zip(WEIGHTS, (qkv, up, out, down), gathered[layer_at]):
                found.append(
                    Stream(
                        len(found), spec, owned_pieces(spec[0], source, layer_at), target,
                        send, recv, xl, xh, z, y, core,
                    )
                )
        streams.append(found)
    count = len(streams[0])

    def tick(time):
        for core in range(2):

            @pl.when(c == core)
            def _():
                for stage in range(7):
                    if 0 <= time - stage < count:
                        getattr(streams[core][time - stage], f"stage{stage}")()

    loads = {}

    def load(layer_at, which):
        loads[layer_at, which] = moves.start(gathered[layer_at][which], weights[layer_at][which])

    def loaded(layer_at, which):
        moves.finish(loads[layer_at, which])

    def keep(layer_at, name):
        moves.start(kept[layer_at][name], kept_out[layer_at][name])

    own, other = pl.ds(0, COUNT), pl.ds(COUNT, COUNT)
    inputs = (x0, x1)

    def vectors_step():
        rows[...] = every[...].reshape(rows.shape)
        for core in range(2):

            @pl.when(c == core)
            def _():
                for layer_at in range(LAYERS):
                    for kind in KINDS:
                        target = kept[layer_at]["gain"] if kind == "gain" else vectors[layer_at][kind]
                        unpack_vector(rows, layer_at, kind, core, target)

        for layer_at in range(LAYERS):
            keep(layer_at, "gain")

    def norm_step(layer_at):
        norm_piece(inputs[layer_at], kept[layer_at]["gain"], vectors[layer_at]["shift"], hidden[layer_at])
        pair.push(hidden[layer_at].at[own], hidden[layer_at].at[other], 2 * layer_at)

    def joined_step(layer_at):
        pair.wait(hidden[layer_at].at[own], hidden[layer_at].at[other], 2 * layer_at)
        loaded(layer_at, 0)
        for third in range(3):
            joined_piece(
                third,
                hidden[layer_at],
                lambda n: all_rows(weights[layer_at][0], n),
                vectors[layer_at]["b_qkv"],
                tables,
                kept[layer_at]["turned"],
            )
        keep(layer_at, "turned")
        flip_piece(hidden[layer_at], kept[layer_at]["flipped"])
        keep(layer_at, "flipped")

    def attention_step(layer_at, start, stop):
        attention_piece(
            kept[layer_at]["turned"], kept[layer_at]["probs"], kept[layer_at]["mixed"], start, stop
        )
        if stop == 8:
            keep(layer_at, "probs")
            keep(layer_at, "mixed")

    def up_step(layer_at):
        loaded(layer_at, 1)
        up_piece(
            hidden[layer_at],
            lambda n: all_rows(weights[layer_at][1], n),
            vectors[layer_at]["b_up"],
            kept[layer_at]["active"],
            kept[layer_at]["slope"],
        )
        keep(layer_at, "active")
        keep(layer_at, "slope")

    def down_step(layer_at):
        loaded(layer_at, 2)
        loaded(layer_at, 3)
        if layer_at:
            pltpu.make_async_copy(partial.at[other], partial.at[other], pair_send.at[1]).wait()
        down_piece(
            kept[layer_at]["active"],
            lambda n: all_rows(weights[layer_at][3], n),
            kept[layer_at]["mixed"],
            lambda n: all_rows(weights[layer_at][2], n),
            partial,
        )
        pair.push(partial.at[other], received[layer_at], 2 * layer_at + 1)

    def residual_step(layer_at):
        target = received[layer_at]
        pltpu.make_async_copy(target, target, pair_recv.at[2 * layer_at + 1]).wait()
        residual_piece(
            inputs[layer_at],
            partial,
            target,
            vectors[layer_at]["out_bias"],
            x1 if layer_at == 0 else last,
        )
        if layer_at == 0:
            moves.start(x1, x_kept)
        else:
            pltpu.make_async_copy(partial.at[other], partial.at[other], pair_send.at[3]).wait()
            moves.start(last, result)

    x0[...] = tokens[...].astype(F32)
    for time in range(7):
        tick(time)
    vectors_step()
    norm_step(0)
    tick(7)
    load(0, 0)
    tick(8)
    load(0, 1)
    joined_step(0)
    tick(9)
    load(0, 2)
    attention_step(0, 0, 8)
    tick(10)
    load(0, 3)
    up_step(0)
    tick(11)
    load(1, 0)
    down_step(0)
    tick(12)
    load(1, 1)
    residual_step(0)
    norm_step(1)
    joined_step(1)
    tick(13)
    load(1, 2)
    attention_step(1, 0, 8)
    tick(14)
    load(1, 3)
    up_step(1)
    down_step(1)
    for core in range(2):

        @pl.when(c == core)
        def _():
            for stream in streams[core]:
                stream.finish()

    residual_step(1)
    for copy in list(moves.open):
        copy.wait()


def forward_call(tokens, b_qkv, b_up, ln_gain, ln_bias, out_bias, tables, qkv, up, out, down):
    vmem, hbm = pl.BlockSpec(memory_space=pltpu.VMEM), pl.BlockSpec(memory_space=pltpu.HBM)
    shape = jax.ShapeDtypeStruct
    outs = [shape((COUNT, D), BF16), shape((COUNT, D), F32)]
    scratch = []
    for layer_at in range(LAYERS):
        outs += [shape(weight_shape(spec), BF16) for spec in WEIGHTS]
    for layer_at in range(LAYERS):
        outs += [shape(dims, kind) for name, dims, kind in KEPT]
        scratch += [pltpu.VMEM(dims, kind) for name, dims, kind in KEPT]
    for layer_at in range(LAYERS):
        scratch += [pltpu.VMEM(weight_shape(spec), BF16) for spec in WEIGHTS]
    for layer_at in range(LAYERS):
        scratch += [pltpu.VMEM((1, n), F32) for n in (1536, 2048, D, D)]
    scratch += [
        pltpu.VMEM((OWNED_ROWS, LANE), F32),
        pltpu.VMEM((2, 4, 4, 2 * OWNED_ROWS, LANE), F32),
        pltpu.VMEM((64 * OWNED_ROWS, LANE), F32),
        pltpu.VMEM((COUNT, D), F32),
        pltpu.VMEM((COUNT, D), F32),
        pltpu.VMEM((COUNT, D), BF16),
        pltpu.VMEM((BOTH, D), BF16),
        pltpu.VMEM((BOTH, D), BF16),
        pltpu.VMEM((BOTH, D), F32),
        pltpu.VMEM((COUNT, D), F32),
        pltpu.VMEM((COUNT, D), F32),
        pltpu.SemaphoreType.DMA((1 + 4 * LAYERS, SLOTS)),
        pltpu.SemaphoreType.DMA((1 + 4 * LAYERS, SLOTS)),
        pltpu.SemaphoreType.DMA((4,)),
        pltpu.SemaphoreType.DMA((4,)),
        pltpu.SemaphoreType.DMA((40,)),
    ]
    return pl.pallas_call(
        forward_kernel,
        out_shape=outs,
        in_specs=[vmem] * 7 + [hbm] * 4,
        out_specs=[hbm] * len(outs),
        scratch_shapes=scratch,
        name="forward",
        compiler_params=pltpu.CompilerParams(
            collective_id=0, has_side_effects=True, vmem_limit_bytes=60 * 2**20
        ),
    )(tokens, b_qkv, b_up, ln_gain, ln_bias, out_bias, tables, qkv, up, out, down)


SUMMED = (
    ("qkv", True, 32, 1536, 3, 9),
    ("up", True, 32, 2048, 4, 12),
    ("out", False, 32, 1024, 2, 6),
    ("down", False, 128, 1024, 2, 6),
    ("small", True, 32, 128, 0, 1),
)
SUM_SLOTS = 18
BUFFERS = 9


def total_shape(spec):
    name, by_columns, rows, columns, swapped, width = spec
    return (2 if by_columns else 1, 4, 4, rows, columns)


def landing_shapes(spec):
    name, by_columns, rows, columns, swapped, width = spec
    banks = 2 if by_columns else 1
    kind = F32 if name == "small" else BF16
    wide = width * LANE
    return [
        pltpu.VMEM((banks, 4, 4, rows, swapped * LANE) if swapped else (8, LANE), kind),
        pltpu.VMEM((2, banks, 4, rows // 2, wide), kind),
        pltpu.VMEM((2, banks, 4, rows, wide), kind),
        pltpu.VMEM((banks, 4, rows, wide), kind),
        pltpu.VMEM((2, banks, rows // 2, wide), kind),
        pltpu.VMEM((2, banks, rows, wide), kind),
        pltpu.VMEM((3, rows, wide), kind),
        pltpu.VMEM((rows, columns), F32),
        pltpu.VMEM((2, 16, LANE), F32),
    ]


def add_into(target, first, *others):
    if len(others) == 1:
        target[...] = first[...] + others[0][...]
    else:
        found = first[...].astype(F32)
        for other in others:
            found = found + other[...].astype(F32)
        target[...] = found.astype(target.dtype)


class Sum:
    def __init__(self, number, which, before, total, landing, output, send, recv, free, where, core):
        spec = SUMMED[which]
        self.name, self.by_columns, self.rows, self.columns, self.swapped, self.width = spec
        self.number, self.which = number, which
        self.before = before
        self.after = not before and self.name != "small"
        self.total, self.output = total, output
        (
            self.swap,
            self.far_line,
            self.near_line,
            self.line,
            self.far_block,
            self.near_block,
            self.last,
            self.ready,
            self.tail,
        ) = landing
        self.send, self.recv, self.free = send, recv, free
        self.xl, self.xh, self.z, self.y = where
        self.core = core
        self.banks = 2 if self.by_columns else 1
        self.half = self.rows // 2
        s, w = self.swapped, self.width
        xl, xh, z, y = where
        self.wide = pl.ds(pl.multiple_of(xl * (s * LANE), LANE), w * LANE)
        self.mine = pl.ds(pl.multiple_of(xl * (w * LANE), LANE), max(s, 1) * LANE)
        self.theirs = pl.ds(pl.multiple_of((1 - xl) * (w * LANE), LANE), max(s, 1) * LANE)
        self.beside = at(1 - xl, xh, z, y, core)
        self.across = at(1 - xl, 1 - xh, z, y, core)
        self.beyond = at(xl, 1 - xh, z, y, core)
        self.sibling = at(xl, xh, z, y, 1 - core)
        self.partner = self.beside if core == 0 else self.across
        self.first, self.second = (y, z) if core == 0 else (z, y)
        self.sent = []

    def neighbour(self, ring, step):
        z, y = self.z, self.y
        if (ring == 0) == (self.core == 0):
            y = around(y, step)
        else:
            z = around(z, step)
        return at(self.xl, self.xh, z, y, self.core)

    def total_line(self, second, rows, columns):
        if self.core == 0:
            return self.total.at[:, second, :, rows, columns]
        return self.total.at[:, :, second, rows, columns]

    def push(self, source, target, slot, device, keep=True):
        if self.before and slot < 12:
            pl.semaphore_wait(self.free.at[self.which, slot], 1)
        pltpu.make_async_remote_copy(
            source(),
            target,
            self.send.at[self.number, slot],
            self.recv.at[self.number, slot],
            device_id=device,
            device_id_type=MESH,
        ).start()
        if keep:
            self.sent.append((source, slot))

    def release(self, slot, device):
        if self.after:
            pl.semaphore_signal(
                self.free.at[self.which, slot], inc=1, device_id=device, device_id_type=MESH
            )

    def arrived(self, region, slot):
        pltpu.make_async_copy(region, region, self.recv.at[self.number, slot]).wait()

    def settle(self):
        for source, slot in self.sent:
            pltpu.make_async_copy(source(), source(), self.send.at[self.number, slot]).wait()
        self.sent = []

    def part(self, core_of):
        return pl.ds(core_of * self.half, self.half)

    def stage1(self):
        if self.swapped:
            self.push(
                lambda: self.total.at[:, :, :, :, self.theirs], self.swap, 0, self.partner
            )

    def stage2(self):
        if self.swapped:
            self.arrived(self.swap, 0)

            def add(step):
                bank, z, y = step // 16, (step // 4) % 4, step % 4
                region = self.total.at[bank, z, y, :, self.mine]
                add_into(region, region, self.swap.at[bank, z, y])

            loop(self.banks * 16, add)
            self.release(0, self.partner)
        for half in range(2):
            self.push(
                lambda half=half: self.total_line(
                    around(self.second, 2), self.part(half), self.wide
                ),
                self.far_line.at[half],
                1 + half,
                self.neighbour(1, 1 - 2 * half),
            )

    def stage3(self):
        for half in range(2):
            self.arrived(self.far_line.at[half], 1 + half)
            toward = 1 - 2 * half
            rows = self.part(half)

            def add(step):
                bank, place_at = step // 4, step % 4
                region = self.total_line(around(self.second, toward), rows, self.wide).at[
                    bank, place_at
                ]
                add_into(region, region, self.far_line.at[half, bank, place_at])

            loop(self.banks * 4, add)
            self.release(1 + half, self.neighbour(1, -toward))
            self.push(
                lambda toward=toward: self.total_line(
                    around(self.second, toward), slice(None), self.wide
                ),
                self.near_line.at[half],
                3 + half,
                self.neighbour(1, toward),
            )

    def stage4(self):
        for half in range(2):
            self.arrived(self.near_line.at[half], 3 + half)

        def add(step):
            bank, place_at = step // 4, step % 4
            add_into(
                self.line.at[bank, place_at],
                self.total_line(self.second, slice(None), self.wide).at[bank, place_at],
                self.near_line.at[0, bank, place_at],
                self.near_line.at[1, bank, place_at],
            )

        loop(self.banks * 4, add)
        for half in range(2):
            self.release(3 + half, self.neighbour(1, 2 * half - 1))
        self.settle()
        for half in range(2):
            self.push(
                lambda half=half: self.line.at[:, around(self.first, 2), self.part(half), :],
                self.far_block.at[half],
                5 + half,
                self.neighbour(0, 1 - 2 * half),
            )

    def stage5(self):
        for half in range(2):
            self.arrived(self.far_block.at[half], 5 + half)
            toward = 1 - 2 * half
            for bank in range(self.banks):
                region = self.line.at[bank, around(self.first, toward), self.part(half), :]
                add_into(region, region, self.far_block.at[half, bank])
            self.release(5 + half, self.neighbour(0, -toward))
            self.push(
                lambda toward=toward: self.line.at[:, around(self.first, toward)],
                self.near_block.at[half],
                7 + half,
                self.neighbour(0, toward),
            )

    def own(self, bank):
        return self.line.at[bank, self.first]

    def stage6(self):
        for half in range(2):
            self.arrived(self.near_block.at[half], 7 + half)
        for bank in range(self.banks):
            add_into(
                self.own(bank),
                self.own(bank),
                self.near_block.at[0, bank],
                self.near_block.at[1, bank],
            )
        for half in range(2):
            self.release(7 + half, self.neighbour(0, 2 * half - 1))
        if self.by_columns:
            self.push(lambda: self.own(self.xh), self.last.at[0], 9, self.beside)
            self.push(lambda: self.own(1 - self.xh), self.last.at[1], 10, self.across)
            self.push(lambda: self.own(1 - self.xh), self.last.at[2], 11, self.beyond)
        else:

            @pl.when(self.xh == self.core)
            def _():
                self.push(lambda: self.own(0), self.last.at[0], 9, self.beside, False)

            @pl.when(self.xh != self.core)
            def _():
                self.push(lambda: self.own(0), self.last.at[1], 10, self.across, False)
                self.push(lambda: self.own(0), self.last.at[2], 11, self.beyond, False)

    def add_last(self):
        for slot in range(3):
            self.arrived(self.last.at[slot], 9 + slot)
        s, w = self.swapped, self.width
        c = w - s
        own = self.own(self.xh if self.by_columns else 0)
        self.ready[:, self.wide] = own[...].astype(F32) + self.last[2].astype(F32)
        if s:
            there = pl.ds(pl.multiple_of((1 - self.xl) * (c * LANE), LANE), s * LANE)
            self.ready[:, self.theirs] = self.last[0, :, there].astype(F32) + self.last[
                1, :, there
            ].astype(F32)
        if c:
            middle = pl.ds(s * LANE, c * LANE)
            there = pl.ds(pl.multiple_of(self.xl * (s * LANE), LANE), c * LANE)
            self.ready[:, middle] = (
                self.ready[:, middle]
                + self.last[0, :, there].astype(F32)
                + self.last[1, :, there].astype(F32)
            )
        for slot, device in ((9, self.beside), (10, self.across), (11, self.beyond)):
            self.release(slot, device)

    def pieces(self, core_of):
        rows = self.part(core_of)
        if self.name == "qkv":
            return [
                (
                    self.ready.at[rows, pl.ds(third * 512, 512)],
                    self.output.at[:, pl.ds(third * 1024 + self.core * 512, 512)],
                )
                for third in range(3)
            ]
        if self.name == "up":
            return [(self.ready.at[rows, :], self.output.at[:, pl.ds(self.core * 2048, 2048)])]
        return [(self.ready.at[rows, :], self.output)]

    def deliver(self):
        for index, (source, target) in enumerate(self.pieces(self.core)):
            pltpu.make_async_copy(source, target, self.recv.at[self.number, 15 + index]).start()
        for index, (source, target) in enumerate(self.pieces(1 - self.core)):
            self.push(lambda: source, target, 12 + index, self.sibling, False)

    def delivered(self):
        for index, (source, target) in enumerate(self.pieces(self.core)):
            pltpu.make_async_copy(source, target, self.recv.at[self.number, 15 + index]).wait()
        for index, (source, target) in enumerate(self.pieces(1 - self.core)):
            pltpu.make_async_copy(source, source, self.send.at[self.number, 12 + index]).wait()

    def stage7(self):
        if self.name == "small":
            self.add_last()
            self.push(
                lambda: self.ready.at[self.part(1 - self.core), :], self.tail.at[0], 12, self.sibling
            )
        elif self.by_columns:
            self.add_last()
            self.deliver()
        else:

            @pl.when(self.xh == self.core)
            def _():
                self.add_last()
                self.deliver()

    def stage8(self):
        core = self.core
        if self.name == "small":
            self.arrived(self.tail.at[0], 12)
            self.tail[1] = self.ready[self.part(core), :] + self.tail[0]
        elif self.by_columns:
            self.delivered()
            for index, (source, target) in enumerate(self.pieces(1 - core)):
                self.arrived(source, 12 + index)
        else:

            @pl.when(self.xh == core)
            def _():
                self.delivered()

            @pl.when(self.xh != core)
            def _():
                self.arrived(self.output, 12)

        self.settle()
        if not self.by_columns:

            @pl.when(self.xh == core)
            def _():
                own = self.own(0)
                pltpu.make_async_copy(own, own, self.send.at[self.number, 9]).wait()

            @pl.when(self.xh != core)
            def _():
                own = self.own(0)
                pltpu.make_async_copy(own, own, self.send.at[self.number, 10]).wait()
                pltpu.make_async_copy(own, own, self.send.at[self.number, 11]).wait()


QKV, UP, OUT, DOWN, SMALL = range(5)

SCHEDULE = """
start1 low1 gdown1 D1 slope1 gup1 U1 dmixed1 gout1 O1 attentionA1 D1 attentionB1 D1 dhidden1 U1 gqkv1 Q1 D1
late1 norm1 free1 start0 U1 O1 low0 D1 gdown0 D1 D0 U1 O1 slope0 Q1 gup0 U0 D1 O1 U1 dmixed0 gout0 O0
Q1 U1 O1 D1 attentionA0 Q1 D0 U1 O1 attentionB0 U1 O1 Q1 D0 U0 gqkv0 Q0 Q1 O1 O0 dhidden0 Q1 D0 U0
norm0 pack1 pack0 S0
""".split()


def whole_schedule():
    steps = list(SCHEDULE)
    stages = {}
    for step in steps:
        if step[0].isupper():
            stages[step] = stages.get(step, 0) + 1
    while any(stage < 8 for stage in stages.values()):
        for step in sorted(stages, key=lambda step: -stages[step]):
            if stages[step] < 8:
                stages[step] += 1
                steps.append(step)
    return steps


def row_tile(weight, index):
    banks, unused, same, rows, columns = weight.shape
    if rows == 128:
        found = weight[0, index // 2, pl.ds((index % 2) * 2, 2)]
    elif banks == 2:
        found = weight[index // 2, pl.ds((index % 2) * 2, 2)]
    else:
        found = weight[0, pl.ds(index * 2, 2)]
    return found.reshape(TILE, columns)


def store_row_tile(total):
    def store(index, found):
        banks, unused, same, rows, columns = total.shape
        if rows == 128:
            total[0, index // 2, pl.ds((index % 2) * 2, 2)] = found.reshape(2, 128, columns)
        else:
            total[0, pl.ds(index * 2, 2)] = found.reshape(2, 4, 32, columns)

    return store


def store_column_tile(total):
    def store(index, found):
        total[:, :, :, :, columns_of(index)] = found.reshape(2, 4, 4, 32, TILE)

    return store


def backward_kernel(schedule, tokens, x_kept, out_grad, tables, *rest):
    rest = list(rest)

    def take(count):
        found = rest[:count]
        del rest[:count]
        return found

    kept_in = [dict(zip((k[0] for k in KEPT), take(len(KEPT)))) for layer_at in range(LAYERS)]
    weights_in = [take(4) for layer_at in range(LAYERS)]
    in_grad, *large_out = take(5)
    small_out = take(5)
    kept = dict(zip((k[0] for k in KEPT), take(len(KEPT))))
    weights = take(4)
    gains = [kept["gain"], *take(1)]
    x_late, dy = take(2)
    dy_low = take(2)
    d_mixed, d_hidden = take(2)
    received = take(2)
    grads = [dict(zip(KINDS, take(5))) for layer_at in range(LAYERS)]
    small_rows, = take(1)
    totals = take(5)
    landing = [take(BUFFERS) for spec in SUMMED]
    send, recv, free, pair_send, pair_recv, moved = take(6)

    xl, xh, z, y, c = place()
    meet(neighbours())
    pair = Pair(pair_send, pair_recv)
    moves = Moves(moved)
    own, other = pl.ds(0, COUNT), pl.ds(COUNT, COUNT)

    sums = {}
    for core in range(2):
        number = 0
        for layer_at in (1, 0):
            for which in (QKV, UP, OUT, DOWN):
                sums[core, layer_at, which] = Sum(
                    number, which, layer_at == 0, totals[which], landing[which],
                    large_out[which].at[layer_at], send, recv, free, (xl, xh, z, y), core,
                )
                number += 1
        sums[core, 0, SMALL] = Sum(
            number, SMALL, False, totals[SMALL], landing[SMALL], None, send, recv, free,
            (xl, xh, z, y), core,
        )
    stage_of = {}

    def advance(layer_at, which):
        stage = stage_of[layer_at, which] = stage_of.get((layer_at, which), 0) + 1
        for core in range(2):

            @pl.when(c == core)
            def _():
                getattr(sums[core, layer_at, which], f"stage{stage}")()

    loads = {}

    def load(layer_at, name):
        if name in ("qkv", "up", "out", "down"):
            which = ("qkv", "up", "out", "down").index(name)
            loads[layer_at, name] = moves.start(weights_in[layer_at][which], weights[which])
        else:
            target = gains[layer_at] if name == "gain" else kept[name]
            loads[layer_at, name] = moves.start(kept_in[layer_at][name], target)

    def need(layer_at, *names):
        for name in names:
            if (layer_at, name) in loads:
                moves.finish(loads.pop((layer_at, name)))

    def used(layer_at, *names):
        if layer_at:
            for name in names:
                load(layer_at - 1, name)

    def start(layer_at):
        start_piece(dy, dy_low[layer_at], grads[layer_at]["out_bias"])
        pair.push(dy_low[layer_at].at[own], dy_low[layer_at].at[other], 2 * layer_at)

    def low_arrived(layer_at):
        pair.wait(dy_low[layer_at].at[own], dy_low[layer_at].at[other], 2 * layer_at)

    def gdown(layer_at):
        need(layer_at, "active")
        rows_grad_piece(8, kept["active"], dy_low[layer_at], store_row_tile(totals[DOWN]))
        used(layer_at, "active")

    def slope(layer_at):
        need(layer_at, "down", "slope")
        slope_piece(
            dy_low[layer_at], lambda n: row_tile(weights[DOWN], n), kept["slope"], kept["slope"],
            grads[layer_at]["b_up"],
        )
        used(layer_at, "down")

    def gup(layer_at):
        need(layer_at, "flipped")
        columns_grad_piece(8, kept["flipped"], kept["slope"], store_column_tile(totals[UP]))

    def dmixed(layer_at):
        need(layer_at, "out")
        d_mixed_piece(dy_low[layer_at], lambda n: row_tile(weights[OUT], n), d_mixed)
        used(layer_at, "out")

    def gout(layer_at):
        need(layer_at, "mixed")
        rows_grad_piece(2, kept["mixed"], dy_low[layer_at], store_row_tile(totals[OUT]))
        used(layer_at, "mixed")

    def attention(layer_at, first, stop):
        need(layer_at, "turned", "probs")
        attention_back_piece(
            kept["turned"], kept["probs"], d_mixed, tables, kept["turned"], grads[layer_at]["b_qkv"], first, stop
        )
        if stop == 8:
            used(layer_at, "probs")

    def dhidden(layer_at):
        need(layer_at, "qkv", "up")
        if layer_at == 0:
            pltpu.make_async_copy(
                d_hidden.at[other], d_hidden.at[other], pair_send.at[3]
            ).wait()
        d_hidden_piece(
            kept["turned"], lambda n: row_tile(weights[QKV], n), kept["slope"],
            lambda n: row_tile(weights[UP], n), d_hidden,
        )
        pair.push(d_hidden.at[other], received[layer_at], 2 * layer_at + 1)
        used(layer_at, "qkv", "up")

    def gqkv(layer_at):
        columns_grad_piece(6, kept["flipped"], kept["turned"], store_column_tile(totals[QKV]))

    def norm(layer_at):
        need(layer_at, "gain")
        target = received[layer_at]
        pltpu.make_async_copy(target, target, pair_recv.at[2 * layer_at + 1]).wait()
        norm_back_piece(
            x_late if layer_at else tokens, gains[layer_at], dy, d_hidden, target, dy,
            grads[layer_at]["gain"], grads[layer_at]["shift"],
        )
        if layer_at == 0:
            moves.start(dy, in_grad)

    def pack(layer_at):
        for core in range(2):

            @pl.when(c == core)
            def _():
                for kind in KINDS:
                    pack_vector(small_rows, layer_at, kind, core, grads[layer_at][kind])

        if layer_at == 0:
            totals[SMALL][...] = small_rows[...].reshape(totals[SMALL].shape)

    for name in ("active", "down", "slope", "flipped", "out", "mixed", "turned", "probs", "qkv", "up", "gain"):
        load(1, name)
    load(0, "gain")
    late = moves.start(x_kept, x_late)
    small_rows[...] = jnp.zeros_like(small_rows)
    dy[...] = out_grad[...].astype(F32)
    steps = {
        "start": start, "low": low_arrived, "gdown": gdown, "slope": slope, "gup": gup,
        "dmixed": dmixed, "gout": gout, "dhidden": dhidden, "gqkv": gqkv, "norm": norm, "pack": pack,
        "attention": lambda layer_at: attention(layer_at, 0, 8),
        "attentionA": lambda layer_at: attention(layer_at, 0, 4),
        "attentionB": lambda layer_at: attention(layer_at, 4, 8),
    }
    streams = {"Q": QKV, "U": UP, "O": OUT, "D": DOWN, "S": SMALL}
    for step in schedule:
        name, layer_at = step[:-1], int(step[-1])
        if name == "free":
            used(layer_at, "slope", "flipped", "turned")
        elif name == "late":
            moves.finish(late)
        elif name in streams:
            advance(layer_at, streams[name])
        else:
            steps[name](layer_at)
    pltpu.make_async_copy(d_hidden.at[other], d_hidden.at[other], pair_send.at[1]).wait()
    tail = landing[SMALL][8]
    for layer_at in range(LAYERS):
        for (kind, (row, size, factor, shift)), target in zip(KINDS.items(), small_out):
            at_row = 5 * layer_at + row
            target[layer_at : layer_at + 1, :] = tail[1, at_row : at_row + 1, :size]
    for copy in list(moves.open):
        copy.wait()


def backward_call(tokens, x_kept, out_grad, tables, kept, weights):
    vmem, hbm = pl.BlockSpec(memory_space=pltpu.VMEM), pl.BlockSpec(memory_space=pltpu.HBM)
    shape = jax.ShapeDtypeStruct
    flat = []
    for layer_at in range(LAYERS):
        flat += list(kept[layer_at])
    for layer_at in range(LAYERS):
        flat += list(weights[layer_at])
    scratch = [pltpu.VMEM(dims, kind) for name, dims, kind in KEPT]
    scratch += [pltpu.VMEM(weight_shape(spec), BF16) for spec in WEIGHTS]
    scratch += [
        pltpu.VMEM((1, D), F32),
        pltpu.VMEM((COUNT, D), F32),
        pltpu.VMEM((COUNT, D), F32),
        pltpu.VMEM((BOTH, D), BF16),
        pltpu.VMEM((BOTH, D), BF16),
        pltpu.VMEM((BOTH, 512), BF16),
        pltpu.VMEM((BOTH, D), F32),
        pltpu.VMEM((COUNT, D), F32),
        pltpu.VMEM((COUNT, D), F32),
    ]
    scratch += [pltpu.VMEM((1, n), F32) for n in (1536, 2048, D, D, D) * LAYERS]
    scratch += [pltpu.VMEM((64 * OWNED_ROWS, LANE), F32)]
    for spec in SUMMED:
        scratch.append(pltpu.VMEM(total_shape(spec), F32 if spec[0] == "small" else BF16))
    for spec in SUMMED:
        scratch += landing_shapes(spec)
    scratch += [
        pltpu.SemaphoreType.DMA((1 + 4 * LAYERS, SUM_SLOTS)),
        pltpu.SemaphoreType.DMA((1 + 4 * LAYERS, SUM_SLOTS)),
        pltpu.SemaphoreType.REGULAR((4, 12)),
        pltpu.SemaphoreType.DMA((4,)),
        pltpu.SemaphoreType.DMA((4,)),
        pltpu.SemaphoreType.DMA((40,)),
    ]
    return pl.pallas_call(
        functools.partial(backward_kernel, whole_schedule()),
        out_shape=[
            shape((COUNT, D), F32),
            shape((LAYERS, 16, 3072), F32),
            shape((LAYERS, 16, 4096), F32),
            shape((LAYERS, 16, 1024), F32),
            shape((LAYERS, 64, 1024), F32),
        ]
        + [shape((LAYERS, size), F32) for row, size, factor, shift in KINDS.values()],
        in_specs=[vmem, hbm, vmem, vmem] + [hbm] * len(flat),
        out_specs=[hbm] * 5 + [vmem] * 5,
        scratch_shapes=scratch,
        name="backward",
        compiler_params=pltpu.CompilerParams(
            collective_id=1, has_side_effects=True, vmem_limit_bytes=63 * 2**20
        ),
    )(tokens, x_kept, out_grad, tables, *flat)


def on_device(
    tokens, w_qkv, b_qkv, w_out, w_up, b_up, w_down, ln_gain, ln_bias, out_bias, out_grad
):
    tables = jnp.asarray(turn_tables())
    found = forward_call(
        tokens, b_qkv, b_up, ln_gain, ln_bias, out_bias, tables, w_qkv, w_up, w_out, w_down
    )
    current, x_kept = found[:2]
    weights = [found[2 + 4 * layer_at : 6 + 4 * layer_at] for layer_at in range(LAYERS)]
    first = 2 + 4 * LAYERS
    kept = [
        found[first + len(KEPT) * layer_at : first + len(KEPT) * (layer_at + 1)]
        for layer_at in range(LAYERS)
    ]
    upstream, g_qkv, g_up, g_out, g_down, *small = backward_call(
        tokens, x_kept, out_grad, tables, kept, weights
    )
    g_b_qkv, g_b_up, g_gain, g_shift, g_out_bias = small
    return (
        current,
        upstream,
        g_qkv,
        g_b_qkv,
        g_out,
        g_up,
        g_b_up,
        g_down,
        g_gain,
        g_shift,
        g_out_bias,
    )


def solution(mesh):
    placed = (
        P(("rep", "shard"), None),
        P(None, "shard", None),
        P(None, "shard"),
        P(None, "shard", None),
        P(None, "shard", None),
        P(None, "shard"),
        P(None, "shard", None),
        P(None, "shard"),
        P(None, "shard"),
        P(None, "shard"),
        P(("rep", "shard"), None),
    )
    return jax.shard_map(
        on_device,
        mesh=mesh,
        in_specs=placed,
        out_specs=(
            P(("rep", "shard"), None),
            P(("rep", "shard"), None),
            P(None, "shard", None),
            P(None, "shard"),
            P(None, "shard", None),
            P(None, "shard", None),
            P(None, "shard"),
            P(None, "shard", None),
            P(None, "shard"),
            P(None, "shard"),
            P(None, "shard"),
        ),
        check_vma=False,
    )
```

```python
import functools
import math

import jax
import jax.numpy as jnp
import numpy as np
from jax import lax
from jax.experimental import pallas as pl
from jax.experimental.pallas import tpu as pltpu
from jax.sharding import PartitionSpec as P


STEP_NAMES = (
    "s", "q", "u", "o", "d", "Q", "U", "O", "D", "S", "vec", "fnorm", "joined", "fattnA",
    "fattnB", "up", "down", "res", "start", "low", "gdown", "slope", "gup", "dmixed", "gout",
    "battnA", "battnB", "dhidden", "gqkv", "norm", "pack",
)
(
    s0, s1, q0, q1, u0, u1, o0, o1, d0, d1, Q0, Q1, U0, U1, O0, O1, D0, D1, S0, S1, vec0, vec1,
    fnorm0, fnorm1, joined0, joined1, fattnA0, fattnA1, fattnB0, fattnB1, up0, up1, down0, down1,
    res0, res1, start0, start1, low0, low1, gdown0, gdown1, slope0, slope1, gup0, gup1, dmixed0,
    dmixed1, gout0, gout1, battnA0, battnA1, battnB0, battnB1, dhidden0, dhidden1, gqkv0, gqkv1,
    norm0, norm1, pack0, pack1,
) = range(2 * len(STEP_NAMES))
SCHEDULE = (
    s0, o0, q0, o1, s0, o0, u0, s0, q0, o1, o0, d0, s0, u1, q1, q0, u0, s0, o1, q0, d1, d0, d0,
    u0, q1, q0, d0, s0, s0, vec0, q1, fnorm0, q0, o0, u0, d0, o0, q0, joined0, u0, fattnA0, o0,
    q1, d1, u1, o1, u0, d0, fattnB0, u1, o0, u0, q1, u1, d0, up0, q1, down0, d1, o1, u1, q1, res0,
    fnorm1, o1, d1, joined1, start1, u1, fattnA1, o1, d1, fattnB1, u1, low1, dmixed1, battnA1, d1,
    gout1, up1, O1, gdown1, D1, d1, battnB1, slope1, O1, gup1, U1, O1, D1, down1, gqkv1, D1, Q1,
    res1, dhidden1, U1, O1, norm1, start0, low0, O1, Q1, gout0, D1, dmixed0, O0, U1, gdown0, D0,
    D1, Q1, battnA0, O0, slope0, D1, U1, gup0, U0, D0, U1, O0, battnB0, Q1, D0, gqkv0, Q0, U0, D1,
    dhidden0, Q1, D1, D0, Q0, U1, pack1, O1, U0, norm0, pack0, U1, U1, S0, Q1, Q0, D0, O1, U0, O1,
    Q1, S0, U0, D0, O0, Q1, Q0, S0, U0, O0, Q0, S0, O0, S0, Q0, D0, O0, U0, S0, Q0, D0, S0, Q0,
    O0, U0, S0,
)


MESH = pl.DeviceIdType.MESH
LANE = 128
LAYERS = 2


def place():
    xl = lax.axis_index("rep")
    s = lax.axis_index("shard")
    return xl, s // 32, (s // 8) % 4, (s // 2) % 4, s % 2


def at(xl, xh, z, y, c):
    return (xl, xh * 32 + z * 8 + y * 2 + c)


def around(value, step):
    return lax.rem(value + (step + 4), 4)


def meet(others):
    barrier = pltpu.get_barrier_semaphore()
    for other in others:
        pl.semaphore_signal(barrier, inc=1, device_id=other, device_id_type=MESH)
    pl.semaphore_wait(barrier, len(others))


GATHERED = (
    ("small", True, 32, 128, 0, 1),
    ("qkv", True, 32, 1536, 4, 8),
    ("up", True, 32, 2048, 5, 11),
    ("out", False, 32, 1024, 3, 5),
    ("down", False, 128, 1024, 3, 5),
)
SLOTS = 18


class Stream:
    def __init__(self, number, spec, source, target, send, recv, xl, xh, z, y, core):
        self.name, self.by_columns, self.rows, self.columns, self.swapped, self.width = spec
        self.number = number
        self.source = source
        self.target = target
        self.send, self.recv = send, recv
        self.xl, self.xh, self.z, self.y, self.core = xl, xh, z, y, core
        self.half = self.rows // 2
        self.wide = pl.ds(pl.multiple_of(xl * (self.swapped * LANE), LANE), self.width * LANE)
        self.mine = pl.ds(
            pl.multiple_of(xl * ((self.width - self.swapped) * LANE) + xl * (self.swapped * LANE), LANE),
            max(self.swapped, 1) * LANE,
        )
        self.theirs = pl.ds(
            pl.multiple_of((1 - xl) * (self.width * LANE), LANE), max(self.swapped, 1) * LANE
        )
        self.across = lambda core_of: at(1 - xl, 1 - xh, z, y, core_of)
        self.partner = at(1 - xl, xh, z, y, core) if core == 0 else self.across(core)
        if core == 0:
            self.first, self.second = y, z
        else:
            self.first, self.second = z, y
        self.sent = []

    def neighbour(self, ring, step):
        z, y = self.z, self.y
        if (ring == 0) == (self.core == 0):
            y = around(y, step)
        else:
            z = around(z, step)
        return at(self.xl, self.xh, z, y, self.core)

    def block(self, first, rows, columns):
        if self.core == 0:
            return self.target.at[:, self.second, first, rows, columns]
        return self.target.at[:, first, self.second, rows, columns]

    def line(self, second, rows, columns):
        if self.core == 0:
            return self.target.at[:, second, :, rows, columns]
        return self.target.at[:, :, second, rows, columns]

    def push(self, region, slot, device):
        copy = pltpu.make_async_remote_copy(
            region(),
            region(),
            self.send.at[self.number, slot],
            self.recv.at[self.number, slot],
            device_id=device,
            device_id_type=MESH,
        )
        copy.start()
        self.sent.append((region, slot))

    def arrived(self, region, slot):
        pltpu.make_async_copy(region, region, self.recv.at[self.number, slot]).wait()

    def part(self, core_of):
        return pl.ds(core_of * self.half, self.half)

    def stage0(self):
        xh, z, y, core = self.xh, self.z, self.y, self.core
        whole = slice(None)
        if self.by_columns:
            region = lambda: self.target.at[xh, z, y, self.part(core), :]
            here = region()
            landed = self.recv.at[self.number, xh * 2 + core]
            for source, columns in self.source(core):
                pltpu.make_async_copy(source, here.at[:, columns], landed).start()
            for slot, half, device in (
                (0, 1 - core, at(self.xl, xh, z, y, 1 - core)),
                (1, core, self.across(core)),
                (2, 1 - core, self.across(1 - core)),
            ):
                for source, columns in self.source(half):
                    pltpu.make_async_remote_copy(
                        source,
                        here.at[:, columns],
                        self.send.at[self.number, slot],
                        landed,
                        device_id=device,
                        device_id_type=MESH,
                    ).start()
                self.sent.append((region, slot))
        else:
            here = self.target.at[0, z, y, self.part(core), :]
            mine = self.source(0)

            @pl.when(xh == core)
            def _():
                pltpu.make_async_copy(mine, here, self.recv.at[self.number, core]).start()

            @pl.when(xh != core)
            def _():
                pltpu.make_async_remote_copy(
                    mine,
                    here,
                    self.send.at[self.number, 0],
                    self.recv.at[self.number, core],
                    device_id=at(self.xl, xh, z, y, 1 - core),
                    device_id_type=MESH,
                ).start()

            pltpu.make_async_remote_copy(
                mine,
                here,
                self.send.at[self.number, 1],
                self.recv.at[self.number, core],
                device_id=self.across(xh),
                device_id_type=MESH,
            ).start()
            self.sent.append((lambda: self.source(0), 1))

    def stage1(self):
        whole = slice(None)
        for bank in range(2 if self.by_columns else 1):
            for core_of in range(2):
                self.arrived(
                    self.target.at[bank, self.z, self.y, self.part(core_of), :], bank * 2 + core_of
                )
        own = lambda: self.block(self.first, whole, self.wide)
        self.push(own, 4, self.neighbour(0, 1))
        self.push(own, 5, self.neighbour(0, -1))

    def share(self, region, slot):
        if self.swapped:
            self.push(lambda: region(self.mine), slot, self.partner)

    def stage2(self):
        whole = slice(None)
        for step, slot in ((-1, 4), (1, 5)):
            found = lambda rows, columns, step=step: self.block(
                around(self.first, step), rows, columns
            )
            self.arrived(found(whole, self.wide), slot)
            self.push(
                lambda found=found, slot=slot: found(self.part(slot - 4), self.wide),
                slot + 2,
                self.neighbour(0, -step),
            )
            self.share(lambda columns, found=found: found(whole, columns), slot + 8)

    def stage3(self):
        whole = slice(None)
        far = lambda rows, columns: self.block(around(self.first, 2), rows, columns)
        for half in range(2):
            self.arrived(far(self.part(half), self.wide), 6 + half)
        own = lambda: self.line(self.second, whole, self.wide)
        self.push(own, 8, self.neighbour(1, 1))
        self.push(own, 9, self.neighbour(1, -1))
        self.share(lambda columns: far(whole, columns), 14)

    def stage4(self):
        whole = slice(None)
        for step, slot in ((-1, 8), (1, 9)):
            found = lambda rows, columns, step=step: self.line(
                around(self.second, step), rows, columns
            )
            self.arrived(found(whole, self.wide), slot)
            self.push(
                lambda found=found, slot=slot: found(self.part(slot - 8), self.wide),
                slot + 2,
                self.neighbour(1, -step),
            )
            self.share(lambda columns, found=found: found(whole, columns), slot + 7)

    def stage5(self):
        whole = slice(None)
        far = lambda rows, columns: self.line(around(self.second, 2), rows, columns)
        for half in range(2):
            self.arrived(far(self.part(half), self.wide), 10 + half)
        self.share(lambda columns: far(whole, columns), 17)

    def stage6(self):
        whole = slice(None)
        if self.swapped:
            for step, slot in ((-1, 12), (1, 13), (2, 14)):
                self.arrived(self.block(around(self.first, step), whole, self.theirs), slot)
            for step, slot in ((-1, 15), (1, 16), (2, 17)):
                self.arrived(self.line(around(self.second, step), whole, self.theirs), slot)

    def finish(self):
        for region, slot in self.sent:
            pltpu.make_async_copy(region(), region(), self.send.at[self.number, slot]).wait()
        self.sent = []
        if not self.by_columns:

            @pl.when(self.xh != self.core)
            def _():
                mine = self.source(0)
                pltpu.make_async_copy(mine, mine, self.send.at[self.number, 0]).wait()


def owned_pieces(name, owned, layer_at):
    if name == "small":
        return lambda half: [(owned, slice(None))]
    if name == "qkv":
        return lambda half: [
            (
                owned.at[layer_at, :, pl.ds(third * 1024 + half * 512, 512)],
                pl.ds(third * 512, 512),
            )
            for third in range(3)
        ]
    if name == "up":
        return lambda half: [(owned.at[layer_at, :, pl.ds(half * 2048, 2048)], slice(None))]
    return lambda half: owned.at[layer_at]


def neighbours():
    xl, xh, z, y, c = place()
    return [
        at(xl, xh, z, y, 1 - c),
        at(1 - xl, 1 - xh, z, y, c),
        at(1 - xl, 1 - xh, z, y, 1 - c),
        at(xl, 1 - xh, z, y, c),
        at(1 - xl, xh, z, y, c),
        at(xl, xh, around(z, 1), y, c),
        at(xl, xh, around(z, -1), y, c),
        at(xl, xh, z, around(y, 1), c),
        at(xl, xh, z, around(y, -1), c),
    ]


COUNT = 256
BOTH = 512
D = 1024
HEAD_DIM = 64
ROT = 16
EPS = 1e-05
FILL = -1e30
F32 = jnp.float32
BF16 = jnp.bfloat16
TILE = 256


def turn_tables():
    places = np.arange(COUNT, dtype=np.float32)
    rates = np.float32(10000.0) ** (-np.arange(0, ROT, 2, dtype=np.float32) / np.float32(ROT))
    angles = places[:, None] * rates[None, :]
    cosine, sine = np.cos(angles), np.sin(angles)
    half = ROT // 2
    keep = np.ones((COUNT, HEAD_DIM), np.float32)
    ahead = np.zeros((COUNT, HEAD_DIM), np.float32)
    behind = np.zeros((COUNT, HEAD_DIM), np.float32)
    keep[:, :half] = cosine
    keep[:, half:ROT] = cosine
    ahead[:, :half] = -sine
    behind[:, half:ROT] = sine
    return np.stack([np.concatenate([t, t], 1) for t in (keep, ahead, behind)])


def turn(values, tables, sign):
    return values * tables[0] + sign * (
        pltpu.roll(values, LANE - ROT // 2, 1) * tables[1]
        + pltpu.roll(values, ROT // 2, 1) * tables[2]
    )


def dot(left, right):
    return jnp.dot(left, right, preferred_element_type=F32)


def dot_nt(left, right):
    return lax.dot_general(left, right, (((1,), (1,)), ((), ())), preferred_element_type=F32)


def dot_tn(left, right):
    return lax.dot_general(left, right, (((0,), (0,)), ((), ())), preferred_element_type=F32)


def columns_of(index, width=TILE):
    return pl.ds(pl.multiple_of(index * width, width), width)


def loop(count, body):
    def step(index, carry):
        body(index)
        return carry

    lax.fori_loop(0, count, step, 0)


KINDS = {
    "b_qkv": (0, 48, 43691, 21),
    "b_up": (1, 64, 1, 6),
    "gain": (2, 16, 1, 4),
    "shift": (3, 16, 1, 4),
    "out_bias": (4, 16, 1, 4),
}
OWNED_ROWS = 16
CHUNK = 512


def chunks_of(kind, core):
    if kind == "b_qkv":
        return [(t * CHUNK, t * 1024 + core * CHUNK) for t in range(3)]
    if kind == "b_up":
        return [(t * CHUNK, core * 2048 + t * CHUNK) for t in range(4)]
    return [(t * CHUNK, t * CHUNK) for t in range(2)]


def owner_masks(kind, start):
    row, size, factor, shift = KINDS[kind]
    place_of = lax.broadcasted_iota(jnp.int32, (LANE, CHUNK), 1) + start
    owner = lax.shift_right_logical(place_of * factor, shift)
    within = place_of - owner * size
    spread = lax.broadcasted_iota(jnp.int32, (LANE, CHUNK), 0) == within
    owned = lax.broadcasted_iota(jnp.int32, (64, CHUNK), 0) == owner[:64]
    return spread, owned


def unpack_vector(rows_ref, layer_at, kind, core, target):
    row = KINDS[kind][0] + 5 * layer_at
    held = rows_ref[pl.ds(row, 64, stride=OWNED_ROWS), :].astype(BF16)
    for place_at, start in chunks_of(kind, core):
        spread, owned = owner_masks(kind, start)
        every = dot(held, jnp.where(spread, 1.0, 0.0).astype(BF16))
        target[:, pl.ds(place_at, CHUNK)] = jnp.sum(
            jnp.where(owned, every, 0.0), 0, keepdims=True
        )


def pack_vector(rows_ref, layer_at, kind, core, vector):
    total = jnp.zeros((64, LANE), F32)
    for place_at, start in chunks_of(kind, core):
        spread, owned = owner_masks(kind, start)
        mine = jnp.where(owned, vector[:, pl.ds(place_at, CHUNK)], 0.0)
        spread = jnp.where(spread, 1.0, 0.0).astype(BF16)
        high = mine.astype(BF16)
        total = total + dot_nt(high, spread)
        total = total + dot_nt((mine - high.astype(F32)).astype(BF16), spread)
    rows_ref[pl.ds(KINDS[kind][0] + 5 * layer_at, 64, stride=OWNED_ROWS), :] = total


def centre(values):
    centred = values - jnp.mean(values, -1, keepdims=True)
    inv_std = lax.rsqrt(jnp.mean(centred * centred, -1, keepdims=True) + EPS)
    return centred * inv_std, inv_std


def norm_piece(x_ref, gain, shift, hidden):
    def body(index):
        rows = columns_of(index, 64)
        normed, unused = centre(x_ref[rows, :].astype(F32))
        hidden[rows, :] = (normed * gain[...] + shift[...]).astype(BF16)

    loop(COUNT // 64, body)


def joined_piece(third, hidden, w_qkv, b_qkv, tables, target):
    def body(index):
        columns = columns_of(index + third * 2)
        found = dot(hidden[...], w_qkv(columns)) + b_qkv[:, columns]
        for sequence in range(2):
            for pair in range(2):
                part = found[sequence * COUNT : (sequence + 1) * COUNT, pair * LANE : (pair + 1) * LANE]
                if third < 2:
                    part = turn(part, tables, 1.0)
                if third == 0:
                    part = part * HEAD_DIM**-0.5
                target[
                    pl.ds(sequence * COUNT, COUNT), columns_of(index * 2 + pair + third * 4, LANE)
                ] = part.astype(BF16)

    loop(2, body)


def first_head():
    return lax.broadcasted_iota(jnp.int32, (COUNT, LANE), 1) < HEAD_DIM


def only_head(values, half):
    keep = first_head() if half == 0 else jnp.logical_not(first_head())
    return jnp.where(keep, values, jnp.zeros_like(values))


def attention_piece(turned, probs, mixed, start=0, stop=8):
    def body(index):
        index = index + start
        sequence, pair = index // 4, index % 4
        rows, columns = columns_of(sequence, COUNT), columns_of(pair, LANE)
        q2, k2, v2 = (turned[rows, columns_of(pair + third * 4, LANE)] for third in range(3))
        causal = lax.broadcasted_iota(jnp.int32, (COUNT, COUNT), 0) >= lax.broadcasted_iota(
            jnp.int32, (COUNT, COUNT), 1
        )
        out = []
        for half in range(2):
            scores = jnp.where(causal, dot_nt(only_head(q2, half), k2), FILL)
            expo = jnp.exp(scores - jnp.max(scores, -1, keepdims=True))
            prob = (expo * (1.0 / jnp.sum(expo, -1, keepdims=True))).astype(BF16)
            probs[index * 2 + half] = prob
            out.append(dot(prob, v2))
        mixed[rows, columns] = jnp.where(first_head(), out[0], out[1]).astype(BF16)

    loop(stop - start, body)


def up_piece(hidden, w_up, b_up, active, slope):
    def body(index):
        columns = columns_of(index)
        upward = dot(hidden[...], w_up(columns)) + b_up[:, columns]
        spread = 0.5 + 0.5 * lax.erf(upward * (0.5**0.5))
        active[:, columns] = (upward * spread).astype(BF16)
        dense = jnp.exp(upward * upward * -0.5) * (1.0 / math.sqrt(2.0 * math.pi))
        slope[:, columns] = (spread + upward * dense).astype(BF16)

    loop(8, body)


def down_piece(active, w_down, mixed, w_out, partial):
    def body(index):
        columns = columns_of(index)
        partial[:, columns] = dot(mixed[...], w_out(columns)) + dot(active[...], w_down(columns))

    loop(4, body)


def residual_piece(x_ref, partial, received, out_bias, target):
    def body(index):
        rows = columns_of(index, 64)
        target[rows, :] = (
            x_ref[rows, :].astype(F32)
            + (partial[rows, :] + received[rows, :])
            + out_bias[...]
        ).astype(target.dtype)

    loop(COUNT // 64, body)


def start_piece(dy, dy_low, out_bias_grad):
    def body(index):
        rows = columns_of(index, 64)
        values = dy[rows, :]
        dy_low[rows, :] = values.astype(BF16)
        out_bias_grad[...] += jnp.sum(values, 0, keepdims=True)

    out_bias_grad[...] = jnp.zeros_like(out_bias_grad)
    loop(COUNT // 64, body)


def flip_piece(source, target):
    rows, columns = source.shape
    for at_row in range(rows // TILE):

        def body(index, at_row=at_row):
            target[columns_of(index), pl.ds(at_row * TILE, TILE)] = source[
                pl.ds(at_row * TILE, TILE), columns_of(index)
            ].T

        loop(columns // TILE, body)


def rows_grad_piece(count, left, right, store):
    def body(index):
        store(index, dot_tn(left[:, columns_of(index)], right[...]).astype(BF16))

    loop(count, body)


def columns_grad_piece(count, left_flipped, right, store):
    def body(index):
        store(index, dot(left_flipped[...], right[:, columns_of(index)]).astype(BF16))

    loop(count, body)


def slope_piece(dy_low, w_down_rows, slope, d_up, b_up_grad):
    def body(index):
        columns = columns_of(index)
        found = (dot_nt(dy_low[...], w_down_rows(index)) * slope[:, columns].astype(F32)).astype(BF16)
        d_up[:, columns] = found
        b_up_grad[:, columns] = jnp.sum(found.astype(F32), 0, keepdims=True)

    loop(8, body)


def d_mixed_piece(dy_low, w_out_rows, d_mixed):
    def body(index):
        d_mixed[:, columns_of(index)] = dot_nt(dy_low[...], w_out_rows(index)).astype(BF16)

    loop(2, body)


def attention_back_piece(turned, probs, d_mixed, tables, d_joined, b_qkv_grad, start=0, stop=8):
    if start == 0:
        b_qkv_grad[...] = jnp.zeros_like(b_qkv_grad)

    def body(index):
        index = index + start
        sequence, pair = index // 4, index % 4
        rows, columns = columns_of(sequence, COUNT), columns_of(pair, LANE)
        q2, k2, v2 = (turned[rows, columns_of(pair + third * 4, LANE)] for third in range(3))
        dm2 = d_mixed[rows, columns]
        found = []
        for half in range(2):
            prob = probs[index * 2 + half]
            full = prob.astype(F32)
            d_probs = dot_nt(only_head(dm2, half), v2)
            d_scores = (
                full * (d_probs - jnp.sum(d_probs * full, -1, keepdims=True))
            ).astype(BF16)
            found.append((dot(d_scores, k2), dot_tn(d_scores, q2), dot_tn(prob, dm2)))
        for third in range(3):
            part = jnp.where(first_head(), found[0][third], found[1][third])
            if third == 0:
                part = part * HEAD_DIM**-0.5
            if third < 2:
                part = turn(part, tables, -1.0)
            part = part.astype(BF16)
            there = columns_of(pair + third * 4, LANE)
            d_joined[rows, there] = part
            b_qkv_grad[:, there] += jnp.sum(part.astype(F32), 0, keepdims=True)

    loop(stop - start, body)


def d_hidden_piece(d_joined, w_qkv_rows, d_up, w_up_rows, d_hidden):
    def body(index):
        d_hidden[:, columns_of(index)] = dot_nt(d_joined[...], w_qkv_rows(index)) + dot_nt(
            d_up[...], w_up_rows(index)
        )

    loop(4, body)


def norm_back_piece(x_ref, gain, dy, d_hidden, received, target, gain_grad, shift_grad):
    gain_grad[...] = jnp.zeros_like(gain_grad)
    shift_grad[...] = jnp.zeros_like(shift_grad)

    def body(index):
        rows = columns_of(index, 64)
        normed, inv_std = centre(x_ref[rows, :].astype(F32))
        total = d_hidden[rows, :] + received[rows, :]
        gain_grad[...] += jnp.sum(total * normed, 0, keepdims=True)
        shift_grad[...] += jnp.sum(total, 0, keepdims=True)
        scaled = total * gain[...]
        target[rows, :] = dy[rows, :].astype(F32) + inv_std * (
            scaled
            - jnp.mean(scaled, -1, keepdims=True)
            - normed * jnp.mean(scaled * normed, -1, keepdims=True)
        )

    loop(COUNT // 64, body)


SUMMED = (
    ("qkv", True, 32, 1536, 3, 9),
    ("up", True, 32, 2048, 4, 12),
    ("out", False, 32, 1024, 2, 6),
    ("down", False, 128, 1024, 2, 6),
    ("small", True, 32, 128, 0, 1),
)
SUM_SLOTS = 18
BUFFERS = 9


def total_shape(spec):
    name, by_columns, rows, columns, swapped, width = spec
    return (2 if by_columns else 1, 4, 4, rows, columns)


def landing_shapes(spec):
    name, by_columns, rows, columns, swapped, width = spec
    banks = 2 if by_columns else 1
    kind = F32 if name == "small" else BF16
    wide = width * LANE
    return [
        pltpu.VMEM((banks, 4, 4, rows, swapped * LANE) if swapped else (8, LANE), kind),
        pltpu.VMEM((2, banks, 4, rows // 2, wide), kind),
        pltpu.VMEM((2, banks, 4, rows, wide), kind),
        pltpu.VMEM((banks, 4, rows, wide), kind),
        pltpu.VMEM((2, banks, rows // 2, wide), kind),
        pltpu.VMEM((2, banks, rows, wide), kind),
        pltpu.VMEM((3, rows, wide), kind),
        pltpu.VMEM((rows, columns), F32),
        pltpu.VMEM((2, 16, LANE), F32),
    ]


def add_into(target, first, *others):
    if len(others) == 1:
        target[...] = first[...] + others[0][...]
    else:
        found = first[...].astype(F32)
        for other in others:
            found = found + other[...].astype(F32)
        target[...] = found.astype(target.dtype)


sum_loop = loop


class Sum:
    def __init__(self, number, which, before, total, landing, output, send, recv, free, where, core):
        spec = SUMMED[which]
        self.name, self.by_columns, self.rows, self.columns, self.swapped, self.width = spec
        self.number, self.which = number, which
        self.before = before
        self.after = not before and self.name != "small"
        self.total, self.output = total, output
        (
            self.swap,
            self.far_line,
            self.near_line,
            self.line,
            self.far_block,
            self.near_block,
            self.last,
            self.ready,
            self.tail,
        ) = landing
        self.send, self.recv, self.free = send, recv, free
        self.xl, self.xh, self.z, self.y = where
        self.core = core
        self.banks = 2 if self.by_columns else 1
        self.half = self.rows // 2
        s, w = self.swapped, self.width
        xl, xh, z, y = where
        self.wide = pl.ds(pl.multiple_of(xl * (s * LANE), LANE), w * LANE)
        self.mine = pl.ds(pl.multiple_of(xl * (w * LANE), LANE), max(s, 1) * LANE)
        self.theirs = pl.ds(pl.multiple_of((1 - xl) * (w * LANE), LANE), max(s, 1) * LANE)
        self.beside = at(1 - xl, xh, z, y, core)
        self.across = at(1 - xl, 1 - xh, z, y, core)
        self.beyond = at(xl, 1 - xh, z, y, core)
        self.sibling = at(xl, xh, z, y, 1 - core)
        self.partner = self.beside if core == 0 else self.across
        self.first, self.second = (y, z) if core == 0 else (z, y)
        self.sent = []

    def neighbour(self, ring, step):
        z, y = self.z, self.y
        if (ring == 0) == (self.core == 0):
            y = around(y, step)
        else:
            z = around(z, step)
        return at(self.xl, self.xh, z, y, self.core)

    def total_line(self, second, rows, columns):
        if self.core == 0:
            return self.total.at[:, second, :, rows, columns]
        return self.total.at[:, :, second, rows, columns]

    def push(self, source, target, slot, device, keep=True):
        if self.before and slot < 12:
            pl.semaphore_wait(self.free.at[self.which, slot], 1)
        pltpu.make_async_remote_copy(
            source(),
            target,
            self.send.at[self.number, slot],
            self.recv.at[self.number, slot],
            device_id=device,
            device_id_type=MESH,
        ).start()
        if keep:
            self.sent.append((source, slot))

    def release(self, slot, device):
        if self.after:
            pl.semaphore_signal(
                self.free.at[self.which, slot], inc=1, device_id=device, device_id_type=MESH
            )

    def arrived(self, region, slot):
        pltpu.make_async_copy(region, region, self.recv.at[self.number, slot]).wait()

    def settle(self):
        for source, slot in self.sent:
            pltpu.make_async_copy(source(), source(), self.send.at[self.number, slot]).wait()
        self.sent = []

    def part(self, core_of):
        return pl.ds(core_of * self.half, self.half)

    def stage1(self):
        if self.swapped:
            self.push(
                lambda: self.total.at[:, :, :, :, self.theirs], self.swap, 0, self.partner
            )

    def stage2(self):
        if self.swapped:
            self.arrived(self.swap, 0)

            def add(step):
                bank, z, y = step // 16, (step // 4) % 4, step % 4
                region = self.total.at[bank, z, y, :, self.mine]
                add_into(region, region, self.swap.at[bank, z, y])

            sum_loop(self.banks * 16, add)
            self.release(0, self.partner)
        for half in range(2):
            self.push(
                lambda half=half: self.total_line(
                    around(self.second, 2), self.part(half), self.wide
                ),
                self.far_line.at[half],
                1 + half,
                self.neighbour(1, 1 - 2 * half),
            )

    def stage3(self):
        for half in range(2):
            self.arrived(self.far_line.at[half], 1 + half)
            toward = 1 - 2 * half
            rows = self.part(half)

            def add(step):
                bank, place_at = step // 4, step % 4
                region = self.total_line(around(self.second, toward), rows, self.wide).at[
                    bank, place_at
                ]
                add_into(region, region, self.far_line.at[half, bank, place_at])

            sum_loop(self.banks * 4, add)
            self.release(1 + half, self.neighbour(1, -toward))
            self.push(
                lambda toward=toward: self.total_line(
                    around(self.second, toward), slice(None), self.wide
                ),
                self.near_line.at[half],
                3 + half,
                self.neighbour(1, toward),
            )

    def stage4(self):
        for half in range(2):
            self.arrived(self.near_line.at[half], 3 + half)

        def add(step):
            bank, place_at = step // 4, step % 4
            add_into(
                self.line.at[bank, place_at],
                self.total_line(self.second, slice(None), self.wide).at[bank, place_at],
                self.near_line.at[0, bank, place_at],
                self.near_line.at[1, bank, place_at],
            )

        sum_loop(self.banks * 4, add)
        for half in range(2):
            self.release(3 + half, self.neighbour(1, 2 * half - 1))
        self.settle()
        for half in range(2):
            self.push(
                lambda half=half: self.line.at[:, around(self.first, 2), self.part(half), :],
                self.far_block.at[half],
                5 + half,
                self.neighbour(0, 1 - 2 * half),
            )

    def stage5(self):
        for half in range(2):
            self.arrived(self.far_block.at[half], 5 + half)
            toward = 1 - 2 * half
            for bank in range(self.banks):
                region = self.line.at[bank, around(self.first, toward), self.part(half), :]
                add_into(region, region, self.far_block.at[half, bank])
            self.release(5 + half, self.neighbour(0, -toward))
            self.push(
                lambda toward=toward: self.line.at[:, around(self.first, toward)],
                self.near_block.at[half],
                7 + half,
                self.neighbour(0, toward),
            )

    def own(self, bank):
        return self.line.at[bank, self.first]

    def stage6(self):
        for half in range(2):
            self.arrived(self.near_block.at[half], 7 + half)
        for bank in range(self.banks):
            add_into(
                self.own(bank),
                self.own(bank),
                self.near_block.at[0, bank],
                self.near_block.at[1, bank],
            )
        for half in range(2):
            self.release(7 + half, self.neighbour(0, 2 * half - 1))
        if self.by_columns:
            self.push(lambda: self.own(self.xh), self.last.at[0], 9, self.beside)
            self.push(lambda: self.own(1 - self.xh), self.last.at[1], 10, self.across)
            self.push(lambda: self.own(1 - self.xh), self.last.at[2], 11, self.beyond)
        else:

            @pl.when(self.xh == self.core)
            def _():
                self.push(lambda: self.own(0), self.last.at[0], 9, self.beside, False)

            @pl.when(self.xh != self.core)
            def _():
                self.push(lambda: self.own(0), self.last.at[1], 10, self.across, False)
                self.push(lambda: self.own(0), self.last.at[2], 11, self.beyond, False)

    def add_last(self):
        for slot in range(3):
            self.arrived(self.last.at[slot], 9 + slot)
        s, w = self.swapped, self.width
        c = w - s
        own = self.own(self.xh if self.by_columns else 0)
        self.ready[:, self.wide] = own[...].astype(F32) + self.last[2].astype(F32)
        if s:
            there = pl.ds(pl.multiple_of((1 - self.xl) * (c * LANE), LANE), s * LANE)
            self.ready[:, self.theirs] = self.last[0, :, there].astype(F32) + self.last[
                1, :, there
            ].astype(F32)
        if c:
            middle = pl.ds(s * LANE, c * LANE)
            there = pl.ds(pl.multiple_of(self.xl * (s * LANE), LANE), c * LANE)
            self.ready[:, middle] = (
                self.ready[:, middle]
                + self.last[0, :, there].astype(F32)
                + self.last[1, :, there].astype(F32)
            )
        for slot, device in ((9, self.beside), (10, self.across), (11, self.beyond)):
            self.release(slot, device)

    def pieces(self, core_of):
        rows = self.part(core_of)
        if self.name == "qkv":
            return [
                (
                    self.ready.at[rows, pl.ds(third * 512, 512)],
                    self.output.at[:, pl.ds(third * 1024 + self.core * 512, 512)],
                )
                for third in range(3)
            ]
        if self.name == "up":
            return [(self.ready.at[rows, :], self.output.at[:, pl.ds(self.core * 2048, 2048)])]
        return [(self.ready.at[rows, :], self.output)]

    def deliver(self):
        for index, (source, target) in enumerate(self.pieces(self.core)):
            pltpu.make_async_copy(source, target, self.recv.at[self.number, 15 + index]).start()
        for index, (source, target) in enumerate(self.pieces(1 - self.core)):
            self.push(lambda: source, target, 12 + index, self.sibling, False)

    def delivered(self):
        for index, (source, target) in enumerate(self.pieces(self.core)):
            pltpu.make_async_copy(source, target, self.recv.at[self.number, 15 + index]).wait()
        for index, (source, target) in enumerate(self.pieces(1 - self.core)):
            pltpu.make_async_copy(source, source, self.send.at[self.number, 12 + index]).wait()

    def stage7(self):
        if self.name == "small":
            self.add_last()
            self.push(
                lambda: self.ready.at[self.part(1 - self.core), :], self.tail.at[0], 12, self.sibling
            )
        elif self.by_columns:
            self.add_last()
            self.deliver()
        else:

            @pl.when(self.xh == self.core)
            def _():
                self.add_last()
                self.deliver()

    def stage8(self):
        core = self.core
        if self.name == "small":
            self.arrived(self.tail.at[0], 12)
            self.tail[1] = self.ready[self.part(core), :] + self.tail[0]
        elif self.by_columns:
            self.delivered()
            for index, (source, target) in enumerate(self.pieces(1 - core)):
                self.arrived(source, 12 + index)
        else:

            @pl.when(self.xh == core)
            def _():
                self.delivered()

            @pl.when(self.xh != core)
            def _():
                self.arrived(self.output, 12)

        self.settle()
        if not self.by_columns:

            @pl.when(self.xh == core)
            def _():
                own = self.own(0)
                pltpu.make_async_copy(own, own, self.send.at[self.number, 9]).wait()

            @pl.when(self.xh != core)
            def _():
                own = self.own(0)
                pltpu.make_async_copy(own, own, self.send.at[self.number, 10]).wait()
                pltpu.make_async_copy(own, own, self.send.at[self.number, 11]).wait()


QKV, UP, OUT, DOWN, SMALL = range(5)
WEIGHTS = GATHERED[1:]
WEIGHT_NAMES = tuple(spec[0] for spec in WEIGHTS)

FLIPPED, TURNED, PROBS, MIXED, ACTIVE = range(5)

KEPT = (
    (FLIPPED, (D, BOTH), BF16),
    (TURNED, (BOTH, 1536), BF16),
    (PROBS, (16, COUNT, COUNT), BF16),
    (MIXED, (BOTH, 512), BF16),
    (ACTIVE, (BOTH, 2048), BF16),
    ("slope", (BOTH, 2048), BF16),
)
KEPT_NAMES = tuple(name for name, dims, kind in KEPT)

TOUCHED = {
    "joined": ("qkv", TURNED, FLIPPED),
    "fattnA": (TURNED, PROBS, MIXED),
    "fattnB": (TURNED, PROBS, MIXED),
    "up": ("up", ACTIVE, "slope"),
    "down": ("down", "out", ACTIVE, MIXED),
    "gdown": (ACTIVE,),
    "slope": ("down", "slope"),
    "gup": (FLIPPED, "slope"),
    "dmixed": ("out",),
    "gout": (MIXED,),
    "battnA": (TURNED, PROBS),
    "battnB": (TURNED, PROBS),
    "dhidden": ("qkv", "up", TURNED, "slope"),
    "gqkv": (FLIPPED, TURNED),
}
FORWARD = ("joined", "fattnA", "fattnB", "up", "down")
WHOLE_AFTER = {
    TURNED: "joined",
    FLIPPED: "joined",
    PROBS: "fattnB",
    MIXED: "fattnB",
    ACTIVE: "up",
    "slope": "up",
}
GATHERS = {"s": 0, "q": 1, "u": 2, "o": 3, "d": 4}
SUMS = {"Q": QKV, "U": UP, "O": OUT, "D": DOWN, "S": SMALL}


class Pair:
    def __init__(self, send, recv):
        xl, xh, z, y, c = place()
        self.device = at(xl, xh, z, y, 1 - c)
        self.send, self.recv = send, recv

    def push(self, source, target, slot):
        pltpu.make_async_remote_copy(
            source,
            target,
            self.send.at[slot],
            self.recv.at[slot],
            device_id=self.device,
            device_id_type=MESH,
        ).start()

    def sent(self, source, slot):
        pltpu.make_async_copy(source, source, self.send.at[slot]).wait()

    def arrived(self, target, slot):
        pltpu.make_async_copy(target, target, self.recv.at[slot]).wait()


class Moves:
    def __init__(self, done):
        self.done = done
        self.count = 0
        self.open = []

    def start(self, source, target):
        copy = pltpu.make_async_copy(source, target, self.done.at[self.count])
        self.count += 1
        copy.start()
        self.open.append(copy)
        return copy

    def finish(self, copy):
        if any(other is copy for other in self.open):
            copy.wait()
            self.open = [other for other in self.open if other is not copy]


EARLY, LATE, LAST, GATHER = range(4)


def phase_of(step, layer_at):
    return LATE if layer_at else (EARLY if step in FORWARD else LAST)


def weight_shape(spec):
    name, by_columns, rows, columns, swapped, width = spec
    return (2 if by_columns else 1, 4, 4, rows, columns)


def all_rows(weight, columns):
    found = weight[:, :, :, :, columns]
    return found.reshape(-1, found.shape[-1])


def row_tile(weight, index):
    banks, unused, same, rows, columns = weight.shape
    if rows == 128:
        found = weight[0, index // 2, pl.ds((index % 2) * 2, 2)]
    elif banks == 2:
        found = weight[index // 2, pl.ds((index % 2) * 2, 2)]
    else:
        found = weight[0, pl.ds(index * 2, 2)]
    return found.reshape(TILE, columns)


def store_row_tile(total):
    def store(index, found):
        banks, unused, same, rows, columns = total.shape
        if rows == 128:
            total[0, index // 2, pl.ds((index % 2) * 2, 2)] = found.reshape(2, 128, columns)
        else:
            total[0, pl.ds(index * 2, 2)] = found.reshape(2, 4, 32, columns)

    return store


def store_column_tile(total):
    def store(index, found):
        total[:, :, :, :, columns_of(index)] = found.reshape(2, 4, 4, 32, TILE)

    return store


def blocks_kernel(schedule, tokens, out_grad, b_qkv, b_up, ln_gain, ln_bias, out_bias, tables, *rest):
    rest = list(rest)

    def take(count):
        found = rest[:count]
        del rest[:count]
        return found

    owned_weights = take(4)
    result, in_grad = take(2)
    large_out = take(4)
    gathered = [take(4) for layer_at in range(LAYERS)]
    spilled = dict(zip(KEPT_NAMES, take(len(KEPT))))
    (small_out,) = take(1)
    held = dict(zip(KEPT_NAMES + WEIGHT_NAMES, take(len(KEPT) + 4)))
    vectors = [dict(zip(KINDS, take(5))) for layer_at in range(LAYERS)]
    grads = [dict(zip(KINDS, take(5))) for layer_at in range(LAYERS)]
    owned, rows, x_late, dy = take(4)
    early, late = take(2)
    d_mixed, partial = take(2)
    received_one, received_two = take(2)
    totals = take(5)
    landing = [take(BUFFERS) for spec in SUMMED]
    send, recv, sum_send, sum_recv, free, pair_send, pair_recv, moved = take(8)
    every = totals[SMALL]
    hidden, dy_low = (early, late), (late, early)
    received = (received_one, received_two)
    received_grad = (received_one, received_one)
    inputs = (tokens, x_late)

    owned[...] = jnp.zeros_like(owned)
    for layer_at in range(LAYERS):
        for row, vector in enumerate((b_qkv, b_up, ln_gain, ln_bias, out_bias)):
            owned[5 * layer_at + row : 5 * layer_at + row + 1, : vector.shape[1]] = vector[
                layer_at : layer_at + 1, :
            ].astype(F32)
    xl, xh, z, y, c = place()
    where = (xl, xh, z, y)
    meet(neighbours())
    pair = Pair(pair_send, pair_recv)
    moves = Moves(moved)
    own, other = pl.ds(0, COUNT), pl.ds(COUNT, COUNT)

    streams, sums = {}, {}
    for core in range(2):
        streams[core, 0, 0] = Stream(
            0, GATHERED[0], owned_pieces("small", owned, 0), every, send, recv, *where, core
        )
        number = 0
        for layer_at in range(LAYERS):
            for which in range(4):
                number += 1
                streams[core, layer_at, which + 1] = Stream(
                    number, WEIGHTS[which],
                    owned_pieces(WEIGHT_NAMES[which], owned_weights[which], layer_at),
                    gathered[layer_at][which], send, recv, *where, core,
                )
                sums[core, layer_at, which] = Sum(
                    number, which, layer_at == 0, totals[which], landing[which],
                    large_out[which].at[layer_at], sum_send, sum_recv, free, where, core,
                )
        sums[core, 0, SMALL] = Sum(
            0, SMALL, False, totals[SMALL], landing[SMALL], None, sum_send, sum_recv, free, where, core
        )
    stage_of = {}

    def advance(table, layer_at, which, first):
        key = (id(table), layer_at, which)
        stage = stage_of[key] = stage_of.get(key, first - 1) + 1
        for core in range(2):

            @pl.when(c == core)
            def _():
                getattr(table[core, layer_at, which], f"stage{stage}")()

        return stage

    pending = {}
    for step, layer_at in schedule:
        for name in TOUCHED.get(step, ()):
            turn_of = phase_of(step, layer_at)
            pending[name, turn_of] = pending.get((name, turn_of), 0) + 1
    for name in WEIGHT_NAMES:
        for layer_at in range(LAYERS):
            pending[name, GATHER + layer_at] = 1
    loads, keeps = {}, {}

    def settle_load(name):
        if name in WEIGHT_NAMES:
            which = WEIGHT_NAMES.index(name)
            if not pending[name, GATHER] and (name, 0) not in loads:
                loads[name, 0] = moves.start(gathered[0][which], held[name])
            if not pending[name, GATHER + 1] and not pending[name, EARLY] and (name, 1) not in loads:
                loads[name, 1] = moves.start(gathered[1][which], held[name])
            source = gathered[0][which]
        else:
            source = spilled[name]
        if not pending[name, EARLY] and not pending[name, LATE] and (name, 2) not in loads:
            loads[name, 2] = moves.start(source, held[name])

    def before(step, layer_at):
        for name in TOUCHED.get(step, ()):
            if name in WEIGHT_NAMES:
                moves.finish(loads[name, phase_of(step, layer_at)])
            elif layer_at == 0 and step not in FORWARD:
                moves.finish(loads[name, 2])
            elif layer_at == 1 and step in FORWARD:
                moves.finish(keeps[name])

    def after(step, layer_at):
        for name in TOUCHED.get(step, ()):
            if layer_at == 0 and WHOLE_AFTER.get(name) == step:
                keeps[name] = moves.start(held[name], spilled[name])
            pending[name, phase_of(step, layer_at)] -= 1
            settle_load(name)

    def vec(layer_at):
        rows[...] = every[...].reshape(rows.shape)
        for core in range(2):

            @pl.when(c == core)
            def _():
                for layer in range(LAYERS):
                    for kind in KINDS:
                        unpack_vector(rows, layer, kind, core, vectors[layer][kind])

        rows[...] = jnp.zeros_like(rows)

    def fnorm(layer_at):
        norm_piece(inputs[layer_at], vectors[layer_at]["gain"], vectors[layer_at]["shift"], hidden[layer_at])
        pair.push(hidden[layer_at].at[own], hidden[layer_at].at[other], layer_at)

    def joined(layer_at):
        pair.sent(hidden[layer_at].at[own], layer_at)
        pair.arrived(hidden[layer_at].at[other], layer_at)
        for third in range(3):
            joined_piece(
                third, hidden[layer_at], lambda n: all_rows(held["qkv"], n),
                vectors[layer_at]["b_qkv"], tables, held[TURNED],
            )
        flip_piece(hidden[layer_at], held[FLIPPED])

    def fattn(start, stop):
        return lambda layer_at: attention_piece(held[TURNED], held[PROBS], held[MIXED], start, stop)

    def up(layer_at):
        up_piece(
            hidden[layer_at], lambda n: all_rows(held["up"], n), vectors[layer_at]["b_up"],
            held[ACTIVE], held["slope"],
        )

    def down(layer_at):
        if layer_at:
            pair.sent(partial.at[other], 2)
        down_piece(
            held[ACTIVE], lambda n: all_rows(held["down"], n), held[MIXED],
            lambda n: all_rows(held["out"], n), partial,
        )
        pair.push(partial.at[other], received[layer_at], 2 + layer_at)

    def res(layer_at):
        pair.arrived(received[layer_at], 2 + layer_at)
        target = late.at[own] if layer_at else x_late
        residual_piece(
            inputs[layer_at], partial, received[layer_at], vectors[layer_at]["out_bias"], target
        )
        if layer_at:
            loads["result"] = moves.start(target, result)

    def start(layer_at):
        if layer_at:
            for half in range(2):
                moves.finish(loads["out_grad", half])
                dy[:, pl.ds(half * 512, 512)] = d_mixed[pl.ds(half * COUNT, COUNT), :].astype(F32)
        else:
            moves.finish(loads["result"])
        start_piece(dy, dy_low[layer_at], grads[layer_at]["out_bias"])
        pair.push(dy_low[layer_at].at[own], dy_low[layer_at].at[other], 4 + layer_at)

    def low(layer_at):
        pair.sent(dy_low[layer_at].at[own], 4 + layer_at)
        pair.arrived(dy_low[layer_at].at[other], 4 + layer_at)

    def gdown(layer_at):
        rows_grad_piece(8, held[ACTIVE], dy_low[layer_at], store_row_tile(totals[DOWN]))

    def slope(layer_at):
        slope_piece(
            dy_low[layer_at], lambda n: row_tile(held["down"], n), held["slope"], held["slope"],
            grads[layer_at]["b_up"],
        )

    def gup(layer_at):
        columns_grad_piece(8, held[FLIPPED], held["slope"], store_column_tile(totals[UP]))

    def dmixed(layer_at):
        d_mixed_piece(dy_low[layer_at], lambda n: row_tile(held["out"], n), d_mixed)

    def gout(layer_at):
        rows_grad_piece(2, held[MIXED], dy_low[layer_at], store_row_tile(totals[OUT]))

    def battn(first, stop):
        return lambda layer_at: attention_back_piece(
            held[TURNED], held[PROBS], d_mixed, tables, held[TURNED], grads[layer_at]["b_qkv"],
            first, stop,
        )

    def dhidden(layer_at):
        pair.sent(partial.at[other], 3 if layer_at else 7)
        d_hidden_piece(
            held[TURNED], lambda n: row_tile(held["qkv"], n), held["slope"],
            lambda n: row_tile(held["up"], n), partial,
        )
        pair.push(partial.at[other], received_grad[layer_at], 6 + layer_at)

    def gqkv(layer_at):
        columns_grad_piece(6, held[FLIPPED], held[TURNED], store_column_tile(totals[QKV]))

    def norm(layer_at):
        pair.arrived(received_grad[layer_at], 6 + layer_at)
        norm_back_piece(
            inputs[layer_at], vectors[layer_at]["gain"], dy, partial, received_grad[layer_at], dy,
            grads[layer_at]["gain"], grads[layer_at]["shift"],
        )
        if layer_at == 0:
            moves.start(dy, in_grad)

    def pack(layer_at):
        for core in range(2):

            @pl.when(c == core)
            def _():
                for kind in KINDS:
                    pack_vector(rows, layer_at, kind, core, grads[layer_at][kind])
                if layer_at == 0:
                    streams[core, 0, 0].finish()

        if layer_at == 0:
            totals[SMALL][...] = rows[...].reshape(totals[SMALL].shape)

    for half in range(2):
        loads["out_grad", half] = moves.start(
            out_grad.at[:, pl.ds(half * 512, 512)], d_mixed.at[pl.ds(half * COUNT, COUNT), :]
        )
    steps = {
        "vec": vec, "fnorm": fnorm, "joined": joined, "fattnA": fattn(0, 4), "fattnB": fattn(4, 8),
        "up": up, "down": down, "res": res, "start": start, "low": low, "gdown": gdown, "slope": slope,
        "gup": gup, "dmixed": dmixed, "gout": gout, "battnA": battn(0, 4), "battnB": battn(4, 8),
        "dhidden": dhidden, "gqkv": gqkv, "norm": norm, "pack": pack,
    }
    for name, layer_at in schedule:
        with jax.named_scope(name):
            if name in GATHERS:
                stage = advance(streams, layer_at, GATHERS[name], 0)
                if stage == 6 and GATHERS[name]:
                    weight = WEIGHT_NAMES[GATHERS[name] - 1]
                    pending[weight, GATHER + layer_at] = 0
                    settle_load(weight)
            elif name in SUMS:
                advance(sums, layer_at, SUMS[name], 1)
            else:
                before(name, layer_at)
                steps[name](layer_at)
                after(name, layer_at)
    pair.sent(partial.at[other], 6)
    for core in range(2):

        @pl.when(c == core)
        def _():
            for (core_of, layer_at, which), stream in streams.items():
                if core_of == core:
                    stream.finish()

    small_out[...] = landing[SMALL][8][1]
    for copy in list(moves.open):
        copy.wait()


def blocks_call(tokens, out_grad, b_qkv, b_up, ln_gain, ln_bias, out_bias, tables, *owned_weights):
    vmem, hbm = pl.BlockSpec(memory_space=pltpu.VMEM), pl.BlockSpec(memory_space=pltpu.HBM)
    shape = jax.ShapeDtypeStruct
    outs = [
        shape((COUNT, D), BF16),
        shape((COUNT, D), F32),
        shape((LAYERS, 16, 3072), F32),
        shape((LAYERS, 16, 4096), F32),
        shape((LAYERS, 16, 1024), F32),
        shape((LAYERS, 64, 1024), F32),
    ]
    for layer_at in range(LAYERS):
        outs += [shape(weight_shape(spec), BF16) for spec in WEIGHTS]
    outs += [shape(dims, kind) for name, dims, kind in KEPT]
    in_hbm = len(outs)
    outs += [shape((OWNED_ROWS, LANE), F32)]
    scratch = [pltpu.VMEM(dims, kind) for name, dims, kind in KEPT]
    scratch += [pltpu.VMEM(weight_shape(spec), BF16) for spec in WEIGHTS]
    scratch += [pltpu.VMEM((1, n), F32) for n in (1536, 2048, D, D, D) * (2 * LAYERS)]
    scratch += [
        pltpu.VMEM((OWNED_ROWS, LANE), F32),
        pltpu.VMEM((64 * OWNED_ROWS, LANE), F32),
        pltpu.VMEM((COUNT, D), F32),
        pltpu.VMEM((COUNT, D), F32),
        pltpu.VMEM((BOTH, D), BF16),
        pltpu.VMEM((BOTH, D), BF16),
        pltpu.VMEM((BOTH, 512), BF16),
        pltpu.VMEM((BOTH, D), F32),
        pltpu.VMEM((COUNT, D), F32),
        pltpu.VMEM((COUNT, D), F32),
    ]
    for spec in SUMMED:
        scratch.append(pltpu.VMEM(total_shape(spec), F32 if spec[0] == "small" else BF16))
    for spec in SUMMED:
        scratch += landing_shapes(spec)
    count = 1 + 4 * LAYERS
    scratch += [
        pltpu.SemaphoreType.DMA((count, SLOTS)),
        pltpu.SemaphoreType.DMA((count, SLOTS)),
        pltpu.SemaphoreType.DMA((count, SUM_SLOTS)),
        pltpu.SemaphoreType.DMA((count, SUM_SLOTS)),
        pltpu.SemaphoreType.REGULAR((4, 12)),
        pltpu.SemaphoreType.DMA((8,)),
        pltpu.SemaphoreType.DMA((8,)),
        pltpu.SemaphoreType.DMA((40,)),
    ]
    found = pl.pallas_call(
        functools.partial(blocks_kernel, [(STEP_NAMES[step // 2], step % 2) for step in SCHEDULE]),
        out_shape=outs,
        in_specs=[vmem, hbm] + [vmem] * 6 + [hbm] * 4,
        out_specs=[hbm] * in_hbm + [vmem],
        scratch_shapes=scratch,
        name="blocks",
        compiler_params=pltpu.CompilerParams(
            collective_id=0, has_side_effects=True, vmem_limit_bytes=63 * 2**20
        ),
    )(tokens, out_grad, b_qkv, b_up, ln_gain, ln_bias, out_bias, tables, *owned_weights)
    return found[:6] + found[in_hbm:]


def hand_over_kernel(*refs):
    sources, small, targets, parts = refs[:6], refs[6], refs[7:13], refs[13:18]
    held, (read, written) = refs[18:24], refs[24:]
    copies_in, copies_out = [
        [
            pltpu.make_async_copy(source, target, done.at[number])
            for number, (source, target) in enumerate(zip(left, right))
        ]
        for left, right, done in ((sources, held, read), (held, targets, written))
    ]
    for copy in copies_in:
        copy.start()
    for layer_at in range(LAYERS):
        for (row, size, factor, shift), target in zip(KINDS.values(), parts):
            at_row = 5 * layer_at + row
            target[layer_at : layer_at + 1, :] = small[at_row : at_row + 1, :size]
    for copy, onward in zip(copies_in, copies_out):
        copy.wait()
        onward.start()
    for copy in copies_out:
        copy.wait()


def hand_over(found):
    vmem, hbm = pl.BlockSpec(memory_space=pltpu.VMEM), pl.BlockSpec(memory_space=pltpu.HBM)
    shape = jax.ShapeDtypeStruct
    return pl.pallas_call(
        hand_over_kernel,
        out_shape=[shape(item.shape, item.dtype) for item in found[:6]]
        + [shape((LAYERS, size), F32) for row, size, factor, shift in KINDS.values()],
        in_specs=[hbm] * 6 + [vmem],
        out_specs=[hbm] * 6 + [vmem] * 5,
        scratch_shapes=[pltpu.VMEM(item.shape, item.dtype) for item in found[:6]]
        + [pltpu.SemaphoreType.DMA((6,))] * 2,
        name="hand_over",
    )(*found)


def on_device(
    tokens, w_qkv, b_qkv, w_out, w_up, b_up, w_down, ln_gain, ln_bias, out_bias, out_grad
):
    tables = jnp.asarray(turn_tables())
    found = blocks_call(
        tokens, out_grad, b_qkv, b_up, ln_gain, ln_bias, out_bias, tables, w_qkv, w_up, w_out, w_down
    )
    result, in_grad, g_qkv, g_up, g_out, g_down, *small = hand_over(found)
    g_b_qkv, g_b_up, g_gain, g_shift, g_out_bias = small
    return (
        result,
        in_grad,
        g_qkv,
        g_b_qkv,
        g_out,
        g_up,
        g_b_up,
        g_down,
        g_gain,
        g_shift,
        g_out_bias,
    )


def solution(mesh):
    placed = (
        P(("rep", "shard"), None),
        P(None, "shard", None),
        P(None, "shard"),
        P(None, "shard", None),
        P(None, "shard", None),
        P(None, "shard"),
        P(None, "shard", None),
        P(None, "shard"),
        P(None, "shard"),
        P(None, "shard"),
        P(("rep", "shard"), None),
    )
    return jax.shard_map(
        on_device,
        mesh=mesh,
        in_specs=placed,
        out_specs=(
            P(("rep", "shard"), None),
            P(("rep", "shard"), None),
            P(None, "shard", None),
            P(None, "shard"),
            P(None, "shard", None),
            P(None, "shard", None),
            P(None, "shard"),
            P(None, "shard", None),
            P(None, "shard"),
            P(None, "shard"),
            P(None, "shard"),
        ),
        check_vma=False,
    )
```

```python
import functools
import math

import jax
import jax.numpy as jnp
import numpy as np
from jax import lax
from jax.experimental import pallas as pl
from jax.experimental.pallas import tpu as pltpu
from jax.sharding import PartitionSpec as P


STEP_NAMES = (
    "s", "q", "u", "o", "d", "Q", "R", "U", "V", "O", "D", "E", "S", "vec", "fnorm", "joined",
    "fattn", "up", "down", "res", "start", "low", "gdown", "slope", "gup", "dmixed", "gout",
    "battnA", "battnB", "dhidden", "gqkv", "norm", "pack",
)
(
    s0, s1, q0, q1, u0, u1, o0, o1, d0, d1, Q0, Q1, R0, R1, U0, U1, V0, V1, O0, O1, D0, D1, E0,
    E1, S0, S1, vec0, vec1, fnorm0, fnorm1, joined0, joined1, fattn0, fattn1, up0, up1, down0,
    down1, res0, res1, start0, start1, low0, low1, gdown0, gdown1, slope0, slope1, gup0, gup1,
    dmixed0, dmixed1, gout0, gout1, battnA0, battnA1, battnB0, battnB1, dhidden0, dhidden1, gqkv0,
    gqkv1, norm0, norm1, pack0, pack1,
) = range(2 * len(STEP_NAMES))
SCHEDULE = (
    o1, s0, q0, q1, o1, o0, u0, s0, q0, s0, d0, q1, o0, q0, s0, d1, u0, o0, q0, u1, o1, u0, o0,
    u0, d0, q0, q1, o0, s0, d0, d0, u0, s0, s0, vec0, q0, d0, q1, fnorm0, u0, o1, u1, q0, o0,
    joined0, d0, u1, d1, q1, fattn0, u1, u0, o0, d0, up0, q1, down0, d1, o1, u1, res0, q1, fnorm1,
    d1, o1, joined1, u1, start1, fattn1, low1, gout1, o1, O1, u1, O1, dmixed1, d1, up1, gdown1,
    d1, D1, D1, E1, O1, battnA1, battnB1, d1, D1, gqkv1, Q1, Q1, O1, slope1, gup1, V1, O1, D1, E1,
    Q1, down1, U1, U1, E1, D1, R1, res1, dhidden1, V1, U1, norm1, start0, E1, V1, Q1, O1, low0,
    gdown0, E0, D0, R1, gout0, D0, slope0, E1, U1, R1, V1, O0, O0, gup0, U0, U0, D1, U1, D0,
    dmixed0, R1, V0, E0, battnA0, O0, D1, Q1, battnB0, U0, U1, gqkv0, E1, Q1, D1, D0, R0,
    dhidden0, V0, E1, V1, E0, Q0, D0, pack1, E1, U1, Q1, U1, U0, Q0, O1, V1, norm0, R1, O1, V0,
    O0, U0, D0, E0, R1, V1, O0, Q1, V1, R0, Q0, pack0, O0, S0, D0, S0, U0, R0, R1, V0, Q0, S0, O0,
    U0, R1, V0, E0, R0, D0, Q0, S0, V0, E0, R0, Q0, O0, S0, R0, V0, S0, Q0, E0, R0, V0, Q0, S0,
    S0, R0, E0, U0,
)


MESH = pl.DeviceIdType.MESH
LANE = 128
LAYERS = 2


def place():
    xl = lax.axis_index("rep")
    s = lax.axis_index("shard")
    return xl, s // 32, (s // 8) % 4, (s // 2) % 4, s % 2


def at(xl, xh, z, y, c):
    return (xl, xh * 32 + z * 8 + y * 2 + c)


def around(value, step):
    return lax.rem(value + (step + 4), 4)


def greet(others):
    barrier = pltpu.get_barrier_semaphore()
    for other in others:
        pl.semaphore_signal(barrier, inc=1, device_id=other, device_id_type=MESH)
    return len(others)


def await_greetings(count):
    pl.semaphore_wait(pltpu.get_barrier_semaphore(), count)


SMALL_GATHERED = ("small", True, 32, 128, 0, 1)
GATHERED = (
    (
        ("qkv", True, 32, 1536, 4, 8),
        ("up", True, 32, 2048, 6, 10),
        ("out", False, 32, 1024, 3, 5),
        ("down", False, 128, 1024, 3, 5),
    ),
    (
        ("qkv", True, 32, 1536, 4, 8),
        ("up", True, 32, 2048, 4, 12),
        ("out", False, 32, 1024, 2, 6),
        ("down", False, 128, 1024, 2, 6),
    ),
)
SLOTS = 18


class Stream:
    def __init__(self, number, spec, source, target, send, recv, xl, xh, z, y, core):
        self.name, self.by_columns, self.rows, self.columns, self.swapped, self.width = spec
        self.number = number
        self.source = source
        self.target = target
        self.send, self.recv = send, recv
        self.xl, self.xh, self.z, self.y, self.core = xl, xh, z, y, core
        self.half = self.rows // 2
        self.wide = pl.ds(pl.multiple_of(xl * (self.swapped * LANE), LANE), self.width * LANE)
        self.mine = pl.ds(
            pl.multiple_of(xl * ((self.width - self.swapped) * LANE) + xl * (self.swapped * LANE), LANE),
            max(self.swapped, 1) * LANE,
        )
        self.theirs = pl.ds(
            pl.multiple_of((1 - xl) * (self.width * LANE), LANE), max(self.swapped, 1) * LANE
        )
        self.across = lambda core_of: at(1 - xl, 1 - xh, z, y, core_of)
        self.partner = at(1 - xl, xh, z, y, core) if core == 0 else self.across(core)
        if core == 0:
            self.first, self.second = y, z
        else:
            self.first, self.second = z, y
        self.sent = []

    def neighbour(self, ring, step):
        z, y = self.z, self.y
        if (ring == 0) == (self.core == 0):
            y = around(y, step)
        else:
            z = around(z, step)
        return at(self.xl, self.xh, z, y, self.core)

    def block(self, first, rows, columns):
        if self.core == 0:
            return self.target.at[:, self.second, first, rows, columns]
        return self.target.at[:, first, self.second, rows, columns]

    def line(self, second, rows, columns):
        if self.core == 0:
            return self.target.at[:, second, :, rows, columns]
        return self.target.at[:, :, second, rows, columns]

    def push(self, region, slot, device):
        copy = pltpu.make_async_remote_copy(
            region(),
            region(),
            self.send.at[self.number, slot],
            self.recv.at[self.number, slot],
            device_id=device,
            device_id_type=MESH,
        )
        copy.start()
        self.sent.append((region, slot))

    def arrived(self, region, slot):
        pltpu.make_async_copy(region, region, self.recv.at[self.number, slot]).wait()

    def part(self, core_of):
        return pl.ds(core_of * self.half, self.half)

    def stage0(self):
        xh, z, y, core = self.xh, self.z, self.y, self.core
        whole = slice(None)
        if self.by_columns:
            region = lambda: self.target.at[xh, z, y, self.part(core), :]
            here = region()
            landed = self.recv.at[self.number, xh * 2 + core]
            for source, columns in self.source(core):
                pltpu.make_async_copy(source, here.at[:, columns], landed).start()
            for slot, half, device in (
                (0, 1 - core, at(self.xl, xh, z, y, 1 - core)),
                (1, core, self.across(core)),
                (2, 1 - core, self.across(1 - core)),
            ):
                for source, columns in self.source(half):
                    pltpu.make_async_remote_copy(
                        source,
                        here.at[:, columns],
                        self.send.at[self.number, slot],
                        landed,
                        device_id=device,
                        device_id_type=MESH,
                    ).start()
                self.sent.append((region, slot))
        else:
            here = self.target.at[0, z, y, self.part(core), :]
            mine = self.source(0)

            @pl.when(xh == core)
            def _():
                pltpu.make_async_copy(mine, here, self.recv.at[self.number, core]).start()

            @pl.when(xh != core)
            def _():
                pltpu.make_async_remote_copy(
                    mine,
                    here,
                    self.send.at[self.number, 0],
                    self.recv.at[self.number, core],
                    device_id=at(self.xl, xh, z, y, 1 - core),
                    device_id_type=MESH,
                ).start()

            pltpu.make_async_remote_copy(
                mine,
                here,
                self.send.at[self.number, 1],
                self.recv.at[self.number, core],
                device_id=self.across(xh),
                device_id_type=MESH,
            ).start()
            self.sent.append((lambda: self.source(0), 1))

    def stage1(self):
        whole = slice(None)
        for bank in range(2 if self.by_columns else 1):
            for core_of in range(2):
                self.arrived(
                    self.target.at[bank, self.z, self.y, self.part(core_of), :], bank * 2 + core_of
                )
        own = lambda: self.block(self.first, whole, self.wide)
        self.push(own, 4, self.neighbour(0, 1))
        self.push(own, 5, self.neighbour(0, -1))

    def share(self, region, slot):
        if self.swapped:
            self.push(lambda: region(self.mine), slot, self.partner)

    def stage2(self):
        whole = slice(None)
        for step, slot in ((-1, 4), (1, 5)):
            found = lambda rows, columns, step=step: self.block(
                around(self.first, step), rows, columns
            )
            self.arrived(found(whole, self.wide), slot)
            self.push(
                lambda found=found, slot=slot: found(self.part(slot - 4), self.wide),
                slot + 2,
                self.neighbour(0, -step),
            )
            self.share(lambda columns, found=found: found(whole, columns), slot + 8)

    def stage3(self):
        whole = slice(None)
        far = lambda rows, columns: self.block(around(self.first, 2), rows, columns)
        for half in range(2):
            self.arrived(far(self.part(half), self.wide), 6 + half)
        own = lambda: self.line(self.second, whole, self.wide)
        self.push(own, 8, self.neighbour(1, 1))
        self.push(own, 9, self.neighbour(1, -1))
        self.share(lambda columns: far(whole, columns), 14)

    def stage4(self):
        whole = slice(None)
        for step, slot in ((-1, 8), (1, 9)):
            found = lambda rows, columns, step=step: self.line(
                around(self.second, step), rows, columns
            )
            self.arrived(found(whole, self.wide), slot)
            self.push(
                lambda found=found, slot=slot: found(self.part(slot - 8), self.wide),
                slot + 2,
                self.neighbour(1, -step),
            )
            self.share(lambda columns, found=found: found(whole, columns), slot + 7)

    def stage5(self):
        whole = slice(None)
        far = lambda rows, columns: self.line(around(self.second, 2), rows, columns)
        for half in range(2):
            self.arrived(far(self.part(half), self.wide), 10 + half)
        self.share(lambda columns: far(whole, columns), 17)

    def stage6(self):
        whole = slice(None)
        if self.swapped:
            for step, slot in ((-1, 12), (1, 13), (2, 14)):
                self.arrived(self.block(around(self.first, step), whole, self.theirs), slot)
            for step, slot in ((-1, 15), (1, 16), (2, 17)):
                self.arrived(self.line(around(self.second, step), whole, self.theirs), slot)

    def finish(self):
        for region, slot in self.sent:
            pltpu.make_async_copy(region(), region(), self.send.at[self.number, slot]).wait()
        self.sent = []
        if not self.by_columns:

            @pl.when(self.xh != self.core)
            def _():
                mine = self.source(0)
                pltpu.make_async_copy(mine, mine, self.send.at[self.number, 0]).wait()


def owned_pieces(name, owned, layer_at):
    if name == "small":
        return lambda half: [(owned, slice(None))]
    if name == "qkv":
        return lambda half: [
            (
                owned.at[layer_at, :, pl.ds(third * 1024 + half * 512, 512)],
                pl.ds(third * 512, 512),
            )
            for third in range(3)
        ]
    if name == "up":
        return lambda half: [(owned.at[layer_at, :, pl.ds(half * 2048, 2048)], slice(None))]
    return lambda half: owned.at[layer_at]


def neighbours():
    xl, xh, z, y, c = place()
    return [
        at(xl, xh, z, y, 1 - c),
        at(1 - xl, 1 - xh, z, y, c),
        at(1 - xl, 1 - xh, z, y, 1 - c),
        at(xl, 1 - xh, z, y, c),
        at(1 - xl, xh, z, y, c),
        at(xl, xh, around(z, 1), y, c),
        at(xl, xh, around(z, -1), y, c),
        at(xl, xh, z, around(y, 1), c),
        at(xl, xh, z, around(y, -1), c),
    ]


COUNT = 256
BOTH = 512
D = 1024
HEAD_DIM = 64
ROT = 16
EPS = 1e-05
FILL = -1e30
F32 = jnp.float32
BF16 = jnp.bfloat16
TILE = 256
WIDE = 512


def turn_tables():
    places = np.arange(COUNT, dtype=np.float32)
    rates = np.float32(10000.0) ** (-np.arange(0, ROT, 2, dtype=np.float32) / np.float32(ROT))
    angles = places[:, None] * rates[None, :]
    cosine, sine = np.cos(angles), np.sin(angles)
    half = ROT // 2
    keep = np.ones((COUNT, HEAD_DIM), np.float32)
    ahead = np.zeros((COUNT, HEAD_DIM), np.float32)
    behind = np.zeros((COUNT, HEAD_DIM), np.float32)
    keep[:, :half] = cosine
    keep[:, half:ROT] = cosine
    ahead[:, :half] = -sine
    behind[:, half:ROT] = sine
    return np.stack([np.concatenate([t, t], 1) for t in (keep, ahead, behind)])


def turn(values, tables, sign):
    return values * tables[0] + sign * (
        pltpu.roll(values, LANE - ROT // 2, 1) * tables[1]
        + pltpu.roll(values, ROT // 2, 1) * tables[2]
    )


def dot(left, right):
    return jnp.dot(left, right, preferred_element_type=F32)


def dot_nt(left, right):
    return lax.dot_general(left, right, (((1,), (1,)), ((), ())), preferred_element_type=F32)


def dot_tn(left, right):
    return lax.dot_general(left, right, (((0,), (0,)), ((), ())), preferred_element_type=F32)


def columns_of(index, width=TILE):
    return pl.ds(pl.multiple_of(index * width, width), width)


def loop(count, body):
    def step(index, carry):
        body(index)
        return carry

    lax.fori_loop(0, count, step, 0)


KINDS = {
    "b_qkv": (0, 48, 43691, 21),
    "b_up": (1, 64, 1, 6),
    "gain": (2, 16, 1, 4),
    "shift": (3, 16, 1, 4),
    "out_bias": (4, 16, 1, 4),
}
OWNED_ROWS = 16
CHUNK = 512


def chunks_of(kind, core):
    if kind == "b_qkv":
        return [(t * CHUNK, t * 1024 + core * CHUNK) for t in range(3)]
    if kind == "b_up":
        return [(t * CHUNK, core * 2048 + t * CHUNK) for t in range(4)]
    return [(t * CHUNK, t * CHUNK) for t in range(2)]


def owner_masks(kind, start):
    row, size, factor, shift = KINDS[kind]
    place_of = lax.broadcasted_iota(jnp.int32, (LANE, CHUNK), 1) + start
    owner = lax.shift_right_logical(place_of * factor, shift)
    within = place_of - owner * size
    spread = lax.broadcasted_iota(jnp.int32, (LANE, CHUNK), 0) == within
    owned = lax.broadcasted_iota(jnp.int32, (64, CHUNK), 0) == owner[:64]
    return spread, owned


def unpack_vector(rows_ref, layer_at, kind, core, target):
    row = KINDS[kind][0] + 5 * layer_at
    held = rows_ref[pl.ds(row, 64, stride=OWNED_ROWS), :].astype(BF16)
    for place_at, start in chunks_of(kind, core):
        spread, owned = owner_masks(kind, start)
        every = dot(held, jnp.where(spread, 1.0, 0.0).astype(BF16))
        target[:, pl.ds(place_at, CHUNK)] = jnp.sum(
            jnp.where(owned, every, 0.0), 0, keepdims=True
        )


def pack_vector(rows_ref, layer_at, kind, core, vector):
    total = jnp.zeros((64, LANE), F32)
    for place_at, start in chunks_of(kind, core):
        spread, owned = owner_masks(kind, start)
        mine = jnp.where(owned, vector[:, pl.ds(place_at, CHUNK)], 0.0)
        spread = jnp.where(spread, 1.0, 0.0).astype(BF16)
        high = mine.astype(BF16)
        total = total + dot_nt(high, spread)
        total = total + dot_nt((mine - high.astype(F32)).astype(BF16), spread)
    rows_ref[pl.ds(KINDS[kind][0] + 5 * layer_at, 64, stride=OWNED_ROWS), :] = total


def centre(values):
    centred = values - jnp.mean(values, -1, keepdims=True)
    inv_std = lax.rsqrt(jnp.mean(centred * centred, -1, keepdims=True) + EPS)
    return centred * inv_std, inv_std


def norm_piece(x_ref, gain, shift, hidden):
    def body(index):
        rows = columns_of(index, 64)
        normed, unused = centre(x_ref[rows, :].astype(F32))
        hidden[rows, :] = (normed * gain[...] + shift[...]).astype(BF16)

    loop(COUNT // 64, body)


def joined_piece(third, hidden, w_qkv, b_qkv, tables, target):
    columns = pl.ds(third * 512, 512)
    found = dot(hidden[...], w_qkv(columns)) + b_qkv[:, columns]
    for sequence in range(2):
        for pair in range(4):
            part = found[sequence * COUNT : (sequence + 1) * COUNT, pair * LANE : (pair + 1) * LANE]
            if third < 2:
                part = turn(part, tables, 1.0)
            if third == 0:
                part = part * HEAD_DIM**-0.5
            target[
                pl.ds(sequence * COUNT, COUNT), pl.ds(pair * LANE + third * 512, LANE)
            ] = part.astype(BF16)


def first_head():
    return lax.broadcasted_iota(jnp.int32, (COUNT, LANE), 1) < HEAD_DIM


def only_head(values, half):
    keep = first_head() if half == 0 else jnp.logical_not(first_head())
    return jnp.where(keep, values, jnp.zeros_like(values))


def pair_of_heads(turned, index):
    sequence, pair = index // 4, index % 4
    rows, columns = columns_of(sequence, COUNT), columns_of(pair, LANE)
    return rows, columns, *(turned[rows, columns_of(pair + third * 4, LANE)] for third in range(3))


def attention_piece(turned, probs, mixed):
    def one(index):
        rows, columns, q2, k2, v2 = pair_of_heads(turned, index)
        causal = lax.broadcasted_iota(jnp.int32, (COUNT, COUNT), 0) <= lax.broadcasted_iota(
            jnp.int32, (COUNT, COUNT), 1
        )
        out = []
        for half in range(2):
            scores = jnp.where(causal, dot_nt(k2, only_head(q2, half)), FILL)
            expo = jnp.exp(scores - jnp.max(scores, 0, keepdims=True))
            prob = (expo * (1.0 / jnp.sum(expo, 0, keepdims=True))).astype(BF16)
            probs[index * 2 + half] = prob
            out.append(dot_tn(prob, v2))
        mixed[rows, columns] = jnp.where(first_head(), out[0], out[1]).astype(BF16)

    def body(index):
        for pair in range(4):
            one(index * 4 + pair)

    loop(2, body)


def up_piece(hidden, w_up, b_up, active, slope):
    def body(index):
        columns = columns_of(index, WIDE)
        upward = dot(hidden[...], w_up(columns)) + b_up[:, columns]
        spread = 0.5 + 0.5 * lax.erf(upward * (0.5**0.5))
        active[:, columns] = (upward * spread).astype(BF16)
        dense = jnp.exp(upward * upward * -0.5) * (1.0 / math.sqrt(2.0 * math.pi))
        slope[:, columns] = (spread + upward * dense).astype(BF16)

    loop(2048 // WIDE, body)


def down_piece(active, w_down, mixed, w_out, partial):
    def body(index):
        columns = columns_of(index, WIDE)
        partial[:, columns] = dot(mixed[...], w_out(columns)) + dot(active[...], w_down(columns))

    loop(D // WIDE, body)


def residual_piece(x_ref, partial, received, out_bias, target):
    def body(index):
        rows = columns_of(index, 64)
        target[rows, :] = (
            x_ref[rows, :].astype(F32)
            + (partial[rows, :] + received[rows, :])
            + out_bias[...]
        ).astype(target.dtype)

    loop(COUNT // 64, body)


def start_piece(dy, dy_low, out_bias_grad):
    def body(index):
        rows = columns_of(index, 64)
        values = dy[rows, :].astype(F32)
        dy_low[rows, :] = values.astype(BF16)
        out_bias_grad[...] += jnp.sum(values, 0, keepdims=True)

    out_bias_grad[...] = jnp.zeros_like(out_bias_grad)
    loop(COUNT // 64, body)


def flip_piece(source, target):
    rows, columns = source.shape
    for at_row in range(rows // TILE):

        def body(index, at_row=at_row):
            target[columns_of(index), pl.ds(at_row * TILE, TILE)] = source[
                pl.ds(at_row * TILE, TILE), columns_of(index)
            ].T

        loop(columns // TILE, body)


def rows_grad_piece(size, left, right, store):
    def body(index):
        store(index, dot_tn(left[:, columns_of(index, size)], right[...]).astype(BF16))

    loop(left.shape[1] // size, body)


def columns_grad_piece(size, left_flipped, right, store):
    def body(index):
        store(index, dot(left_flipped[...], right[:, columns_of(index, size)]).astype(BF16))

    loop(right.shape[1] // size, body)


def slope_piece(dy_low, w_down_rows, slope, d_up, b_up_grad):
    def body(index):
        columns = columns_of(index, D)
        found = (dot_nt(dy_low[...], w_down_rows(index)) * slope[:, columns].astype(F32)).astype(BF16)
        d_up[:, columns] = found
        b_up_grad[:, columns] = jnp.sum(found.astype(F32), 0, keepdims=True)

    loop(2048 // D, body)


def d_mixed_piece(dy_low, w_out_rows, d_mixed):
    d_mixed[...] = dot_nt(dy_low[...], w_out_rows(0)).astype(BF16)


def attention_back_piece(turned, probs, d_mixed, tables, d_joined, b_qkv_grad, sequence):
    if sequence == 0:
        b_qkv_grad[...] = jnp.zeros_like(b_qkv_grad)
    for index in range(sequence * 4, sequence * 4 + 4):
        rows, columns, q2, k2, v2 = pair_of_heads(turned, index)
        dm2 = d_mixed[rows, columns]
        both_probs = [probs[index * 2 + half] for half in range(2)]
        d_scores = []
        for half, prob in enumerate(both_probs):
            full = prob.astype(F32)
            d_probs = dot_nt(v2, only_head(dm2, half))
            d_scores.append(
                (full * (d_probs - jnp.sum(d_probs * full, 0, keepdims=True))).astype(BF16)
            )
        apart = lambda values: jnp.concatenate([only_head(values, 0), only_head(values, 1)], 0)
        parts = (
            dot_tn(jnp.concatenate(d_scores, 0), apart(k2)) * HEAD_DIM**-0.5,
            dot(jnp.concatenate(d_scores, 1), apart(q2)),
            dot(jnp.concatenate(both_probs, 1), apart(dm2)),
        )
        for third, part in enumerate(parts):
            if third < 2:
                part = turn(part, tables, -1.0)
            part = part.astype(BF16)
            there = columns_of(index % 4 + third * 4, LANE)
            d_joined[rows, there] = part
            b_qkv_grad[:, there] += jnp.sum(part.astype(F32), 0, keepdims=True)


def d_hidden_piece(d_joined, w_qkv_rows, d_up, w_up_rows, d_hidden):
    d_hidden[...] = dot_nt(d_joined[...], w_qkv_rows(0)) + dot_nt(d_up[...], w_up_rows(0))


def norm_back_piece(x_ref, gain, dy, d_hidden, received, target, gain_grad, shift_grad):
    gain_grad[...] = jnp.zeros_like(gain_grad)
    shift_grad[...] = jnp.zeros_like(shift_grad)

    def body(index):
        rows = columns_of(index, 64)
        normed, inv_std = centre(x_ref[rows, :].astype(F32))
        total = d_hidden[rows, :] + received[rows, :]
        gain_grad[...] += jnp.sum(total * normed, 0, keepdims=True)
        shift_grad[...] += jnp.sum(total, 0, keepdims=True)
        scaled = total * gain[...]
        target[rows, :] = dy[rows, :].astype(F32) + inv_std * (
            scaled
            - jnp.mean(scaled, -1, keepdims=True)
            - normed * jnp.mean(scaled * normed, -1, keepdims=True)
        )

    loop(COUNT // 64, body)


SUMMED = (
    (0, True, 32, 0, 768, 0, 6),
    (0, True, 32, 768, 768, 3, 3),
    (1, True, 32, 0, 1024, 0, 8),
    (1, True, 32, 1024, 1024, 4, 4),
    (2, False, 32, 0, 1024, 0, 8),
    (3, False, 128, 0, 512, 0, 4),
    (3, False, 128, 512, 512, 2, 2),
    (4, True, 32, 0, 128, 0, 1),
)
SMALL_SUM = 7
QKV, UP, OUT, DOWN, SMALL = range(5)
SUM_SLOTS = 18
BUFFERS = 9


def landing_shapes(spec):
    gradient, by_columns, rows, base, columns, swapped, width = spec
    banks = 2 if by_columns else 1
    kind = F32 if gradient == SMALL else BF16
    wide = width * LANE
    return [
        pltpu.VMEM((banks, 4, 4, rows, swapped * LANE) if swapped else (8, LANE), kind),
        pltpu.VMEM((2, banks, 4, rows // 2, wide), kind),
        pltpu.VMEM((2, banks, 4, rows, wide), kind),
        pltpu.VMEM((banks, 4, rows, wide), kind),
        pltpu.VMEM((2, banks, rows // 2, wide), kind),
        pltpu.VMEM((2, banks, rows, wide), kind),
        pltpu.VMEM((3, rows, wide), kind),
        pltpu.VMEM((rows, columns), F32),
        pltpu.VMEM((2, 16 if gradient == SMALL else 1, LANE), F32),
    ]


def add_into(target, first, *others):
    if len(others) == 1:
        target[...] = first[...] + others[0][...]
    else:
        found = first[...].astype(F32)
        for other in others:
            found = found + other[...].astype(F32)
        target[...] = found.astype(target.dtype)


sum_loop = loop


class Sum:
    def __init__(self, number, which, before, total, landing, output, send, recv, free, where, core):
        spec = SUMMED[which]
        self.gradient, self.by_columns, self.rows, base, self.columns, self.swapped, self.width = spec
        self.base = base
        self.number, self.which = number, which
        self.before = before
        self.after = not before and self.gradient != SMALL
        self.total, self.output = total, output
        (
            self.swap,
            self.far_line,
            self.near_line,
            self.line,
            self.far_block,
            self.near_block,
            self.last,
            self.ready,
            self.tail,
        ) = landing
        self.send, self.recv, self.free = send, recv, free
        self.xl, self.xh, self.z, self.y = where
        self.core = core
        self.banks = 2 if self.by_columns else 1
        self.half = self.rows // 2
        s, w = self.swapped, self.width
        xl, xh, z, y = where
        self.wide = pl.ds(pl.multiple_of(base + xl * (s * LANE), LANE), w * LANE)
        self.mine = pl.ds(pl.multiple_of(base + xl * (w * LANE), LANE), max(s, 1) * LANE)
        self.theirs = pl.ds(pl.multiple_of(base + (1 - xl) * (w * LANE), LANE), max(s, 1) * LANE)
        self.wide_here = pl.ds(pl.multiple_of(xl * (s * LANE), LANE), w * LANE)
        self.theirs_here = pl.ds(pl.multiple_of((1 - xl) * (w * LANE), LANE), max(s, 1) * LANE)
        self.beside = at(1 - xl, xh, z, y, core)
        self.across = at(1 - xl, 1 - xh, z, y, core)
        self.beyond = at(xl, 1 - xh, z, y, core)
        self.sibling = at(xl, xh, z, y, 1 - core)
        self.partner = self.beside if core == 0 else self.across
        self.first, self.second = (y, z) if core == 0 else (z, y)
        self.sent = []

    def neighbour(self, ring, step):
        z, y = self.z, self.y
        if (ring == 0) == (self.core == 0):
            y = around(y, step)
        else:
            z = around(z, step)
        return at(self.xl, self.xh, z, y, self.core)

    def total_line(self, second, rows, columns):
        if self.core == 0:
            return self.total.at[:, second, :, rows, columns]
        return self.total.at[:, :, second, rows, columns]

    def push(self, source, target, slot, device, keep=True):
        if self.before and slot < 12:
            pl.semaphore_wait(self.free.at[self.which, slot], 1)
        pltpu.make_async_remote_copy(
            source(),
            target,
            self.send.at[self.number, slot],
            self.recv.at[self.number, slot],
            device_id=device,
            device_id_type=MESH,
        ).start()
        if keep:
            self.sent.append((source, slot))

    def release(self, slot, device):
        if self.after:
            pl.semaphore_signal(
                self.free.at[self.which, slot], inc=1, device_id=device, device_id_type=MESH
            )

    def arrived(self, region, slot):
        pltpu.make_async_copy(region, region, self.recv.at[self.number, slot]).wait()

    def settle(self):
        for source, slot in self.sent:
            pltpu.make_async_copy(source(), source(), self.send.at[self.number, slot]).wait()
        self.sent = []

    def part(self, core_of):
        return pl.ds(core_of * self.half, self.half)

    def stage1(self):
        if self.swapped:
            self.push(
                lambda: self.total.at[:, :, :, :, self.theirs], self.swap, 0, self.partner
            )

    def stage2(self):
        if self.swapped:
            self.arrived(self.swap, 0)

            def add(step):
                bank, z = step // 4, step % 4
                region = self.total.at[bank, z, :, :, self.mine]
                add_into(region, region, self.swap.at[bank, z])

            sum_loop(self.banks * 4, add)
            self.release(0, self.partner)
        for half in range(2):
            self.push(
                lambda half=half: self.total_line(
                    around(self.second, 2), self.part(half), self.wide
                ),
                self.far_line.at[half],
                1 + half,
                self.neighbour(1, 1 - 2 * half),
            )

    def stage3(self):
        for half in range(2):
            self.arrived(self.far_line.at[half], 1 + half)
            toward = 1 - 2 * half
            rows = self.part(half)

            def add(step):
                bank, place_at = step // 4, step % 4
                region = self.total_line(around(self.second, toward), rows, self.wide).at[
                    bank, place_at
                ]
                add_into(region, region, self.far_line.at[half, bank, place_at])

            sum_loop(self.banks * 4, add)
            self.release(1 + half, self.neighbour(1, -toward))
            self.push(
                lambda toward=toward: self.total_line(
                    around(self.second, toward), slice(None), self.wide
                ),
                self.near_line.at[half],
                3 + half,
                self.neighbour(1, toward),
            )

    def stage4(self):
        for half in range(2):
            self.arrived(self.near_line.at[half], 3 + half)

        def add(step):
            bank, place_at = step // 4, step % 4
            add_into(
                self.line.at[bank, place_at],
                self.total_line(self.second, slice(None), self.wide).at[bank, place_at],
                self.near_line.at[0, bank, place_at],
                self.near_line.at[1, bank, place_at],
            )

        sum_loop(self.banks * 4, add)
        for half in range(2):
            self.release(3 + half, self.neighbour(1, 2 * half - 1))
        self.settle()
        for half in range(2):
            self.push(
                lambda half=half: self.line.at[:, around(self.first, 2), self.part(half), :],
                self.far_block.at[half],
                5 + half,
                self.neighbour(0, 1 - 2 * half),
            )

    def stage5(self):
        for half in range(2):
            self.arrived(self.far_block.at[half], 5 + half)
            toward = 1 - 2 * half
            for bank in range(self.banks):
                region = self.line.at[bank, around(self.first, toward), self.part(half), :]
                add_into(region, region, self.far_block.at[half, bank])
            self.release(5 + half, self.neighbour(0, -toward))
            self.push(
                lambda toward=toward: self.line.at[:, around(self.first, toward)],
                self.near_block.at[half],
                7 + half,
                self.neighbour(0, toward),
            )

    def own(self, bank):
        return self.line.at[bank, self.first]

    def stage6(self):
        for half in range(2):
            self.arrived(self.near_block.at[half], 7 + half)
        for bank in range(self.banks):
            add_into(
                self.own(bank),
                self.own(bank),
                self.near_block.at[0, bank],
                self.near_block.at[1, bank],
            )
        for half in range(2):
            self.release(7 + half, self.neighbour(0, 2 * half - 1))
        if self.by_columns:
            self.push(lambda: self.own(self.xh), self.last.at[0], 9, self.beside)
            self.push(lambda: self.own(1 - self.xh), self.last.at[1], 10, self.across)
            self.push(lambda: self.own(1 - self.xh), self.last.at[2], 11, self.beyond)
        else:

            @pl.when(self.xh == self.core)
            def _():
                self.push(lambda: self.own(0), self.last.at[0], 9, self.beside, False)

            @pl.when(self.xh != self.core)
            def _():
                self.push(lambda: self.own(0), self.last.at[1], 10, self.across, False)
                self.push(lambda: self.own(0), self.last.at[2], 11, self.beyond, False)

    def add_last(self):
        for slot in range(3):
            self.arrived(self.last.at[slot], 9 + slot)
        s, w = self.swapped, self.width
        c = w - s
        own = self.own(self.xh if self.by_columns else 0)
        self.ready[:, self.wide_here] = own[...].astype(F32) + self.last[2].astype(F32)
        if s:
            there = pl.ds(pl.multiple_of((1 - self.xl) * (c * LANE), LANE), s * LANE)
            self.ready[:, self.theirs_here] = self.last[0, :, there].astype(F32) + self.last[
                1, :, there
            ].astype(F32)
        if c:
            middle = pl.ds(s * LANE, c * LANE)
            there = pl.ds(pl.multiple_of(self.xl * (s * LANE), LANE), c * LANE)
            self.ready[:, middle] = (
                self.ready[:, middle]
                + self.last[0, :, there].astype(F32)
                + self.last[1, :, there].astype(F32)
            )
        for slot, device in ((9, self.beside), (10, self.across), (11, self.beyond)):
            self.release(slot, device)

    def pieces(self, core_of):
        rows, base, columns = self.part(core_of), self.base, self.columns
        if self.gradient != QKV:
            first = base + (self.core * 2048 if self.gradient == UP else 0)
            return [(self.ready.at[rows, :], self.output.at[:, pl.ds(first, columns)])]
        found = []
        start = base
        while start < base + columns:
            third, within = start // 512, start % 512
            run = min(512 - within, base + columns - start)
            found.append(
                (
                    self.ready.at[rows, pl.ds(start - base, run)],
                    self.output.at[:, pl.ds(third * 1024 + self.core * 512 + within, run)],
                )
            )
            start += run
        return found

    def deliver(self):
        for index, (source, target) in enumerate(self.pieces(self.core)):
            pltpu.make_async_copy(source, target, self.recv.at[self.number, 15 + index]).start()
        for index, (source, target) in enumerate(self.pieces(1 - self.core)):
            self.push(lambda: source, target, 12 + index, self.sibling, False)

    def delivered(self):
        for index, (source, target) in enumerate(self.pieces(self.core)):
            pltpu.make_async_copy(source, target, self.recv.at[self.number, 15 + index]).wait()
        for index, (source, target) in enumerate(self.pieces(1 - self.core)):
            pltpu.make_async_copy(source, source, self.send.at[self.number, 12 + index]).wait()

    def stage7(self):
        if self.gradient == SMALL:
            self.add_last()
            self.push(
                lambda: self.ready.at[self.part(1 - self.core), :], self.tail.at[0], 12, self.sibling
            )
        elif self.by_columns:
            self.add_last()
            self.deliver()
        else:

            @pl.when(self.xh == self.core)
            def _():
                self.add_last()
                self.deliver()

    def stage8(self):
        core = self.core
        if self.gradient == SMALL:
            self.arrived(self.tail.at[0], 12)
            self.tail[1] = self.ready[self.part(core), :] + self.tail[0]
        elif self.by_columns:
            self.delivered()
            for index, (source, target) in enumerate(self.pieces(1 - core)):
                self.arrived(source, 12 + index)
        else:

            @pl.when(self.xh == core)
            def _():
                self.delivered()

            @pl.when(self.xh != core)
            def _():
                self.arrived(self.output.at[:, pl.ds(self.base, self.columns)], 12)

        self.settle()
        if not self.by_columns:

            @pl.when(self.xh == core)
            def _():
                own = self.own(0)
                pltpu.make_async_copy(own, own, self.send.at[self.number, 9]).wait()

            @pl.when(self.xh != core)
            def _():
                own = self.own(0)
                pltpu.make_async_copy(own, own, self.send.at[self.number, 10]).wait()
                pltpu.make_async_copy(own, own, self.send.at[self.number, 11]).wait()


WEIGHTS = GATHERED[0]
WEIGHT_NAMES = tuple(spec[0] for spec in WEIGHTS)

FLIPPED, TURNED, PROBS, MIXED, ACTIVE = range(5)

KEPT = (
    (FLIPPED, (D, BOTH), BF16),
    (TURNED, (BOTH, 1536), BF16),
    (PROBS, (16, COUNT, COUNT), BF16),
    (MIXED, (BOTH, 512), BF16),
    (ACTIVE, (BOTH, 2048), BF16),
    ("slope", (BOTH, 2048), BF16),
)
KEPT_NAMES = tuple(name for name, dims, kind in KEPT)

TOUCHED = {
    "joined": ("qkv", TURNED, FLIPPED),
    "fattn": (TURNED, PROBS, MIXED),
    "up": ("up", ACTIVE, "slope"),
    "down": ("down", "out", ACTIVE, MIXED),
    "gdown": (ACTIVE,),
    "slope": ("down", "slope"),
    "gup": (FLIPPED, "slope"),
    "dmixed": ("out",),
    "gout": (MIXED,),
    "battnA": (TURNED, PROBS),
    "battnB": (TURNED, PROBS),
    "dhidden": ("qkv", "up", TURNED, "slope"),
    "gqkv": (FLIPPED, TURNED),
}
FORWARD = ("joined", "fattn", "up", "down")
WHOLE_AFTER = {
    TURNED: "joined",
    FLIPPED: "joined",
    PROBS: "fattn",
    MIXED: "fattn",
    ACTIVE: "up",
    "slope": "up",
}
GATHERS = {"s": 0, "q": 1, "u": 2, "o": 3, "d": 4}
SUMS = {"Q": 0, "R": 1, "U": 2, "V": 3, "O": 4, "D": 5, "E": 6, "S": SMALL_SUM}


class Pair:
    def __init__(self, send, recv):
        xl, xh, z, y, c = place()
        self.device = at(xl, xh, z, y, 1 - c)
        self.send, self.recv = send, recv

    def push(self, source, target, slot):
        pltpu.make_async_remote_copy(
            source,
            target,
            self.send.at[slot],
            self.recv.at[slot],
            device_id=self.device,
            device_id_type=MESH,
        ).start()

    def sent(self, source, slot):
        pltpu.make_async_copy(source, source, self.send.at[slot]).wait()

    def arrived(self, target, slot):
        pltpu.make_async_copy(target, target, self.recv.at[slot]).wait()


class Moves:
    def __init__(self, done):
        self.done = done
        self.count = 0
        self.open = []

    def start(self, source, target):
        copy = pltpu.make_async_copy(source, target, self.done.at[self.count])
        self.count += 1
        copy.start()
        self.open.append(copy)
        return copy

    def finish(self, copy):
        if any(other is copy for other in self.open):
            copy.wait()
            self.open = [other for other in self.open if other is not copy]


EARLY, LATE, LAST, GATHER = range(4)


def phase_of(step, layer_at):
    return LATE if layer_at else (EARLY if step in FORWARD else LAST)


def weight_shape(spec):
    name, by_columns, rows, columns, swapped, width = spec
    return (2 if by_columns else 1, 4, 4, rows, columns)


def all_rows(weight, columns):
    found = weight[:, :, :, :, columns]
    return found.reshape(-1, found.shape[-1])


def row_tile(weight, index, size):
    banks, unused, same, rows, columns = weight.shape
    count = size // WIDE
    found = weight[0, pl.ds(index * count, count)] if rows == 128 else weight[pl.ds(index * count, count)]
    return found.reshape(size, columns)


def store_row_tile(total):
    def store(index, found):
        banks, unused, same, rows, columns = total.shape
        if rows == 128:
            count = found.shape[0] // WIDE
            total[0, pl.ds(index * count, count)] = found.reshape(count, 4, 128, columns)
        else:
            total[0] = found.reshape(4, 4, 32, columns)

    return store


def store_column_tile(total):
    def store(index, found):
        width = found.shape[1]
        total[:, :, :, :, columns_of(index, width)] = found.reshape(2, 4, 4, 32, width)

    return store


def blocks_kernel(schedule, b_qkv, b_up, ln_gain, ln_bias, out_bias, *rest):
    rest = list(rest)

    def take(count):
        found = rest[:count]
        del rest[:count]
        return found

    arguments = take(3)
    owned_weights = take(4)
    result, in_grad = take(2)
    large_out = take(4)
    gathered = [take(4) for layer_at in range(LAYERS)]
    spilled = dict(zip(KEPT_NAMES, take(len(KEPT))))
    (small_out,) = take(1)
    held = dict(zip(KEPT_NAMES + WEIGHT_NAMES, take(len(KEPT) + 4)))
    vectors = [dict(zip(KINDS, take(5))) for layer_at in range(LAYERS)]
    grads = [dict(zip(KINDS, take(5))) for layer_at in range(LAYERS)]
    owned, x_late, dy = take(3)
    tokens, out_grad, tables = copies = take(3)
    early, late = take(2)
    d_mixed, partial = take(2)
    (received_one,) = take(1)
    totals = take(5)
    landing = [take(BUFFERS) for spec in SUMMED]
    send, recv, sum_send, sum_recv, free, pair_send, pair_recv, moved = take(8)
    every = totals[SMALL]
    rows = every.reshape(64 * OWNED_ROWS, LANE)
    hidden, dy_low = (early, late), (late, early)
    received = (received_one, dy)
    received_grad = (received_one, received_one)
    inputs = (tokens, x_late)
    upstream = (dy, out_grad)

    greeted = greet(neighbours())
    moves = Moves(moved)
    arriving = [moves.start(source, target) for source, target in zip(arguments, copies)]
    owned[...] = jnp.zeros_like(owned)
    for layer_at in range(LAYERS):
        for row, vector in enumerate((b_qkv, b_up, ln_gain, ln_bias, out_bias)):
            owned[5 * layer_at + row : 5 * layer_at + row + 1, : vector.shape[1]] = vector[
                layer_at : layer_at + 1, :
            ].astype(F32)
    xl, xh, z, y, c = place()
    where = (xl, xh, z, y)
    await_greetings(greeted)
    pair = Pair(pair_send, pair_recv)
    own, other = pl.ds(0, COUNT), pl.ds(COUNT, COUNT)

    streams, sums = {}, {}
    for core in range(2):
        streams[core, 0, 0] = Stream(
            0, SMALL_GATHERED, owned_pieces("small", owned, 0), every, send, recv, *where, core
        )
        number = 0
        for layer_at in range(LAYERS):
            for which in range(4):
                number += 1
                streams[core, layer_at, which + 1] = Stream(
                    number, GATHERED[layer_at][which],
                    owned_pieces(WEIGHT_NAMES[which], owned_weights[which], layer_at),
                    gathered[layer_at][which], send, recv, *where, core,
                )
        number = 0
        for which, spec in enumerate(SUMMED):
            gradient = spec[0]
            for layer_at in range(1 if gradient == SMALL else LAYERS):
                sums[core, layer_at, which] = Sum(
                    number, which, layer_at == 0 and gradient != SMALL, totals[gradient], landing[which],
                    None if gradient == SMALL else large_out[gradient].at[layer_at],
                    sum_send, sum_recv, free, where, core,
                )
                number += 1
    stage_of = {}

    def advance(table, layer_at, which, first):
        key = (id(table), layer_at, which)
        stage = stage_of[key] = stage_of.get(key, first - 1) + 1
        for core in range(2):

            @pl.when(c == core)
            def _():
                getattr(table[core, layer_at, which], f"stage{stage}")()

        return stage

    pending = {}
    for step, layer_at in schedule:
        for name in TOUCHED.get(step, ()):
            turn_of = phase_of(step, layer_at)
            pending[name, turn_of] = pending.get((name, turn_of), 0) + 1
    for name in WEIGHT_NAMES:
        for layer_at in range(LAYERS):
            pending[name, GATHER + layer_at] = 1
    loads, keeps = {}, {}

    def settle_load(name):
        if name in WEIGHT_NAMES:
            which = WEIGHT_NAMES.index(name)
            if not pending[name, GATHER] and (name, 0) not in loads:
                loads[name, 0] = moves.start(gathered[0][which], held[name])
            if not pending[name, GATHER + 1] and not pending[name, EARLY] and (name, 1) not in loads:
                loads[name, 1] = moves.start(gathered[1][which], held[name])
            source = gathered[0][which]
        else:
            source = spilled[name]
        if not pending[name, EARLY] and not pending[name, LATE] and (name, 2) not in loads:
            loads[name, 2] = moves.start(source, held[name])

    def before(step, layer_at):
        for name in TOUCHED.get(step, ()):
            if name in WEIGHT_NAMES:
                moves.finish(loads[name, phase_of(step, layer_at)])
            elif layer_at == 0 and step not in FORWARD:
                moves.finish(loads[name, 2])
            elif layer_at == 1 and step in FORWARD:
                moves.finish(keeps[name])

    def after(step, layer_at):
        for name in TOUCHED.get(step, ()):
            if layer_at == 0 and WHOLE_AFTER.get(name) == step:
                keeps[name] = moves.start(held[name], spilled[name])
            pending[name, phase_of(step, layer_at)] -= 1
            settle_load(name)

    def vec(layer_at):
        for core in range(2):

            @pl.when(c == core)
            def _():
                for layer in range(LAYERS):
                    for kind in KINDS:
                        unpack_vector(rows, layer, kind, core, vectors[layer][kind])

    def fnorm(layer_at):
        if layer_at == 0:
            for copy in arriving:
                moves.finish(copy)
        norm_piece(inputs[layer_at], vectors[layer_at]["gain"], vectors[layer_at]["shift"], hidden[layer_at])
        pair.push(hidden[layer_at].at[own], hidden[layer_at].at[other], layer_at)

    def joined(layer_at):
        pair.sent(hidden[layer_at].at[own], layer_at)
        pair.arrived(hidden[layer_at].at[other], layer_at)
        for third in range(3):
            joined_piece(
                third, hidden[layer_at], lambda n: all_rows(held["qkv"], n),
                vectors[layer_at]["b_qkv"], tables, held[TURNED],
            )
        flip_piece(hidden[layer_at], held[FLIPPED])

    def fattn(layer_at):
        attention_piece(held[TURNED], held[PROBS], held[MIXED])

    def up(layer_at):
        up_piece(
            hidden[layer_at], lambda n: all_rows(held["up"], n), vectors[layer_at]["b_up"],
            held[ACTIVE], held["slope"],
        )

    def down(layer_at):
        if layer_at:
            pair.sent(partial.at[other], 2)
        down_piece(
            held[ACTIVE], lambda n: all_rows(held["down"], n), held[MIXED],
            lambda n: all_rows(held["out"], n), partial,
        )
        pair.push(partial.at[other], received[layer_at], 2 + layer_at)

    def res(layer_at):
        pair.arrived(received[layer_at], 2 + layer_at)
        target = late.at[own] if layer_at else x_late
        residual_piece(
            inputs[layer_at], partial, received[layer_at], vectors[layer_at]["out_bias"], target
        )
        if layer_at:
            loads["result"] = moves.start(target, result)

    def start(layer_at):
        if not layer_at:
            moves.finish(loads["result"])
        start_piece(upstream[layer_at], dy_low[layer_at], grads[layer_at]["out_bias"])
        pair.push(dy_low[layer_at].at[own], dy_low[layer_at].at[other], 4 + layer_at)

    def low(layer_at):
        pair.sent(dy_low[layer_at].at[own], 4 + layer_at)
        pair.arrived(dy_low[layer_at].at[other], 4 + layer_at)

    def gdown(layer_at):
        rows_grad_piece(D, held[ACTIVE], dy_low[layer_at], store_row_tile(totals[DOWN]))

    def slope(layer_at):
        slope_piece(
            dy_low[layer_at], lambda n: row_tile(held["down"], n, D), held["slope"], held["slope"],
            grads[layer_at]["b_up"],
        )

    def gup(layer_at):
        columns_grad_piece(D, held[FLIPPED], held["slope"], store_column_tile(totals[UP]))

    def dmixed(layer_at):
        d_mixed_piece(dy_low[layer_at], lambda n: row_tile(held["out"], n, WIDE), d_mixed)

    def gout(layer_at):
        rows_grad_piece(WIDE, held[MIXED], dy_low[layer_at], store_row_tile(totals[OUT]))

    def battn(sequence):
        return lambda layer_at: attention_back_piece(
            held[TURNED], held[PROBS], d_mixed, tables, held[TURNED], grads[layer_at]["b_qkv"],
            sequence,
        )

    def dhidden(layer_at):
        pair.sent(partial.at[other], 3 if layer_at else 7)
        d_hidden_piece(
            held[TURNED], lambda n: row_tile(held["qkv"], n, D), held["slope"],
            lambda n: row_tile(held["up"], n, D), partial,
        )
        pair.push(partial.at[other], received_grad[layer_at], 6 + layer_at)

    def gqkv(layer_at):
        columns_grad_piece(1536, held[FLIPPED], held[TURNED], store_column_tile(totals[QKV]))

    def norm(layer_at):
        pair.arrived(received_grad[layer_at], 6 + layer_at)
        norm_back_piece(
            inputs[layer_at], vectors[layer_at]["gain"], upstream[layer_at], partial, received_grad[layer_at], dy,
            grads[layer_at]["gain"], grads[layer_at]["shift"],
        )
        if layer_at == 0:
            moves.start(dy, in_grad)

    def pack(layer_at):
        for core in range(2):

            @pl.when(c == core)
            def _():
                if layer_at:
                    streams[core, 0, 0].finish()
                    every[...] = jnp.zeros_like(every)
                for kind in KINDS:
                    pack_vector(rows, layer_at, kind, core, grads[layer_at][kind])

    steps = {
        "vec": vec, "fnorm": fnorm, "joined": joined, "fattn": fattn,
        "up": up, "down": down, "res": res, "start": start, "low": low, "gdown": gdown, "slope": slope,
        "gup": gup, "dmixed": dmixed, "gout": gout, "battnA": battn(0), "battnB": battn(1),
        "dhidden": dhidden, "gqkv": gqkv, "norm": norm, "pack": pack,
    }
    for name, layer_at in schedule:
        with jax.named_scope(name):
            if name in GATHERS:
                stage = advance(streams, layer_at, GATHERS[name], 0)
                if stage == 6 and GATHERS[name]:
                    weight = WEIGHT_NAMES[GATHERS[name] - 1]
                    pending[weight, GATHER + layer_at] = 0
                    settle_load(weight)
            elif name in SUMS:
                advance(sums, layer_at, SUMS[name], 1)
            else:
                before(name, layer_at)
                steps[name](layer_at)
                after(name, layer_at)
    pair.sent(partial.at[other], 6)
    for core in range(2):

        @pl.when(c == core)
        def _():
            for (core_of, layer_at, which), stream in streams.items():
                if core_of == core:
                    stream.finish()

    small_out[...] = landing[SMALL_SUM][8][1]
    for copy in list(moves.open):
        copy.wait()


def blocks_call(tokens, out_grad, tables, vectors, owned_weights):
    vmem, hbm = pl.BlockSpec(memory_space=pltpu.VMEM), pl.BlockSpec(memory_space=pltpu.HBM)
    shape = jax.ShapeDtypeStruct
    outs = [
        shape((COUNT, D), BF16),
        shape((COUNT, D), F32),
        shape((LAYERS, 16, 3072), F32),
        shape((LAYERS, 16, 4096), F32),
        shape((LAYERS, 16, 1024), F32),
        shape((LAYERS, 64, 1024), F32),
    ]
    for layer_at in range(LAYERS):
        outs += [shape(weight_shape(spec), BF16) for spec in WEIGHTS]
    outs += [shape(dims, kind) for name, dims, kind in KEPT]
    in_hbm = len(outs)
    outs += [shape((OWNED_ROWS, LANE), F32)]
    scratch = [pltpu.VMEM(dims, kind) for name, dims, kind in KEPT]
    scratch += [pltpu.VMEM(weight_shape(spec), BF16) for spec in WEIGHTS]
    scratch += [pltpu.VMEM((1, n), F32) for n in (1536, 2048, D, D, D) * (2 * LAYERS)]
    scratch += [
        pltpu.VMEM((OWNED_ROWS, LANE), F32),
        pltpu.VMEM((COUNT, D), F32),
        pltpu.VMEM((COUNT, D), F32),
        pltpu.VMEM((COUNT, D), BF16),
        pltpu.VMEM((COUNT, D), BF16),
        pltpu.VMEM((3, COUNT, LANE), F32),
        pltpu.VMEM((BOTH, D), BF16),
        pltpu.VMEM((BOTH, D), BF16),
        pltpu.VMEM((BOTH, 512), BF16),
        pltpu.VMEM((BOTH, D), F32),
        pltpu.VMEM((COUNT, D), F32),
    ]
    scratch += [pltpu.VMEM(weight_shape(spec), BF16) for spec in WEIGHTS]
    scratch.append(pltpu.VMEM(weight_shape(SMALL_GATHERED), F32))
    for spec in SUMMED:
        scratch += landing_shapes(spec)
    count = 1 + 4 * LAYERS
    scratch += [
        pltpu.SemaphoreType.DMA((count, SLOTS)),
        pltpu.SemaphoreType.DMA((count, SLOTS)),
        pltpu.SemaphoreType.DMA((2 * len(SUMMED), SUM_SLOTS)),
        pltpu.SemaphoreType.DMA((2 * len(SUMMED), SUM_SLOTS)),
        pltpu.SemaphoreType.REGULAR((len(SUMMED), 12)),
        pltpu.SemaphoreType.DMA((8,)),
        pltpu.SemaphoreType.DMA((8,)),
        pltpu.SemaphoreType.DMA((40,)),
    ]
    found = pl.pallas_call(
        functools.partial(blocks_kernel, [(STEP_NAMES[step // 2], step % 2) for step in SCHEDULE]),
        out_shape=outs,
        in_specs=[vmem] * 5 + [hbm] * 7,
        out_specs=[hbm] * in_hbm + [vmem],
        scratch_shapes=scratch,
        name="blocks",
        compiler_params=pltpu.CompilerParams(
            collective_id=0, has_side_effects=True, vmem_limit_bytes=639 * 2**20 // 10
        ),
    )(*vectors, tokens, out_grad, tables, *owned_weights)
    return found[:6] + found[in_hbm:]


def hand_over_kernel(*refs):
    sources, small, targets, parts = refs[:6], refs[6], refs[7:13], refs[13:18]
    held, (read, written) = refs[18:24], refs[24:]
    copies_in, copies_out = [
        [
            pltpu.make_async_copy(source, target, done.at[number])
            for number, (source, target) in enumerate(zip(left, right))
        ]
        for left, right, done in ((sources, held, read), (held, targets, written))
    ]
    for copy in copies_in:
        copy.start()
    for layer_at in range(LAYERS):
        for (row, size, factor, shift), target in zip(KINDS.values(), parts):
            at_row = 5 * layer_at + row
            target[layer_at : layer_at + 1, :] = small[at_row : at_row + 1, :size]
    for copy, onward in zip(copies_in, copies_out):
        copy.wait()
        onward.start()
    for copy in copies_out:
        copy.wait()


def hand_over(found):
    vmem, hbm = pl.BlockSpec(memory_space=pltpu.VMEM), pl.BlockSpec(memory_space=pltpu.HBM)
    shape = jax.ShapeDtypeStruct
    return pl.pallas_call(
        hand_over_kernel,
        out_shape=[shape(item.shape, item.dtype) for item in found[:6]]
        + [shape((LAYERS, size), F32) for row, size, factor, shift in KINDS.values()],
        in_specs=[hbm] * 6 + [vmem],
        out_specs=[hbm] * 6 + [vmem] * 5,
        scratch_shapes=[pltpu.VMEM(item.shape, item.dtype) for item in found[:6]]
        + [pltpu.SemaphoreType.DMA((6,))] * 2,
        name="hand_over",
    )(*found)


def on_device(
    tokens, w_qkv, b_qkv, w_out, w_up, b_up, w_down, ln_gain, ln_bias, out_bias, out_grad
):
    tables = jnp.asarray(turn_tables())
    found = blocks_call(
        tokens,
        out_grad,
        tables,
        (b_qkv, b_up, ln_gain, ln_bias, out_bias),
        (w_qkv, w_up, w_out, w_down),
    )
    result, in_grad, g_qkv, g_up, g_out, g_down, *small = hand_over(found)
    g_b_qkv, g_b_up, g_gain, g_shift, g_out_bias = small
    return (
        result,
        in_grad,
        g_qkv,
        g_b_qkv,
        g_out,
        g_up,
        g_b_up,
        g_down,
        g_gain,
        g_shift,
        g_out_bias,
    )


def solution(mesh):
    placed = (
        P(("rep", "shard"), None),
        P(None, "shard", None),
        P(None, "shard"),
        P(None, "shard", None),
        P(None, "shard", None),
        P(None, "shard"),
        P(None, "shard", None),
        P(None, "shard"),
        P(None, "shard"),
        P(None, "shard"),
        P(("rep", "shard"), None),
    )
    return jax.shard_map(
        on_device,
        mesh=mesh,
        in_specs=placed,
        out_specs=(
            P(("rep", "shard"), None),
            P(("rep", "shard"), None),
            P(None, "shard", None),
            P(None, "shard"),
            P(None, "shard", None),
            P(None, "shard", None),
            P(None, "shard"),
            P(None, "shard", None),
            P(None, "shard"),
            P(None, "shard"),
            P(None, "shard"),
        ),
        check_vma=False,
    )
```

```python
import functools
import math

import jax
import jax.numpy as jnp
import numpy as np
from jax import lax
from jax.experimental import pallas as pl
from jax.experimental.pallas import tpu as pltpu
from jax.sharding import PartitionSpec as P


STEP_NAMES = (
    "s", "q", "u", "o", "d", "Q", "R", "U", "V", "O", "D", "E", "S", "vec", "fnorm", "joined",
    "fattn", "up", "down", "res", "start", "low", "gdown", "slope", "gup", "dmixed", "gout",
    "battnA", "battnB", "dhidden", "gqkv", "norm", "pack",
)
(
    s0, s1, q0, q1, u0, u1, o0, o1, d0, d1, Q0, Q1, R0, R1, U0, U1, V0, V1, O0, O1, D0, D1, E0,
    E1, S0, S1, vec0, vec1, fnorm0, fnorm1, joined0, joined1, fattn0, fattn1, up0, up1, down0,
    down1, res0, res1, start0, start1, low0, low1, gdown0, gdown1, slope0, slope1, gup0, gup1,
    dmixed0, dmixed1, gout0, gout1, battnA0, battnA1, battnB0, battnB1, dhidden0, dhidden1, gqkv0,
    gqkv1, norm0, norm1, pack0, pack1,
) = range(2 * len(STEP_NAMES))
SCHEDULE = (
    o0, s0, q0, o1, q1, d0, d1, o0, u0, s0, q0, o0, o1, s0, q1, q0, o0, u1, d0, q0, o0, q1, s0,
    d0, u0, o1, q0, d0, o0, u0, q0, s0, u0, d0, u0, q1, s0, s0, u1, vec0, q0, o1, fnorm0, u0, d0,
    u1, d1, joined0, q1, u1, u0, o0, fattn0, d0, up0, q1, down0, o1, d1, u1, res0, q1, fnorm1, o1,
    d1, joined1, u1, start1, o1, fattn1, low1, gout1, O1, O1, u1, dmixed1, d1, up1, gdown1, d1,
    D1, D1, E1, O1, battnA1, battnB1, d1, D1, gqkv1, O1, Q1, Q1, slope1, gup1, V1, O1, D1, U1, E1,
    Q1, down1, D1, U1, R1, E1, res1, dhidden1, V1, Q1, U1, D1, norm1, start0, E1, V1, low0,
    gdown0, R1, gout0, E0, D0, D0, O0, U1, slope0, O0, O1, U1, R1, dmixed0, V1, Q1, gup0, V0, E1,
    U0, O0, U0, V1, D0, U1, battnA0, battnB0, E0, dhidden0, U0, D1, R1, Q1, V1, E1, O1, D1, gqkv0,
    U1, E0, O1, R0, U1, Q1, D0, norm0, V0, Q0, U0, Q0, E1, pack1, D0, O0, E1, U0, Q1, V1, R1, V0,
    R0, Q0, R1, U0, pack0, S0, S0, R0, R1, E0, V1, R1, V0, Q0, O0, S0, U0, D0, V0, E0, R0, Q0, O0,
    S0, V0, E0, R0, Q0, S0, D0, V0, R0, S0, O0, Q0, E0, U0, R0, O0, D0, V0, Q0, S0, S0, R0, E0,
)


MESH = pl.DeviceIdType.MESH
LANE = 128
LAYERS = 2


def place():
    xl = lax.axis_index("rep")
    s = lax.axis_index("shard")
    return xl, s // 32, (s // 8) % 4, (s // 2) % 4, s % 2


def at(xl, xh, z, y, c):
    return (xl, xh * 32 + z * 8 + y * 2 + c)


def around(value, step):
    return lax.rem(value + (step + 4), 4)


def greet(others):
    barrier = pltpu.get_barrier_semaphore()
    for other in others:
        pl.semaphore_signal(barrier, inc=1, device_id=other, device_id_type=MESH)
    return len(others)


def await_greetings(count):
    pl.semaphore_wait(pltpu.get_barrier_semaphore(), count)


SMALL_GATHERED = ("small", True, 32, 128, 0, 1)
GATHERED = (
    (
        ("qkv", True, 32, 1536, 4, 8),
        ("up", True, 32, 2048, 6, 10),
        ("out", False, 32, 1024, 3, 5),
        ("down", False, 128, 1024, 3, 5),
    ),
    (
        ("qkv", True, 32, 1536, 4, 8),
        ("up", True, 32, 2048, 4, 12),
        ("out", False, 32, 1024, 2, 6),
        ("down", False, 128, 1024, 2, 6),
    ),
)
SLOTS = 18


class Stream:
    def __init__(self, number, spec, source, target, send, recv, xl, xh, z, y, core):
        self.name, self.by_columns, self.rows, self.columns, self.swapped, self.width = spec
        self.number = number
        self.source = source
        self.target = target
        self.send, self.recv = send, recv
        self.xl, self.xh, self.z, self.y, self.core = xl, xh, z, y, core
        self.half = self.rows // 2
        self.wide = pl.ds(pl.multiple_of(xl * (self.swapped * LANE), LANE), self.width * LANE)
        self.mine = pl.ds(
            pl.multiple_of(xl * ((self.width - self.swapped) * LANE) + xl * (self.swapped * LANE), LANE),
            max(self.swapped, 1) * LANE,
        )
        self.theirs = pl.ds(
            pl.multiple_of((1 - xl) * (self.width * LANE), LANE), max(self.swapped, 1) * LANE
        )
        self.across = lambda core_of: at(1 - xl, 1 - xh, z, y, core_of)
        self.partner = at(1 - xl, xh, z, y, core) if core == 0 else self.across(core)
        if core == 0:
            self.first, self.second = y, z
        else:
            self.first, self.second = z, y
        self.sent = []

    def neighbour(self, ring, step):
        z, y = self.z, self.y
        if (ring == 0) == (self.core == 0):
            y = around(y, step)
        else:
            z = around(z, step)
        return at(self.xl, self.xh, z, y, self.core)

    def block(self, first, rows, columns):
        if self.core == 0:
            return self.target.at[:, self.second, first, rows, columns]
        return self.target.at[:, first, self.second, rows, columns]

    def line(self, second, rows, columns):
        if self.core == 0:
            return self.target.at[:, second, :, rows, columns]
        return self.target.at[:, :, second, rows, columns]

    def push(self, region, slot, device):
        copy = pltpu.make_async_remote_copy(
            region(),
            region(),
            self.send.at[self.number, slot],
            self.recv.at[self.number, slot],
            device_id=device,
            device_id_type=MESH,
        )
        copy.start()
        self.sent.append((region, slot))

    def arrived(self, region, slot):
        pltpu.make_async_copy(region, region, self.recv.at[self.number, slot]).wait()

    def part(self, core_of):
        return pl.ds(core_of * self.half, self.half)

    def stage0(self):
        xh, z, y, core = self.xh, self.z, self.y, self.core
        whole = slice(None)
        if self.by_columns:
            region = lambda: self.target.at[xh, z, y, self.part(core), :]
            here = region()
            landed = self.recv.at[self.number, xh * 2 + core]
            for source, columns in self.source(core):
                pltpu.make_async_copy(source, here.at[:, columns], landed).start()
            for slot, half, device in (
                (0, 1 - core, at(self.xl, xh, z, y, 1 - core)),
                (1, core, self.across(core)),
                (2, 1 - core, self.across(1 - core)),
            ):
                for source, columns in self.source(half):
                    pltpu.make_async_remote_copy(
                        source,
                        here.at[:, columns],
                        self.send.at[self.number, slot],
                        landed,
                        device_id=device,
                        device_id_type=MESH,
                    ).start()
                self.sent.append((region, slot))
        else:
            here = self.target.at[0, z, y, self.part(core), :]
            mine = self.source(0)

            @pl.when(xh == core)
            def _():
                pltpu.make_async_copy(mine, here, self.recv.at[self.number, core]).start()

            @pl.when(xh != core)
            def _():
                pltpu.make_async_remote_copy(
                    mine,
                    here,
                    self.send.at[self.number, 0],
                    self.recv.at[self.number, core],
                    device_id=at(self.xl, xh, z, y, 1 - core),
                    device_id_type=MESH,
                ).start()

            pltpu.make_async_remote_copy(
                mine,
                here,
                self.send.at[self.number, 1],
                self.recv.at[self.number, core],
                device_id=self.across(xh),
                device_id_type=MESH,
            ).start()
            self.sent.append((lambda: self.source(0), 1))

    def stage1(self):
        whole = slice(None)
        for bank in range(2 if self.by_columns else 1):
            for core_of in range(2):
                self.arrived(
                    self.target.at[bank, self.z, self.y, self.part(core_of), :], bank * 2 + core_of
                )
        own = lambda: self.block(self.first, whole, self.wide)
        self.push(own, 4, self.neighbour(0, 1))
        self.push(own, 5, self.neighbour(0, -1))

    def share(self, region, slot):
        if self.swapped:
            self.push(lambda: region(self.mine), slot, self.partner)

    def stage2(self):
        whole = slice(None)
        for step, slot in ((-1, 4), (1, 5)):
            found = lambda rows, columns, step=step: self.block(
                around(self.first, step), rows, columns
            )
            self.arrived(found(whole, self.wide), slot)
            self.push(
                lambda found=found, slot=slot: found(self.part(slot - 4), self.wide),
                slot + 2,
                self.neighbour(0, -step),
            )
            self.share(lambda columns, found=found: found(whole, columns), slot + 8)

    def stage3(self):
        whole = slice(None)
        far = lambda rows, columns: self.block(around(self.first, 2), rows, columns)
        for half in range(2):
            self.arrived(far(self.part(half), self.wide), 6 + half)
        own = lambda: self.line(self.second, whole, self.wide)
        self.push(own, 8, self.neighbour(1, 1))
        self.push(own, 9, self.neighbour(1, -1))
        self.share(lambda columns: far(whole, columns), 14)

    def stage4(self):
        whole = slice(None)
        for step, slot in ((-1, 8), (1, 9)):
            found = lambda rows, columns, step=step: self.line(
                around(self.second, step), rows, columns
            )
            self.arrived(found(whole, self.wide), slot)
            self.push(
                lambda found=found, slot=slot: found(self.part(slot - 8), self.wide),
                slot + 2,
                self.neighbour(1, -step),
            )
            self.share(lambda columns, found=found: found(whole, columns), slot + 7)

    def stage5(self):
        whole = slice(None)
        far = lambda rows, columns: self.line(around(self.second, 2), rows, columns)
        for half in range(2):
            self.arrived(far(self.part(half), self.wide), 10 + half)
        self.share(lambda columns: far(whole, columns), 17)

    def stage6(self):
        whole = slice(None)
        if self.swapped:
            for step, slot in ((-1, 12), (1, 13), (2, 14)):
                self.arrived(self.block(around(self.first, step), whole, self.theirs), slot)
            for step, slot in ((-1, 15), (1, 16), (2, 17)):
                self.arrived(self.line(around(self.second, step), whole, self.theirs), slot)

    def finish(self):
        for region, slot in self.sent:
            pltpu.make_async_copy(region(), region(), self.send.at[self.number, slot]).wait()
        self.sent = []
        if not self.by_columns:

            @pl.when(self.xh != self.core)
            def _():
                mine = self.source(0)
                pltpu.make_async_copy(mine, mine, self.send.at[self.number, 0]).wait()


def owned_pieces(name, owned, layer_at):
    if name == "small":
        return lambda half: [(owned, slice(None))]
    if name == "qkv":
        return lambda half: [
            (
                owned.at[layer_at, :, pl.ds(third * 1024 + half * 512, 512)],
                pl.ds(third * 512, 512),
            )
            for third in range(3)
        ]
    if name == "up":
        return lambda half: [(owned.at[layer_at, :, pl.ds(half * 2048, 2048)], slice(None))]
    return lambda half: owned.at[layer_at]


def neighbours():
    xl, xh, z, y, c = place()
    return [
        at(xl, xh, z, y, 1 - c),
        at(1 - xl, 1 - xh, z, y, c),
        at(1 - xl, 1 - xh, z, y, 1 - c),
        at(xl, 1 - xh, z, y, c),
        at(1 - xl, xh, z, y, c),
        at(xl, xh, around(z, 1), y, c),
        at(xl, xh, around(z, -1), y, c),
        at(xl, xh, z, around(y, 1), c),
        at(xl, xh, z, around(y, -1), c),
    ]


COUNT = 256
BOTH = 512
D = 1024
HEAD_DIM = 64
ROT = 16
EPS = 1e-05
FILL = -1e30
F32 = jnp.float32
BF16 = jnp.bfloat16
TILE = 256
WIDE = 512


def turn_tables():
    places = np.arange(COUNT, dtype=np.float32)
    rates = np.float32(10000.0) ** (-np.arange(0, ROT, 2, dtype=np.float32) / np.float32(ROT))
    angles = places[:, None] * rates[None, :]
    cosine, sine = np.cos(angles), np.sin(angles)
    half = ROT // 2
    keep = np.ones((COUNT, HEAD_DIM), np.float32)
    ahead = np.zeros((COUNT, HEAD_DIM), np.float32)
    behind = np.zeros((COUNT, HEAD_DIM), np.float32)
    keep[:, :half] = cosine
    keep[:, half:ROT] = cosine
    ahead[:, :half] = -sine
    behind[:, half:ROT] = sine
    return np.stack([np.concatenate([t, t], 1) for t in (keep, ahead, behind)])


def turn(values, tables, sign):
    return values * tables[0] + sign * (
        pltpu.roll(values, LANE - ROT // 2, 1) * tables[1]
        + pltpu.roll(values, ROT // 2, 1) * tables[2]
    )


def dot(left, right):
    return jnp.dot(left, right, preferred_element_type=F32)


def dot_nt(left, right):
    return lax.dot_general(left, right, (((1,), (1,)), ((), ())), preferred_element_type=F32)


def dot_tn(left, right):
    return lax.dot_general(left, right, (((0,), (0,)), ((), ())), preferred_element_type=F32)


def columns_of(index, width=TILE):
    return pl.ds(pl.multiple_of(index * width, width), width)


def loop(count, body):
    def step(index, carry):
        body(index)
        return carry

    lax.fori_loop(0, count, step, 0)


KINDS = {
    "b_qkv": (0, 48, 43691, 21),
    "b_up": (1, 64, 1, 6),
    "gain": (2, 16, 1, 4),
    "shift": (3, 16, 1, 4),
    "out_bias": (4, 16, 1, 4),
}
OWNED_ROWS = 16
CHUNK = 512


def chunks_of(kind, core):
    if kind == "b_qkv":
        return [(t * CHUNK, t * 1024 + core * CHUNK) for t in range(3)]
    if kind == "b_up":
        return [(t * CHUNK, core * 2048 + t * CHUNK) for t in range(4)]
    return [(t * CHUNK, t * CHUNK) for t in range(2)]


def owner_masks(kind, start):
    row, size, factor, shift = KINDS[kind]
    place_of = lax.broadcasted_iota(jnp.int32, (LANE, CHUNK), 1) + start
    owner = lax.shift_right_logical(place_of * factor, shift)
    within = place_of - owner * size
    spread = lax.broadcasted_iota(jnp.int32, (LANE, CHUNK), 0) == within
    owned = lax.broadcasted_iota(jnp.int32, (64, CHUNK), 0) == owner[:64]
    return spread, owned


def unpack_vector(rows_ref, layer_at, kind, core, target):
    row = KINDS[kind][0] + 5 * layer_at
    held = rows_ref[pl.ds(row, 64, stride=OWNED_ROWS), :].astype(BF16)
    for place_at, start in chunks_of(kind, core):
        spread, owned = owner_masks(kind, start)
        every = dot(held, jnp.where(spread, 1.0, 0.0).astype(BF16))
        target[:, pl.ds(place_at, CHUNK)] = jnp.sum(
            jnp.where(owned, every, 0.0), 0, keepdims=True
        )


def pack_vector(rows_ref, layer_at, kind, core, vector):
    total = jnp.zeros((64, LANE), F32)
    for place_at, start in chunks_of(kind, core):
        spread, owned = owner_masks(kind, start)
        mine = jnp.where(owned, vector[:, pl.ds(place_at, CHUNK)], 0.0)
        spread = jnp.where(spread, 1.0, 0.0).astype(BF16)
        high = mine.astype(BF16)
        total = total + dot_nt(high, spread)
        total = total + dot_nt((mine - high.astype(F32)).astype(BF16), spread)
    rows_ref[pl.ds(KINDS[kind][0] + 5 * layer_at, 64, stride=OWNED_ROWS), :] = total


def centre(values):
    centred = values - jnp.mean(values, -1, keepdims=True)
    inv_std = lax.rsqrt(jnp.mean(centred * centred, -1, keepdims=True) + EPS)
    return centred * inv_std, inv_std


def norm_piece(x_ref, gain, shift, hidden):
    def body(index):
        rows = columns_of(index, 64)
        normed, unused = centre(x_ref[rows, :].astype(F32))
        hidden[rows, :] = (normed * gain[...] + shift[...]).astype(BF16)

    loop(COUNT // 64, body)


def joined_piece(third, hidden, w_qkv, b_qkv, tables, target):
    columns = pl.ds(third * 512, 512)
    found = dot(hidden[...], w_qkv(columns)) + b_qkv[:, columns]
    for sequence in range(2):
        for pair in range(4):
            part = found[sequence * COUNT : (sequence + 1) * COUNT, pair * LANE : (pair + 1) * LANE]
            if third < 2:
                part = turn(part, tables, 1.0)
            if third == 0:
                part = part * HEAD_DIM**-0.5
            target[
                pl.ds(sequence * COUNT, COUNT), pl.ds(pair * LANE + third * 512, LANE)
            ] = part.astype(BF16)


def first_head():
    return lax.broadcasted_iota(jnp.int32, (COUNT, LANE), 1) < HEAD_DIM


def only_head(values, half):
    keep = first_head() if half == 0 else jnp.logical_not(first_head())
    return jnp.where(keep, values, jnp.zeros_like(values))


def pair_of_heads(turned, index):
    sequence, pair = index // 4, index % 4
    rows, columns = columns_of(sequence, COUNT), columns_of(pair, LANE)
    return rows, columns, *(turned[rows, columns_of(pair + third * 4, LANE)] for third in range(3))


def attention_piece(turned, probs, mixed):
    def one(index):
        rows, columns, q2, k2, v2 = pair_of_heads(turned, index)
        causal = lax.broadcasted_iota(jnp.int32, (COUNT, COUNT), 0) <= lax.broadcasted_iota(
            jnp.int32, (COUNT, COUNT), 1
        )
        out = []
        for half in range(2):
            scores = jnp.where(causal, dot_nt(k2, only_head(q2, half)), FILL)
            expo = jnp.exp(scores - jnp.max(scores, 0, keepdims=True))
            prob = (expo * (1.0 / jnp.sum(expo, 0, keepdims=True))).astype(BF16)
            probs[index * 2 + half] = prob
            out.append(dot_tn(prob, v2))
        mixed[rows, columns] = jnp.where(first_head(), out[0], out[1]).astype(BF16)

    def body(index):
        for pair in range(4):
            one(index * 4 + pair)

    loop(2, body)


def up_piece(hidden, w_up, b_up, active, slope):
    def body(index):
        columns = columns_of(index, WIDE)
        upward = dot(hidden[...], w_up(columns)) + b_up[:, columns]
        spread = 0.5 + 0.5 * lax.erf(upward * (0.5**0.5))
        active[:, columns] = (upward * spread).astype(BF16)
        dense = jnp.exp(upward * upward * -0.5) * (1.0 / math.sqrt(2.0 * math.pi))
        slope[:, columns] = (spread + upward * dense).astype(BF16)

    loop(2048 // WIDE, body)


def down_piece(active, w_down, mixed, w_out, partial):
    def body(index):
        columns = columns_of(index, WIDE)
        partial[:, columns] = dot(mixed[...], w_out(columns)) + dot(active[...], w_down(columns))

    loop(D // WIDE, body)


def residual_piece(x_ref, partial, received, out_bias, target):
    def body(index):
        rows = columns_of(index, 64)
        target[rows, :] = (
            x_ref[rows, :].astype(F32)
            + (partial[rows, :] + received[rows, :])
            + out_bias[...]
        ).astype(target.dtype)

    loop(COUNT // 64, body)


def start_piece(dy, dy_low, out_bias_grad):
    def body(index):
        rows = columns_of(index, 64)
        values = dy[rows, :].astype(F32)
        dy_low[rows, :] = values.astype(BF16)
        out_bias_grad[...] += jnp.sum(values, 0, keepdims=True)

    out_bias_grad[...] = jnp.zeros_like(out_bias_grad)
    loop(COUNT // 64, body)


def flip_piece(source, target):
    rows, columns = source.shape
    for at_row in range(rows // TILE):

        def body(index, at_row=at_row):
            target[columns_of(index), pl.ds(at_row * TILE, TILE)] = source[
                pl.ds(at_row * TILE, TILE), columns_of(index)
            ].T

        loop(columns // TILE, body)


def rows_grad_piece(size, left, right, store):
    def body(index):
        store(index, dot_tn(left[:, columns_of(index, size)], right[...]).astype(BF16))

    loop(left.shape[1] // size, body)


def columns_grad_piece(size, left_flipped, right, store):
    def body(index):
        store(index, dot(left_flipped[...], right[:, columns_of(index, size)]).astype(BF16))

    loop(right.shape[1] // size, body)


def slope_piece(dy_low, w_down_rows, slope, d_up, b_up_grad):
    def body(index):
        columns = columns_of(index, D)
        found = (dot_nt(dy_low[...], w_down_rows(index)) * slope[:, columns].astype(F32)).astype(BF16)
        d_up[:, columns] = found
        b_up_grad[:, columns] = jnp.sum(found.astype(F32), 0, keepdims=True)

    loop(2048 // D, body)


def d_mixed_piece(dy_low, w_out_rows, d_mixed):
    d_mixed[...] = dot_nt(dy_low[...], w_out_rows(0)).astype(BF16)


def attention_back_piece(turned, probs, d_mixed, tables, d_joined, b_qkv_grad, sequence):
    if sequence == 0:
        b_qkv_grad[...] = jnp.zeros_like(b_qkv_grad)
    for index in range(sequence * 4, sequence * 4 + 4):
        rows, columns, q2, k2, v2 = pair_of_heads(turned, index)
        dm2 = d_mixed[rows, columns]
        both_probs = [probs[index * 2 + half] for half in range(2)]
        d_scores = []
        for half, prob in enumerate(both_probs):
            full = prob.astype(F32)
            d_probs = dot_nt(v2, only_head(dm2, half))
            d_scores.append(
                (full * (d_probs - jnp.sum(d_probs * full, 0, keepdims=True))).astype(BF16)
            )
        apart = lambda values: jnp.concatenate([only_head(values, 0), only_head(values, 1)], 0)
        parts = (
            dot_tn(jnp.concatenate(d_scores, 0), apart(k2)) * HEAD_DIM**-0.5,
            dot(jnp.concatenate(d_scores, 1), apart(q2)),
            dot(jnp.concatenate(both_probs, 1), apart(dm2)),
        )
        for third, part in enumerate(parts):
            if third < 2:
                part = turn(part, tables, -1.0)
            part = part.astype(BF16)
            there = columns_of(index % 4 + third * 4, LANE)
            d_joined[rows, there] = part
            b_qkv_grad[:, there] += jnp.sum(part.astype(F32), 0, keepdims=True)


def d_hidden_piece(d_joined, w_qkv_rows, d_up, w_up_rows, d_hidden):
    d_hidden[...] = dot_nt(d_joined[...], w_qkv_rows(0)) + dot_nt(d_up[...], w_up_rows(0))


def norm_back_piece(x_ref, gain, dy, d_hidden, received, target, gain_grad, shift_grad):
    gain_grad[...] = jnp.zeros_like(gain_grad)
    shift_grad[...] = jnp.zeros_like(shift_grad)

    def body(index):
        rows = columns_of(index, 64)
        normed, inv_std = centre(x_ref[rows, :].astype(F32))
        total = d_hidden[rows, :] + received[rows, :]
        gain_grad[...] += jnp.sum(total * normed, 0, keepdims=True)
        shift_grad[...] += jnp.sum(total, 0, keepdims=True)
        scaled = total * gain[...]
        target[rows, :] = dy[rows, :].astype(F32) + inv_std * (
            scaled
            - jnp.mean(scaled, -1, keepdims=True)
            - normed * jnp.mean(scaled * normed, -1, keepdims=True)
        )

    loop(COUNT // 64, body)


SUMMED = (
    (0, True, 32, 0, 768, 0, 6),
    (0, True, 32, 768, 768, 3, 3),
    (1, True, 32, 0, 1024, 0, 8),
    (1, True, 32, 1024, 1024, 4, 4),
    (2, False, 32, 0, 1024, 0, 8),
    (3, False, 128, 0, 512, 0, 4),
    (3, False, 128, 512, 512, 2, 2),
    (4, True, 32, 0, 128, 0, 1),
)
SMALL_SUM = 7
QKV, UP, OUT, DOWN, SMALL = range(5)
SUM_SLOTS = 18
BUFFERS = 9


def landing_shapes(spec):
    gradient, by_columns, rows, base, columns, swapped, width = spec
    banks = 2 if by_columns else 1
    kind = F32 if gradient == SMALL else BF16
    wide = width * LANE
    return [
        pltpu.VMEM((banks, 4, 4, rows, swapped * LANE) if swapped else (8, LANE), kind),
        pltpu.VMEM((2, banks, 4, rows // 2, wide), kind),
        pltpu.VMEM((2, banks, 4, rows, wide), kind),
        pltpu.VMEM((banks, 4, rows, wide), kind),
        pltpu.VMEM((2, banks, rows // 2, wide), kind),
        pltpu.VMEM((2, banks, rows, wide), kind),
        pltpu.VMEM((3, rows, wide), kind),
        pltpu.VMEM((rows, columns), F32),
        pltpu.VMEM((2, 16 if gradient == SMALL else 1, LANE), F32),
    ]


def add_into(target, first, *others):
    if len(others) == 1:
        target[...] = first[...] + others[0][...]
    else:
        found = first[...].astype(F32)
        for other in others:
            found = found + other[...].astype(F32)
        target[...] = found.astype(target.dtype)


sum_loop = loop


class Sum:
    def __init__(self, number, which, before, total, landing, output, send, recv, free, where, core):
        spec = SUMMED[which]
        self.gradient, self.by_columns, self.rows, base, self.columns, self.swapped, self.width = spec
        self.base = base
        self.number, self.which = number, which
        self.before = before
        self.after = not before and self.gradient != SMALL
        self.total, self.output = total, output
        (
            self.swap,
            self.far_line,
            self.near_line,
            self.line,
            self.far_block,
            self.near_block,
            self.last,
            self.ready,
            self.tail,
        ) = landing
        self.send, self.recv, self.free = send, recv, free
        self.xl, self.xh, self.z, self.y = where
        self.core = core
        self.banks = 2 if self.by_columns else 1
        self.half = self.rows // 2
        s, w = self.swapped, self.width
        xl, xh, z, y = where
        self.wide = pl.ds(pl.multiple_of(base + xl * (s * LANE), LANE), w * LANE)
        self.mine = pl.ds(pl.multiple_of(base + xl * (w * LANE), LANE), max(s, 1) * LANE)
        self.theirs = pl.ds(pl.multiple_of(base + (1 - xl) * (w * LANE), LANE), max(s, 1) * LANE)
        self.wide_here = pl.ds(pl.multiple_of(xl * (s * LANE), LANE), w * LANE)
        self.theirs_here = pl.ds(pl.multiple_of((1 - xl) * (w * LANE), LANE), max(s, 1) * LANE)
        self.beside = at(1 - xl, xh, z, y, core)
        self.across = at(1 - xl, 1 - xh, z, y, core)
        self.beyond = at(xl, 1 - xh, z, y, core)
        self.sibling = at(xl, xh, z, y, 1 - core)
        self.partner = self.beside if core == 0 else self.across
        self.first, self.second = (y, z) if core == 0 else (z, y)
        self.sent = []

    def neighbour(self, ring, step):
        z, y = self.z, self.y
        if (ring == 0) == (self.core == 0):
            y = around(y, step)
        else:
            z = around(z, step)
        return at(self.xl, self.xh, z, y, self.core)

    def total_line(self, second, rows, columns):
        if self.core == 0:
            return self.total.at[:, second, :, rows, columns]
        return self.total.at[:, :, second, rows, columns]

    def push(self, source, target, slot, device, keep=True):
        if self.before and slot < 12:
            pl.semaphore_wait(self.free.at[self.which, slot], 1)
        pltpu.make_async_remote_copy(
            source(),
            target,
            self.send.at[self.number, slot],
            self.recv.at[self.number, slot],
            device_id=device,
            device_id_type=MESH,
        ).start()
        if keep:
            self.sent.append((source, slot))

    def release(self, slot, device):
        if self.after:
            pl.semaphore_signal(
                self.free.at[self.which, slot], inc=1, device_id=device, device_id_type=MESH
            )

    def arrived(self, region, slot):
        pltpu.make_async_copy(region, region, self.recv.at[self.number, slot]).wait()

    def settle(self):
        for source, slot in self.sent:
            pltpu.make_async_copy(source(), source(), self.send.at[self.number, slot]).wait()
        self.sent = []

    def part(self, core_of):
        return pl.ds(core_of * self.half, self.half)

    def stage1(self):
        if self.swapped:
            self.push(
                lambda: self.total.at[:, :, :, :, self.theirs], self.swap, 0, self.partner
            )

    def stage2(self):
        if self.swapped:
            self.arrived(self.swap, 0)

            def add(step):
                bank, z = step // 4, step % 4
                region = self.total.at[bank, z, :, :, self.mine]
                add_into(region, region, self.swap.at[bank, z])

            sum_loop(self.banks * 4, add)
            self.release(0, self.partner)
        for half in range(2):
            self.push(
                lambda half=half: self.total_line(
                    around(self.second, 2), self.part(half), self.wide
                ),
                self.far_line.at[half],
                1 + half,
                self.neighbour(1, 1 - 2 * half),
            )

    def stage3(self):
        for half in range(2):
            self.arrived(self.far_line.at[half], 1 + half)
            toward = 1 - 2 * half
            rows = self.part(half)

            def add(step):
                bank, place_at = step // 4, step % 4
                region = self.total_line(around(self.second, toward), rows, self.wide).at[
                    bank, place_at
                ]
                add_into(region, region, self.far_line.at[half, bank, place_at])

            sum_loop(self.banks * 4, add)
            self.release(1 + half, self.neighbour(1, -toward))
            self.push(
                lambda toward=toward: self.total_line(
                    around(self.second, toward), slice(None), self.wide
                ),
                self.near_line.at[half],
                3 + half,
                self.neighbour(1, toward),
            )

    def stage4(self):
        for half in range(2):
            self.arrived(self.near_line.at[half], 3 + half)

        def add(step):
            bank, place_at = step // 4, step % 4
            add_into(
                self.line.at[bank, place_at],
                self.total_line(self.second, slice(None), self.wide).at[bank, place_at],
                self.near_line.at[0, bank, place_at],
                self.near_line.at[1, bank, place_at],
            )

        sum_loop(self.banks * 4, add)
        for half in range(2):
            self.release(3 + half, self.neighbour(1, 2 * half - 1))
        self.settle()
        for half in range(2):
            self.push(
                lambda half=half: self.line.at[:, around(self.first, 2), self.part(half), :],
                self.far_block.at[half],
                5 + half,
                self.neighbour(0, 1 - 2 * half),
            )

    def stage5(self):
        for half in range(2):
            self.arrived(self.far_block.at[half], 5 + half)
            toward = 1 - 2 * half
            for bank in range(self.banks):
                region = self.line.at[bank, around(self.first, toward), self.part(half), :]
                add_into(region, region, self.far_block.at[half, bank])
            self.release(5 + half, self.neighbour(0, -toward))
            self.push(
                lambda toward=toward: self.line.at[:, around(self.first, toward)],
                self.near_block.at[half],
                7 + half,
                self.neighbour(0, toward),
            )

    def own(self, bank):
        return self.line.at[bank, self.first]

    def stage6(self):
        for half in range(2):
            self.arrived(self.near_block.at[half], 7 + half)
        for bank in range(self.banks):
            add_into(
                self.own(bank),
                self.own(bank),
                self.near_block.at[0, bank],
                self.near_block.at[1, bank],
            )
        for half in range(2):
            self.release(7 + half, self.neighbour(0, 2 * half - 1))
        if self.by_columns:
            self.push(lambda: self.own(self.xh), self.last.at[0], 9, self.beside)
            self.push(lambda: self.own(1 - self.xh), self.last.at[1], 10, self.across)
            self.push(lambda: self.own(1 - self.xh), self.last.at[2], 11, self.beyond)
        else:

            @pl.when(self.xh == self.core)
            def _():
                self.push(lambda: self.own(0), self.last.at[0], 9, self.beside, False)

            @pl.when(self.xh != self.core)
            def _():
                self.push(lambda: self.own(0), self.last.at[1], 10, self.across, False)
                self.push(lambda: self.own(0), self.last.at[2], 11, self.beyond, False)

    def add_last(self):
        for slot in range(3):
            self.arrived(self.last.at[slot], 9 + slot)
        s, w = self.swapped, self.width
        c = w - s
        own = self.own(self.xh if self.by_columns else 0)
        self.ready[:, self.wide_here] = own[...].astype(F32) + self.last[2].astype(F32)
        if s:
            there = pl.ds(pl.multiple_of((1 - self.xl) * (c * LANE), LANE), s * LANE)
            self.ready[:, self.theirs_here] = self.last[0, :, there].astype(F32) + self.last[
                1, :, there
            ].astype(F32)
        if c:
            middle = pl.ds(s * LANE, c * LANE)
            there = pl.ds(pl.multiple_of(self.xl * (s * LANE), LANE), c * LANE)
            self.ready[:, middle] = (
                self.ready[:, middle]
                + self.last[0, :, there].astype(F32)
                + self.last[1, :, there].astype(F32)
            )
        for slot, device in ((9, self.beside), (10, self.across), (11, self.beyond)):
            self.release(slot, device)

    def pieces(self, core_of):
        rows, base, columns = self.part(core_of), self.base, self.columns
        if self.gradient != QKV:
            first = base + (self.core * 2048 if self.gradient == UP else 0)
            return [(self.ready.at[rows, :], self.output.at[:, pl.ds(first, columns)])]
        found = []
        start = base
        while start < base + columns:
            third, within = start // 512, start % 512
            run = min(512 - within, base + columns - start)
            found.append(
                (
                    self.ready.at[rows, pl.ds(start - base, run)],
                    self.output.at[:, pl.ds(third * 1024 + self.core * 512 + within, run)],
                )
            )
            start += run
        return found

    def deliver(self):
        for index, (source, target) in enumerate(self.pieces(self.core)):
            pltpu.make_async_copy(source, target, self.recv.at[self.number, 15 + index]).start()
        for index, (source, target) in enumerate(self.pieces(1 - self.core)):
            self.push(lambda: source, target, 12 + index, self.sibling, False)

    def delivered(self):
        for index, (source, target) in enumerate(self.pieces(self.core)):
            pltpu.make_async_copy(source, target, self.recv.at[self.number, 15 + index]).wait()
        for index, (source, target) in enumerate(self.pieces(1 - self.core)):
            pltpu.make_async_copy(source, source, self.send.at[self.number, 12 + index]).wait()

    def stage7(self):
        if self.gradient == SMALL:
            self.add_last()
            self.push(
                lambda: self.ready.at[self.part(1 - self.core), :], self.tail.at[0], 12, self.sibling
            )
        elif self.by_columns:
            self.add_last()
            self.deliver()
        else:

            @pl.when(self.xh == self.core)
            def _():
                self.add_last()
                self.deliver()

    def stage8(self):
        core = self.core
        if self.gradient == SMALL:
            self.arrived(self.tail.at[0], 12)
            self.tail[1] = self.ready[self.part(core), :] + self.tail[0]
        elif self.by_columns:
            self.delivered()
            for index, (source, target) in enumerate(self.pieces(1 - core)):
                self.arrived(source, 12 + index)
        else:

            @pl.when(self.xh == core)
            def _():
                self.delivered()

            @pl.when(self.xh != core)
            def _():
                self.arrived(self.output.at[:, pl.ds(self.base, self.columns)], 12)

        self.settle()
        if not self.by_columns:

            @pl.when(self.xh == core)
            def _():
                own = self.own(0)
                pltpu.make_async_copy(own, own, self.send.at[self.number, 9]).wait()

            @pl.when(self.xh != core)
            def _():
                own = self.own(0)
                pltpu.make_async_copy(own, own, self.send.at[self.number, 10]).wait()
                pltpu.make_async_copy(own, own, self.send.at[self.number, 11]).wait()


WEIGHTS = GATHERED[0]
WEIGHT_NAMES = tuple(spec[0] for spec in WEIGHTS)

FLIPPED, TURNED, PROBS, MIXED, ACTIVE = range(5)

KEPT = (
    (FLIPPED, (D, BOTH), BF16),
    (TURNED, (BOTH, 1536), BF16),
    (PROBS, (16, COUNT, COUNT), BF16),
    (MIXED, (BOTH, 512), BF16),
    (ACTIVE, (BOTH, 2048), BF16),
    ("slope", (BOTH, 2048), BF16),
)
KEPT_NAMES = tuple(name for name, dims, kind in KEPT)

TOUCHED = {
    "joined": ("qkv", TURNED, FLIPPED),
    "fattn": (TURNED, PROBS, MIXED),
    "up": ("up", ACTIVE, "slope"),
    "down": ("down", "out", ACTIVE, MIXED),
    "gdown": (ACTIVE,),
    "slope": ("down", "slope"),
    "gup": (FLIPPED, "slope"),
    "dmixed": ("out",),
    "gout": (MIXED,),
    "battnA": (TURNED, PROBS),
    "battnB": (TURNED, PROBS),
    "dhidden": ("qkv", "up", TURNED, "slope"),
    "gqkv": (FLIPPED, TURNED),
}
FORWARD = ("joined", "fattn", "up", "down")
WHOLE_AFTER = {
    TURNED: "joined",
    FLIPPED: "joined",
    PROBS: "fattn",
    MIXED: "fattn",
    ACTIVE: "up",
    "slope": "up",
}
GATHERS = {"s": 0, "q": 1, "u": 2, "o": 3, "d": 4}
SUMS = {"Q": 0, "R": 1, "U": 2, "V": 3, "O": 4, "D": 5, "E": 6, "S": SMALL_SUM}


class Pair:
    def __init__(self, send, recv):
        xl, xh, z, y, c = place()
        self.device = at(xl, xh, z, y, 1 - c)
        self.send, self.recv = send, recv

    def push(self, source, target, slot):
        pltpu.make_async_remote_copy(
            source,
            target,
            self.send.at[slot],
            self.recv.at[slot],
            device_id=self.device,
            device_id_type=MESH,
        ).start()

    def sent(self, source, slot):
        pltpu.make_async_copy(source, source, self.send.at[slot]).wait()

    def arrived(self, target, slot):
        pltpu.make_async_copy(target, target, self.recv.at[slot]).wait()


class Moves:
    def __init__(self, done):
        self.done = done
        self.count = 0
        self.open = []

    def start(self, source, target):
        copy = pltpu.make_async_copy(source, target, self.done.at[self.count])
        self.count += 1
        copy.start()
        self.open.append(copy)
        return copy

    def finish(self, copy):
        if any(other is copy for other in self.open):
            copy.wait()
            self.open = [other for other in self.open if other is not copy]


EARLY, LATE, LAST, GATHER = range(4)


def phase_of(step, layer_at):
    return LATE if layer_at else (EARLY if step in FORWARD else LAST)


def weight_shape(spec):
    name, by_columns, rows, columns, swapped, width = spec
    return (2 if by_columns else 1, 4, 4, rows, columns)


def all_rows(weight, columns):
    found = weight[:, :, :, :, columns]
    return found.reshape(-1, found.shape[-1])


def row_tile(weight, index, size):
    banks, unused, same, rows, columns = weight.shape
    count = size // WIDE
    found = weight[0, pl.ds(index * count, count)] if rows == 128 else weight[pl.ds(index * count, count)]
    return found.reshape(size, columns)


def store_row_tile(total):
    def store(index, found):
        banks, unused, same, rows, columns = total.shape
        if rows == 128:
            count = found.shape[0] // WIDE
            total[0, pl.ds(index * count, count)] = found.reshape(count, 4, 128, columns)
        else:
            total[0] = found.reshape(4, 4, 32, columns)

    return store


def store_column_tile(total):
    def store(index, found):
        width = found.shape[1]
        total[:, :, :, :, columns_of(index, width)] = found.reshape(2, 4, 4, 32, width)

    return store


def blocks_kernel(schedule, b_qkv, b_up, ln_gain, ln_bias, out_bias, *rest):
    rest = list(rest)

    def take(count):
        found = rest[:count]
        del rest[:count]
        return found

    arguments = take(3)
    owned_weights = take(4)
    result, in_grad = take(2)
    large_out = take(4)
    gathered = [take(4) for layer_at in range(LAYERS)]
    spilled = dict(zip(KEPT_NAMES, take(len(KEPT))))
    (small_out,) = take(1)
    held = dict(zip(KEPT_NAMES + WEIGHT_NAMES, take(len(KEPT) + 4)))
    vectors = [dict(zip(KINDS, take(5))) for layer_at in range(LAYERS)]
    grads = [dict(zip(KINDS, take(5))) for layer_at in range(LAYERS)]
    owned, x_late, dy = take(3)
    tokens, out_grad, tables = copies = take(3)
    early, late = take(2)
    d_mixed, partial = take(2)
    (received_one,) = take(1)
    totals = take(5)
    landing = [take(BUFFERS) for spec in SUMMED]
    send, recv, sum_send, sum_recv, free, pair_send, pair_recv, moved = take(8)
    every = totals[SMALL]
    rows = every.reshape(64 * OWNED_ROWS, LANE)
    hidden, dy_low = (early, late), (late, early)
    received = (received_one, dy)
    received_grad = (received_one, received_one)
    inputs = (tokens, x_late)
    upstream = (dy, out_grad)

    greeted = greet(neighbours())
    moves = Moves(moved)
    arriving = [moves.start(source, target) for source, target in zip(arguments, copies)]
    owned[...] = jnp.zeros_like(owned)
    for layer_at in range(LAYERS):
        for row, vector in enumerate((b_qkv, b_up, ln_gain, ln_bias, out_bias)):
            owned[5 * layer_at + row : 5 * layer_at + row + 1, : vector.shape[1]] = vector[
                layer_at : layer_at + 1, :
            ].astype(F32)
    xl, xh, z, y, c = place()
    where = (xl, xh, z, y)
    await_greetings(greeted)
    pair = Pair(pair_send, pair_recv)
    own, other = pl.ds(0, COUNT), pl.ds(COUNT, COUNT)

    streams, sums = {}, {}
    for core in range(2):
        streams[core, 0, 0] = Stream(
            0, SMALL_GATHERED, owned_pieces("small", owned, 0), every, send, recv, *where, core
        )
        number = 0
        for layer_at in range(LAYERS):
            for which in range(4):
                number += 1
                streams[core, layer_at, which + 1] = Stream(
                    number, GATHERED[layer_at][which],
                    owned_pieces(WEIGHT_NAMES[which], owned_weights[which], layer_at),
                    gathered[layer_at][which], send, recv, *where, core,
                )
        number = 0
        for which, spec in enumerate(SUMMED):
            gradient = spec[0]
            for layer_at in range(1 if gradient == SMALL else LAYERS):
                sums[core, layer_at, which] = Sum(
                    number, which, layer_at == 0 and gradient != SMALL, totals[gradient], landing[which],
                    None if gradient == SMALL else large_out[gradient].at[layer_at],
                    sum_send, sum_recv, free, where, core,
                )
                number += 1
    stage_of = {}

    def advance(table, layer_at, which, first):
        key = (id(table), layer_at, which)
        stage = stage_of[key] = stage_of.get(key, first - 1) + 1
        for core in range(2):

            @pl.when(c == core)
            def _():
                getattr(table[core, layer_at, which], f"stage{stage}")()

        return stage

    pending = {}
    for step, layer_at in schedule:
        for name in TOUCHED.get(step, ()):
            turn_of = phase_of(step, layer_at)
            pending[name, turn_of] = pending.get((name, turn_of), 0) + 1
    for name in WEIGHT_NAMES:
        for layer_at in range(LAYERS):
            pending[name, GATHER + layer_at] = 1
    loads, keeps = {}, {}

    def settle_load(name):
        if name in WEIGHT_NAMES:
            which = WEIGHT_NAMES.index(name)
            if not pending[name, GATHER] and (name, 0) not in loads:
                loads[name, 0] = moves.start(gathered[0][which], held[name])
            if not pending[name, GATHER + 1] and not pending[name, EARLY] and (name, 1) not in loads:
                loads[name, 1] = moves.start(gathered[1][which], held[name])
            source = gathered[0][which]
        else:
            source = spilled[name]
        if not pending[name, EARLY] and not pending[name, LATE] and (name, 2) not in loads:
            loads[name, 2] = moves.start(source, held[name])

    def before(step, layer_at):
        for name in TOUCHED.get(step, ()):
            if name in WEIGHT_NAMES:
                moves.finish(loads[name, phase_of(step, layer_at)])
            elif layer_at == 0 and step not in FORWARD:
                moves.finish(loads[name, 2])
            elif layer_at == 1 and step in FORWARD:
                moves.finish(keeps[name])

    def after(step, layer_at):
        for name in TOUCHED.get(step, ()):
            if layer_at == 0 and WHOLE_AFTER.get(name) == step:
                keeps[name] = moves.start(held[name], spilled[name])
            pending[name, phase_of(step, layer_at)] -= 1
            settle_load(name)

    def vec(layer_at):
        for core in range(2):

            @pl.when(c == core)
            def _():
                for layer in range(LAYERS):
                    for kind in KINDS:
                        unpack_vector(rows, layer, kind, core, vectors[layer][kind])

    def fnorm(layer_at):
        if layer_at == 0:
            for copy in arriving:
                moves.finish(copy)
        norm_piece(inputs[layer_at], vectors[layer_at]["gain"], vectors[layer_at]["shift"], hidden[layer_at])
        pair.push(hidden[layer_at].at[own], hidden[layer_at].at[other], layer_at)

    def joined(layer_at):
        pair.sent(hidden[layer_at].at[own], layer_at)
        pair.arrived(hidden[layer_at].at[other], layer_at)
        for third in range(3):
            joined_piece(
                third, hidden[layer_at], lambda n: all_rows(held["qkv"], n),
                vectors[layer_at]["b_qkv"], tables, held[TURNED],
            )
        flip_piece(hidden[layer_at], held[FLIPPED])

    def fattn(layer_at):
        attention_piece(held[TURNED], held[PROBS], held[MIXED])

    def up(layer_at):
        up_piece(
            hidden[layer_at], lambda n: all_rows(held["up"], n), vectors[layer_at]["b_up"],
            held[ACTIVE], held["slope"],
        )

    def down(layer_at):
        if layer_at:
            pair.sent(partial.at[other], 2)
        down_piece(
            held[ACTIVE], lambda n: all_rows(held["down"], n), held[MIXED],
            lambda n: all_rows(held["out"], n), partial,
        )
        pair.push(partial.at[other], received[layer_at], 2 + layer_at)

    def res(layer_at):
        pair.arrived(received[layer_at], 2 + layer_at)
        target = late.at[own] if layer_at else x_late
        residual_piece(
            inputs[layer_at], partial, received[layer_at], vectors[layer_at]["out_bias"], target
        )
        if layer_at:
            loads["result"] = moves.start(target, result)

    def start(layer_at):
        if not layer_at:
            moves.finish(loads["result"])
        start_piece(upstream[layer_at], dy_low[layer_at], grads[layer_at]["out_bias"])
        pair.push(dy_low[layer_at].at[own], dy_low[layer_at].at[other], 4 + layer_at)

    def low(layer_at):
        pair.sent(dy_low[layer_at].at[own], 4 + layer_at)
        pair.arrived(dy_low[layer_at].at[other], 4 + layer_at)

    def gdown(layer_at):
        rows_grad_piece(D, held[ACTIVE], dy_low[layer_at], store_row_tile(totals[DOWN]))

    def slope(layer_at):
        slope_piece(
            dy_low[layer_at], lambda n: row_tile(held["down"], n, D), held["slope"], held["slope"],
            grads[layer_at]["b_up"],
        )

    def gup(layer_at):
        columns_grad_piece(D, held[FLIPPED], held["slope"], store_column_tile(totals[UP]))

    def dmixed(layer_at):
        d_mixed_piece(dy_low[layer_at], lambda n: row_tile(held["out"], n, WIDE), d_mixed)

    def gout(layer_at):
        rows_grad_piece(WIDE, held[MIXED], dy_low[layer_at], store_row_tile(totals[OUT]))

    def battn(sequence):
        return lambda layer_at: attention_back_piece(
            held[TURNED], held[PROBS], d_mixed, tables, held[TURNED], grads[layer_at]["b_qkv"],
            sequence,
        )

    def dhidden(layer_at):
        pair.sent(partial.at[other], 3 if layer_at else 7)
        d_hidden_piece(
            held[TURNED], lambda n: row_tile(held["qkv"], n, D), held["slope"],
            lambda n: row_tile(held["up"], n, D), partial,
        )
        pair.push(partial.at[other], received_grad[layer_at], 6 + layer_at)

    def gqkv(layer_at):
        columns_grad_piece(1536, held[FLIPPED], held[TURNED], store_column_tile(totals[QKV]))

    def norm(layer_at):
        pair.arrived(received_grad[layer_at], 6 + layer_at)
        norm_back_piece(
            inputs[layer_at], vectors[layer_at]["gain"], upstream[layer_at], partial, received_grad[layer_at], dy,
            grads[layer_at]["gain"], grads[layer_at]["shift"],
        )
        if layer_at == 0:
            moves.start(dy, in_grad)

    def pack(layer_at):
        for core in range(2):

            @pl.when(c == core)
            def _():
                if layer_at:
                    streams[core, 0, 0].finish()
                    every[...] = jnp.zeros_like(every)
                for kind in KINDS:
                    pack_vector(rows, layer_at, kind, core, grads[layer_at][kind])

    steps = {
        "vec": vec, "fnorm": fnorm, "joined": joined, "fattn": fattn,
        "up": up, "down": down, "res": res, "start": start, "low": low, "gdown": gdown, "slope": slope,
        "gup": gup, "dmixed": dmixed, "gout": gout, "battnA": battn(0), "battnB": battn(1),
        "dhidden": dhidden, "gqkv": gqkv, "norm": norm, "pack": pack,
    }
    for name, layer_at in schedule:
        with jax.named_scope(name):
            if name in GATHERS:
                stage = advance(streams, layer_at, GATHERS[name], 0)
                if stage == 6 and GATHERS[name]:
                    weight = WEIGHT_NAMES[GATHERS[name] - 1]
                    pending[weight, GATHER + layer_at] = 0
                    settle_load(weight)
            elif name in SUMS:
                advance(sums, layer_at, SUMS[name], 1)
            else:
                before(name, layer_at)
                steps[name](layer_at)
                after(name, layer_at)
    pair.sent(partial.at[other], 6)
    for core in range(2):

        @pl.when(c == core)
        def _():
            for (core_of, layer_at, which), stream in streams.items():
                if core_of == core:
                    stream.finish()

    small_out[...] = landing[SMALL_SUM][8][1]
    for copy in list(moves.open):
        copy.wait()


def blocks_call(tokens, out_grad, tables, vectors, owned_weights):
    vmem, hbm = pl.BlockSpec(memory_space=pltpu.VMEM), pl.BlockSpec(memory_space=pltpu.HBM)
    shape = jax.ShapeDtypeStruct
    outs = [
        shape((COUNT, D), BF16),
        shape((COUNT, D), F32),
        shape((LAYERS, 16, 3072), F32),
        shape((LAYERS, 16, 4096), F32),
        shape((LAYERS, 16, 1024), F32),
        shape((LAYERS, 64, 1024), F32),
    ]
    for layer_at in range(LAYERS):
        outs += [shape(weight_shape(spec), BF16) for spec in WEIGHTS]
    outs += [shape(dims, kind) for name, dims, kind in KEPT]
    in_hbm = len(outs)
    outs += [shape((OWNED_ROWS, LANE), F32)]
    scratch = [pltpu.VMEM(dims, kind) for name, dims, kind in KEPT]
    scratch += [pltpu.VMEM(weight_shape(spec), BF16) for spec in WEIGHTS]
    scratch += [pltpu.VMEM((1, n), F32) for n in (1536, 2048, D, D, D) * (2 * LAYERS)]
    scratch += [
        pltpu.VMEM((OWNED_ROWS, LANE), F32),
        pltpu.VMEM((COUNT, D), F32),
        pltpu.VMEM((COUNT, D), F32),
        pltpu.VMEM((COUNT, D), BF16),
        pltpu.VMEM((COUNT, D), BF16),
        pltpu.VMEM((3, COUNT, LANE), F32),
        pltpu.VMEM((BOTH, D), BF16),
        pltpu.VMEM((BOTH, D), BF16),
        pltpu.VMEM((BOTH, 512), BF16),
        pltpu.VMEM((BOTH, D), F32),
        pltpu.VMEM((COUNT, D), F32),
    ]
    scratch += [pltpu.VMEM(weight_shape(spec), BF16) for spec in WEIGHTS]
    scratch.append(pltpu.VMEM(weight_shape(SMALL_GATHERED), F32))
    for spec in SUMMED:
        scratch += landing_shapes(spec)
    count = 1 + 4 * LAYERS
    scratch += [
        pltpu.SemaphoreType.DMA((count, SLOTS)),
        pltpu.SemaphoreType.DMA((count, SLOTS)),
        pltpu.SemaphoreType.DMA((2 * len(SUMMED), SUM_SLOTS)),
        pltpu.SemaphoreType.DMA((2 * len(SUMMED), SUM_SLOTS)),
        pltpu.SemaphoreType.REGULAR((len(SUMMED), 12)),
        pltpu.SemaphoreType.DMA((8,)),
        pltpu.SemaphoreType.DMA((8,)),
        pltpu.SemaphoreType.DMA((40,)),
    ]
    found = pl.pallas_call(
        functools.partial(blocks_kernel, [(STEP_NAMES[step // 2], step % 2) for step in SCHEDULE]),
        out_shape=outs,
        in_specs=[vmem] * 5 + [hbm] * 7,
        out_specs=[hbm] * in_hbm + [vmem],
        scratch_shapes=scratch,
        name="blocks",
        compiler_params=pltpu.CompilerParams(
            collective_id=0, has_side_effects=True, vmem_limit_bytes=639 * 2**20 // 10
        ),
    )(*vectors, tokens, out_grad, tables, *owned_weights)
    return found[:6] + found[in_hbm:]


def hand_over_kernel(*refs):
    sources, small, targets, parts = refs[:6], refs[6], refs[7:13], refs[13:18]
    held, (read, written) = refs[18:24], refs[24:]
    copies_in, copies_out = [
        [
            pltpu.make_async_copy(source, target, done.at[number])
            for number, (source, target) in enumerate(zip(left, right))
        ]
        for left, right, done in ((sources, held, read), (held, targets, written))
    ]
    for copy in copies_in:
        copy.start()
    for layer_at in range(LAYERS):
        for (row, size, factor, shift), target in zip(KINDS.values(), parts):
            at_row = 5 * layer_at + row
            target[layer_at : layer_at + 1, :] = small[at_row : at_row + 1, :size]
    for copy, onward in zip(copies_in, copies_out):
        copy.wait()
        onward.start()
    for copy in copies_out:
        copy.wait()


def hand_over(found):
    vmem, hbm = pl.BlockSpec(memory_space=pltpu.VMEM), pl.BlockSpec(memory_space=pltpu.HBM)
    shape = jax.ShapeDtypeStruct
    return pl.pallas_call(
        hand_over_kernel,
        out_shape=[shape(item.shape, item.dtype) for item in found[:6]]
        + [shape((LAYERS, size), F32) for row, size, factor, shift in KINDS.values()],
        in_specs=[hbm] * 6 + [vmem],
        out_specs=[hbm] * 6 + [vmem] * 5,
        scratch_shapes=[pltpu.VMEM(item.shape, item.dtype) for item in found[:6]]
        + [pltpu.SemaphoreType.DMA((6,))] * 2,
        name="hand_over",
    )(*found)


def on_device(
    tokens, w_qkv, b_qkv, w_out, w_up, b_up, w_down, ln_gain, ln_bias, out_bias, out_grad
):
    tables = jnp.asarray(turn_tables())
    found = blocks_call(
        tokens,
        out_grad,
        tables,
        (b_qkv, b_up, ln_gain, ln_bias, out_bias),
        (w_qkv, w_up, w_out, w_down),
    )
    result, in_grad, g_qkv, g_up, g_out, g_down, *small = hand_over(found)
    g_b_qkv, g_b_up, g_gain, g_shift, g_out_bias = small
    return (
        result,
        in_grad,
        g_qkv,
        g_b_qkv,
        g_out,
        g_up,
        g_b_up,
        g_down,
        g_gain,
        g_shift,
        g_out_bias,
    )


def solution(mesh):
    placed = (
        P(("rep", "shard"), None),
        P(None, "shard", None),
        P(None, "shard"),
        P(None, "shard", None),
        P(None, "shard", None),
        P(None, "shard"),
        P(None, "shard", None),
        P(None, "shard"),
        P(None, "shard"),
        P(None, "shard"),
        P(("rep", "shard"), None),
    )
    return jax.shard_map(
        on_device,
        mesh=mesh,
        in_specs=placed,
        out_specs=(
            P(("rep", "shard"), None),
            P(("rep", "shard"), None),
            P(None, "shard", None),
            P(None, "shard"),
            P(None, "shard", None),
            P(None, "shard", None),
            P(None, "shard"),
            P(None, "shard", None),
            P(None, "shard"),
            P(None, "shard"),
            P(None, "shard"),
        ),
        check_vma=False,
    )
```
